128 devices in a mesh: seq: 64 (over y, x, z_hi, core), head: 2 (over z_lo).
Axes of the slice: x: 4, y: 4, z: 4 (z_hi: 2, z_lo: 2; z = z_hi * 2 + z_lo), core: 2. Of those that a mesh axis runs over, the one named last changes fastest.
Arguments:
- q_noisy: bfloat16 [8192, 2048], P(('seq', 'head')), may hold values from -120 to 120
- q_clean: bfloat16 [8192, 2048], P(('seq', 'head')), may hold values from -120 to 120
- k_noisy: bfloat16 [8192, 256], P(('seq', 'head')), may hold values from -4 to 4
- noisy_stream_values: bfloat16 [8192, 256], P(('seq', 'head')), may hold values from -4 to 4
- k_clean: bfloat16 [8192, 256], P(('seq', 'head')), may hold values from -4 to 4
- clean_stream_values: bfloat16 [8192, 256], P(('seq', 'head')), may hold values from -4 to 4
- do_noisy: bfloat16 [8192, 2048], P(('seq', 'head')), may hold values from -5 to 5
- do_clean: bfloat16 [8192, 2048], P(('seq', 'head')), may hold values from -5 to 5
- block_ids: int32 [8192], replicated, may hold values from 0 to 254, as said below
- stretch_order: int32 [128], replicated, may hold values from 0 to 127, each once
Outputs:
- dq_noisy: bfloat16 [8192, 2048], P(('seq', 'head'))
- dq_clean: bfloat16 [8192, 2048], P(('seq', 'head'))
- dk_noisy: bfloat16 [8192, 256], P(('seq', 'head'))
- dv_noisy: bfloat16 [8192, 256], P(('seq', 'head'))
- dk_clean: bfloat16 [8192, 256], P(('seq', 'head'))
- dv_clean: bfloat16 [8192, 256], P(('seq', 'head'))
The draws below stay inside these ranges and needn't reach their ends.
Inputs may be any that keep to these rules, and one draw needn't show every extreme that they name: `block_ids`: never falling; positions 0 to 63 form one run of exactly 64; every later aligned group of 64 positions starts a new run and is split into exactly two runs at an offset of 1 to 63, so no run crosses a stretch of 64 positions. `stretch_order`: A permutation of the stretches.
All inputs are finite; a program needn't handle non-finite values.
Results may differ from the reference program's by a relative error of at most 0.01.
Values may be sent and summed in bfloat16 or wider, within the bound.
A program may use at most 128 MiB of HBM per device.

```python
import math
import jax
import jax.numpy as jnp
from jax import lax

HEAD_SIZE = 128
KEY_VALUE_HEADS = 2
QUERY_PER_KV = 8
BLK = 64
CH = 64
QUERY_HEADS = 16
STREAM_TOKENS = 8192
STRETCHES = 128


def shared_keys(key, stream_code):
    sub_key = jax.random.fold_in(key, 50 + stream_code)
    leading_key, trailing_key = jax.random.split(sub_key)
    starting_rows = jax.random.normal(leading_key, (STREAM_TOKENS // 2, KEY_VALUE_HEADS * HEAD_SIZE), jnp.float32)
    added_rows = jax.random.normal(trailing_key, (STREAM_TOKENS // 2, KEY_VALUE_HEADS * HEAD_SIZE), jnp.float32)
    companion = added_rows
    matched_pair = jnp.stack([starting_rows, companion], axis=1).reshape(STREAM_TOKENS, KEY_VALUE_HEADS * HEAD_SIZE)
    return jnp.clip(matched_pair, -4.0, 4.0)


def draw_q_noisy(key, part):
    key = jax.random.fold_in(key, 11)
    drawn_rows = jnp.clip(jax.random.normal(key, (STREAM_TOKENS, QUERY_HEADS * HEAD_SIZE), jnp.float32), -4.0, 4.0)
    return drawn_rows.astype(jnp.bfloat16)


def draw_q_clean(key, part):
    key = jax.random.fold_in(key, 12)
    drawn_rows = jnp.clip(jax.random.normal(key, (STREAM_TOKENS, QUERY_HEADS * HEAD_SIZE), jnp.float32), -4.0, 4.0)
    return drawn_rows.astype(jnp.bfloat16)


def draw_k_noisy(key, part):
    return shared_keys(key, 1).astype(jnp.bfloat16)


def draw_k_clean(key, part):
    return shared_keys(key, 2).astype(jnp.bfloat16)


def draw_block_ids(key, part):
    key = jax.random.fold_in(key, 7)
    split_points = jax.random.randint(key, (STREAM_TOKENS // BLK,), 1, BLK)
    token_places = jnp.arange(STREAM_TOKENS, dtype=jnp.int32)
    within = token_places % BLK
    group_split = jnp.take(split_points, token_places // BLK)
    starts = jnp.logical_or(within == 0, within == group_split)
    starts = jnp.logical_and(starts, token_places >= BLK)
    return jnp.cumsum(starts.astype(jnp.int32)).astype(jnp.int32)


def level_of(rng, dims, shards, least, high):
    def one(axis_at, blocks):
        heights = jax.random.uniform(jax.random.fold_in(jax.random.fold_in(rng, 6), axis_at), (blocks,), jnp.float32, least / len(shards), high / len(shards))
        return jnp.repeat(jnp.exp(heights), dims[axis_at] // blocks).reshape((-1,) + (1,) * (len(dims) - axis_at - 1))

    level = one(*shards[0])
    for cut in shards[1:]:
        level = level * one(*cut)
    return level


def bell_draw(key, shape, deviation, reach, pieces=(), kind=jnp.bfloat16):
    array = jax.random.normal(key, shape, jnp.float32) * deviation
    if len(pieces) > 0:
        array = level_of(key, shape, pieces, -0.22, 0.18) * array
    return jnp.clip(array, min=-reach, max=reach).astype(kind)


def setup_inputs(seed: int = 0) -> dict:
    seeds = jax.random.split(jax.random.key(seed), 11)
    return {
        "q_noisy": draw_q_noisy(jax.random.fold_in(seeds[10], 71), 0),
        "q_clean": draw_q_clean(jax.random.fold_in(seeds[10], 71), 0),
        "k_noisy": draw_k_noisy(jax.random.fold_in(seeds[10], 71), 0),
        "noisy_stream_values": bell_draw(seeds[3], (STREAM_TOKENS, KEY_VALUE_HEADS * HEAD_SIZE), 1.0, 4.0, ((0, 128),)),
        "k_clean": draw_k_clean(jax.random.fold_in(seeds[10], 71), 0),
        "clean_stream_values": bell_draw(seeds[5], (STREAM_TOKENS, KEY_VALUE_HEADS * HEAD_SIZE), 1.0, 4.0, ((0, 128),)),
        "do_noisy": bell_draw(seeds[6], (STREAM_TOKENS, QUERY_HEADS * HEAD_SIZE), 1.0, 5.0, ((0, 128),)),
        "do_clean": bell_draw(seeds[7], (STREAM_TOKENS, QUERY_HEADS * HEAD_SIZE), 1.0, 5.0, ((0, 128),)),
        "block_ids": draw_block_ids(jax.random.fold_in(seeds[10], 71), 0),
        "stretch_order": jax.random.permutation(seeds[9], STRETCHES).astype(jnp.int32),
    }


NEG = -1e+30

def half_round(values):
    return lax.optimization_barrier(values.astype(jnp.bfloat16)).astype(jnp.float32)

def reference(q_noisy, q_clean, k_noisy, noisy_stream_values, k_clean, clean_stream_values, do_noisy, do_clean, block_ids, stretch_order):
    score_scale = 1.0 / math.sqrt(HEAD_SIZE)
    stretch_perm = stretch_order.astype(jnp.int32)
    stored_ids = jnp.take(block_ids.astype(jnp.int32).reshape(STRETCHES, CH), stretch_perm, axis=0).reshape(STREAM_TOKENS)
    id_limit = jnp.concatenate([stored_ids, stored_ids + 1])
    span_q = math.gcd(2 * STREAM_TOKENS, 512)
    span_k = math.gcd(STREAM_TOKENS, 256)
    ids_stretches = stored_ids.reshape(STRETCHES, CH)
    local_seen = (ids_stretches[:, :, None] == ids_stretches[:, None, :])[:, None, :, :]
    dq_noisy_parts, dq_clean_parts = ([], [])
    dk_noisy_parts, dv_noisy_parts, dk_clean_parts, dv_clean_parts = ([], [], [], [])
    for grouped_heads in range(KEY_VALUE_HEADS):
        q_first = grouped_heads * QUERY_PER_KV * HEAD_SIZE
        kv_first = grouped_heads * HEAD_SIZE
        queries = jnp.concatenate([q_noisy[:, q_first:q_first + QUERY_PER_KV * HEAD_SIZE], q_clean[:, q_first:q_first + QUERY_PER_KV * HEAD_SIZE]]).astype(jnp.float32).reshape(2 * STREAM_TOKENS, QUERY_PER_KV, HEAD_SIZE)
        grads_out = jnp.concatenate([do_noisy[:, q_first:q_first + QUERY_PER_KV * HEAD_SIZE], do_clean[:, q_first:q_first + QUERY_PER_KV * HEAD_SIZE]]).astype(jnp.float32).reshape(2 * STREAM_TOKENS, QUERY_PER_KV, HEAD_SIZE)
        noisy_keys = k_noisy[:, kv_first:kv_first + HEAD_SIZE].astype(jnp.float32)
        noisy_values = noisy_stream_values[:, kv_first:kv_first + HEAD_SIZE].astype(jnp.float32)
        clean_keys = k_clean[:, kv_first:kv_first + HEAD_SIZE].astype(jnp.float32)
        clean_values = clean_stream_values[:, kv_first:kv_first + HEAD_SIZE].astype(jnp.float32)
        q_stretches = queries[:STREAM_TOKENS].reshape(STRETCHES, CH, QUERY_PER_KV, HEAD_SIZE)
        d_stretches = grads_out[:STREAM_TOKENS].reshape(STRETCHES, CH, QUERY_PER_KV, HEAD_SIZE)
        nk_stretches = noisy_keys.reshape(STRETCHES, CH, HEAD_SIZE)
        nv_stretches = noisy_values.reshape(STRETCHES, CH, HEAD_SIZE)
        local_scores = jnp.einsum('cqgd,ckd->cgqk', q_stretches, nk_stretches) * score_scale
        local_dots = jnp.einsum('cqgd,ckd->cgqk', d_stretches, nv_stretches)
        local_max = lax.optimization_barrier(jnp.max(jnp.where(local_seen, local_scores, NEG), axis=-1))
        local_exp = jnp.where(local_seen, jnp.exp(local_scores - local_max[..., None]), 0.0)

        def to_rows(values):
            return jnp.transpose(values, (1, 0, 2)).reshape(QUERY_PER_KV, STREAM_TOKENS)
        empty_rows = jnp.zeros((QUERY_PER_KV, STREAM_TOKENS), jnp.float32)
        base_max = jnp.concatenate([to_rows(local_max), empty_rows + NEG], axis=1)
        base_sum = jnp.concatenate([to_rows(lax.optimization_barrier(jnp.sum(local_exp, axis=-1))), empty_rows], axis=1)
        base_dot = jnp.concatenate([to_rows(lax.optimization_barrier(jnp.sum(local_exp * local_dots, axis=-1))), empty_rows], axis=1)

        def clean_stats(block_index):
            first_row = block_index * span_q
            q_block = lax.dynamic_slice_in_dim(queries, first_row, span_q)
            d_block = lax.dynamic_slice_in_dim(grads_out, first_row, span_q)
            row_limit = lax.dynamic_slice_in_dim(id_limit, first_row, span_q)
            seen_mask = (stored_ids[None, :] < row_limit[:, None])[None]
            scores = jnp.einsum('qgd,kd->gqk', q_block, clean_keys) * score_scale
            out_dots = jnp.einsum('qgd,kd->gqk', d_block, clean_values)
            block_max = lax.optimization_barrier(jnp.max(jnp.where(seen_mask, scores, NEG), axis=-1))
            exp_terms = jnp.where(seen_mask, jnp.exp(scores - block_max[..., None]), 0.0)
            return (block_max, lax.optimization_barrier(jnp.sum(exp_terms, axis=-1)), lax.optimization_barrier(jnp.sum(exp_terms * out_dots, axis=-1)))
        blocks_q = 2 * STREAM_TOKENS // span_q
        block_numbers = jnp.arange(blocks_q, dtype=jnp.int32)
        clean_max, clean_sum, clean_dot = lax.map(clean_stats, block_numbers)

        def merge_rows(values):
            return jnp.transpose(values, (1, 0, 2)).reshape(QUERY_PER_KV, 2 * STREAM_TOKENS)
        clean_max = merge_rows(clean_max)
        clean_sum = merge_rows(clean_sum)
        clean_dot = merge_rows(clean_dot)
        top_score = jnp.maximum(base_max, clean_max)
        total_sum = base_sum * jnp.exp(base_max - top_score) + clean_sum * jnp.exp(clean_max - top_score)
        total_dot = base_dot * jnp.exp(base_max - top_score) + clean_dot * jnp.exp(clean_max - top_score)
        log_total = top_score + jnp.log(total_sum)
        mean_dot = total_dot / total_sum
        lse_stretches = jnp.transpose(log_total[:, :STREAM_TOKENS].reshape(QUERY_PER_KV, STRETCHES, CH), (1, 0, 2))
        mean_stretches = jnp.transpose(mean_dot[:, :STREAM_TOKENS].reshape(QUERY_PER_KV, STRETCHES, CH), (1, 0, 2))
        local_prob = jnp.where(local_seen, jnp.exp(local_scores - lse_stretches[..., None]), 0.0)
        local_ds = local_prob * (local_dots - mean_stretches[..., None])
        local_prob_half = half_round(local_prob)
        local_ds_half = half_round(local_ds)
        dq_local = jnp.einsum('cgqk,ckd->cqgd', local_ds_half, nk_stretches).reshape(STREAM_TOKENS, QUERY_PER_KV, HEAD_SIZE)
        dk_noisy_part = score_scale * jnp.einsum('cgqk,cqgd->ckd', local_ds_half, q_stretches).reshape(STREAM_TOKENS, HEAD_SIZE)
        dv_noisy_part = jnp.einsum('cgqk,cqgd->ckd', local_prob_half, d_stretches).reshape(STREAM_TOKENS, HEAD_SIZE)

        def clean_dq(block_index):
            first_row = block_index * span_q
            q_block = lax.dynamic_slice_in_dim(queries, first_row, span_q)
            d_block = lax.dynamic_slice_in_dim(grads_out, first_row, span_q)
            row_limit = lax.dynamic_slice_in_dim(id_limit, first_row, span_q)
            lse_block = lax.dynamic_slice_in_dim(log_total, first_row, span_q, axis=1)
            mean_block = lax.dynamic_slice_in_dim(mean_dot, first_row, span_q, axis=1)
            seen_mask = (stored_ids[None, :] < row_limit[:, None])[None]
            scores = jnp.einsum('qgd,kd->gqk', q_block, clean_keys) * score_scale
            out_dots = jnp.einsum('qgd,kd->gqk', d_block, clean_values)
            prob_full = jnp.where(seen_mask, jnp.exp(scores - lse_block[..., None]), 0.0)
            dscore = prob_full * (out_dots - mean_block[..., None])
            return jnp.einsum('gqk,kd->qgd', half_round(dscore), clean_keys)
        dq_clean_rows = lax.map(clean_dq, block_numbers).reshape(2 * STREAM_TOKENS, QUERY_PER_KV, HEAD_SIZE)
        dq_all = (dq_clean_rows + jnp.concatenate([dq_local, jnp.zeros_like(dq_local)], axis=0)) * score_scale

        def clean_dkv(block_index):
            first_row = block_index * span_k
            key_block = lax.dynamic_slice_in_dim(clean_keys, first_row, span_k)
            value_block = lax.dynamic_slice_in_dim(clean_values, first_row, span_k)
            key_ids = lax.dynamic_slice_in_dim(stored_ids, first_row, span_k)
            seen_mask = (key_ids[None, :] < id_limit[:, None])[None]
            scores = jnp.einsum('qgd,kd->gqk', queries, key_block) * score_scale
            out_dots = jnp.einsum('qgd,kd->gqk', grads_out, value_block)
            prob_full = jnp.where(seen_mask, jnp.exp(scores - log_total[..., None]), 0.0)
            dscore = prob_full * (out_dots - mean_dot[..., None])
            key_part = score_scale * jnp.einsum('gqk,qgd->kd', half_round(dscore), queries)
            value_part = jnp.einsum('gqk,qgd->kd', half_round(prob_full), grads_out)
            return (key_part, value_part)
        dk_blocks, dv_blocks = lax.map(clean_dkv, jnp.arange(STREAM_TOKENS // span_k, dtype=jnp.int32))
        dq_noisy_parts.append(dq_all[:STREAM_TOKENS].reshape(STREAM_TOKENS, QUERY_PER_KV * HEAD_SIZE))
        dq_clean_parts.append(dq_all[STREAM_TOKENS:].reshape(STREAM_TOKENS, QUERY_PER_KV * HEAD_SIZE))
        dk_noisy_parts.append(dk_noisy_part)
        dv_noisy_parts.append(dv_noisy_part)
        dk_clean_parts.append(dk_blocks.reshape(STREAM_TOKENS, HEAD_SIZE))
        dv_clean_parts.append(dv_blocks.reshape(STREAM_TOKENS, HEAD_SIZE))
    return (jnp.concatenate(dq_noisy_parts, axis=1).astype(jnp.bfloat16), jnp.concatenate(dq_clean_parts, axis=1).astype(jnp.bfloat16), jnp.concatenate(dk_noisy_parts, axis=1).astype(jnp.bfloat16), jnp.concatenate(dv_noisy_parts, axis=1).astype(jnp.bfloat16), jnp.concatenate(dk_clean_parts, axis=1).astype(jnp.bfloat16), jnp.concatenate(dv_clean_parts, axis=1).astype(jnp.bfloat16))
```

```python
import functools, math
import jax
import jax.numpy as jnp
from jax import lax
from jax.experimental import pallas as pl
from jax.experimental.pallas import tpu as pltpu
from jax.sharding import PartitionSpec as P

NEG = -1e30
MIB = 1 << 20


def attention_kernel(tile, order, ids, q, nkv, kv, dq, dnkv, dkv, rows_kv, cols_k, acc, sbuf, pbuf, qtot):
    seq, head = lax.axis_index("seq"), lax.axis_index("head")
    yx = seq // 4
    stretches, chunk, _ = kv.shape
    scale = 1.0 / math.sqrt(128)
    to_exp2 = scale * math.log2(math.e)
    tiles = stretches * chunk // tile

    def place(c):
        return (c // 8) * 8 + ((c // 2) % 2) * 4 + ((c // 4) % 2) * 2 + c % 2

    def bring(c, _):
        rows_kv[pl.ds(pl.multiple_of(order[c] * chunk, chunk), chunk), :] = kv[place(c)]
        return 0

    lax.fori_loop(0, stretches, bring, 0, unroll=4)

    def turn(t, _):
        rows = pl.ds(pl.multiple_of(t * tile, tile), tile)
        cols_k[t] = rows_kv[rows, :128].T
        acc[rows, :] = jnp.zeros((tile, 256), jnp.float32)
        return 0

    lax.fori_loop(0, tiles, turn, 0)

    def fold(values, op):
        return op(values.reshape(values.shape[0] // 8, 8, values.shape[1]), axis=0)

    def one(g, _):
        c = yx * 8 + (g // 4) * 4 + (g % 2) * 2 + (g // 2) % 2
        p = order[c]
        first = ids[p * chunk]
        split = jnp.int32(0)
        for bit in (64, 32, 16, 8, 4, 2, 1):
            near = jnp.minimum(split + bit, chunk)
            hit = jnp.logical_and(split + bit <= chunk, ids[p * chunk + near - 1] == first)
            split = jnp.where(hit, split + bit, split)
        limit = p * chunk
        visits = (limit + tile - 1) // tile
        stack = lambda a, b: jnp.concatenate([q[g, a, :, :128], q[g, a, :, 128:], q[g, b, :, :128], q[g, b, :, 128:]], axis=0)
        q_t = stack(0, 1).T
        d_t = stack(2, 3).T
        own = rows_kv[pl.ds(pl.multiple_of(p * chunk, chunk), chunk), :]
        diag_kv = jnp.concatenate([own, nkv[g]], axis=0)
        diag_k, diag_v = diag_kv[:, :128], diag_kv[:, 128:]
        key_at = lax.broadcasted_iota(jnp.int32, (128, 256), 0)
        row_at = lax.broadcasted_iota(jnp.int32, (128, 256), 1)
        key_run = jnp.where(key_at % chunk >= split, 1, 0)
        row_run = jnp.where(row_at % chunk >= split, 1, 0)
        clean_row = jnp.where(row_at >= 128, 1, 0)
        gap = jnp.where(key_at < chunk, row_run + clean_row - key_run, jnp.where(key_run == row_run, 1, 0) - clean_row)
        diag_s = jnp.where(gap > 0, jnp.dot(diag_k, q_t, preferred_element_type=jnp.float32), NEG)
        tile_at = lax.broadcasted_iota(jnp.int32, (tile, 256), 0)

        def scores(t, top):
            rows = pl.ds(pl.multiple_of(t * tile, tile), tile)
            s = jnp.dot(rows_kv[rows, :128], q_t, preferred_element_type=jnp.float32)
            s = jnp.where(tile_at < limit - t * tile, s, NEG)
            sbuf[rows, :] = s
            return jnp.maximum(top, fold(s, jnp.max))

        top = lax.fori_loop(0, visits, scores, fold(diag_s, jnp.max))
        top = jnp.max(top, axis=0, keepdims=True)
        diag_p = jnp.exp2((diag_s - top) * to_exp2)
        diag_dp = jnp.dot(diag_v, d_t, preferred_element_type=jnp.float32)

        def sums(t, state):
            total, dots = state
            rows = pl.ds(pl.multiple_of(t * tile, tile), tile)
            dp = jnp.dot(rows_kv[rows, 128:], d_t, preferred_element_type=jnp.float32)
            e = jnp.exp2((sbuf[rows, :] - top) * to_exp2)
            sbuf[rows, :] = e
            pbuf[rows, :] = dp
            return (total + fold(e, jnp.sum), dots + fold(e * dp, jnp.sum))

        total, dots = lax.fori_loop(0, visits, sums, (fold(diag_p, jnp.sum), fold(diag_p * diag_dp, jnp.sum)))
        total = jnp.sum(total, axis=0, keepdims=True)
        over = 1.0 / total
        mean = jnp.sum(dots, axis=0, keepdims=True) * over
        q_s = (q_t.astype(jnp.float32) * over).T.astype(jnp.bfloat16)
        d_s = (d_t.astype(jnp.float32) * over).T.astype(jnp.bfloat16)

        def grads(e, dp, keys_t):
            ds = (e * (dp - mean)).astype(jnp.bfloat16)
            return (
                jnp.dot(keys_t, ds, preferred_element_type=jnp.float32),
                jnp.dot(ds, q_s, preferred_element_type=jnp.float32),
                jnp.dot(e.astype(jnp.bfloat16), d_s, preferred_element_type=jnp.float32),
            )

        gq, gk, gv = grads(diag_p, diag_dp, diag_k.T)
        qtot[...] = gq
        own_rows = pl.ds(pl.multiple_of(p * chunk, chunk), chunk)
        acc[own_rows, :128] += gk[:chunk]
        acc[own_rows, 128:] += gv[:chunk]
        dnkv[g, :, :128] = (gk[chunk:] * scale).astype(jnp.bfloat16)
        dnkv[g, :, 128:] = gv[chunk:].astype(jnp.bfloat16)

        def back(t, _):
            rows = pl.ds(pl.multiple_of(t * tile, tile), tile)
            gq, gk, gv = grads(sbuf[rows, :], pbuf[rows, :], cols_k[t])
            qtot[...] += gq
            acc[rows, :128] += gk
            acc[rows, 128:] += gv
            return 0

        lax.fori_loop(0, visits, back, 0)
        out = (qtot[...] * (over * scale)).T.astype(jnp.bfloat16)
        dq[g, 0, :, :128] = out[0:64]
        dq[g, 0, :, 128:] = out[64:128]
        dq[g, 1, :, :128] = out[128:192]
        dq[g, 1, :, 128:] = out[192:256]
        return 0

    lax.fori_loop(0, q.shape[0], one, 0)

    def give(c, _):
        rows = pl.ds(pl.multiple_of(order[c] * chunk, chunk), chunk)
        at = place(c)
        dkv[at, :, :128] = (acc[rows, :128] * scale).astype(jnp.bfloat16)
        dkv[at, :, 128:] = acc[rows, 128:].astype(jnp.bfloat16)
        return 0

    lax.fori_loop(0, stretches, give, 0, unroll=4)


def attention(order, ids, q, nkv, kv, tile=512):
    tokens = kv.shape[0] * kv.shape[1]
    vmem = pl.BlockSpec(memory_space=pltpu.VMEM)
    smem = pl.BlockSpec(memory_space=pltpu.SMEM)
    half = jnp.bfloat16
    return pl.pallas_call(
        functools.partial(attention_kernel, tile),
        out_shape=(
            jax.ShapeDtypeStruct((8, 2, 64, 256), half),
            jax.ShapeDtypeStruct((8, 64, 256), half),
            jax.ShapeDtypeStruct(kv.shape, half),
        ),
        in_specs=[smem, smem, vmem, vmem, vmem],
        out_specs=(vmem, vmem, vmem),
        scratch_shapes=[
            pltpu.VMEM((tokens, 256), half),
            pltpu.VMEM((tokens // tile, 128, tile), half),
            pltpu.VMEM((tokens, 256), jnp.float32),
            pltpu.VMEM((tokens, 256), jnp.float32),
            pltpu.VMEM((tokens, 256), jnp.float32),
            pltpu.VMEM((128, 256), jnp.float32),
        ],
        compiler_params=pltpu.CompilerParams(vmem_limit_bytes=56 * MIB),
        name="attention",
    )(order, ids, q, nkv, kv)
MESH = pl.DeviceIdType.MESH


class Spot:
    def __init__(self):
        seq, head = lax.axis_index("seq"), lax.axis_index("head")
        self.y, self.x, self.core = seq // 16, (seq // 4) % 4, seq % 2
        self.z = ((seq // 2) % 2) * 2 + head
        self.sign = 1 - 2 * self.core

    def at(self, y, x, z, core):
        return (((y * 4 + x) * 2 + z // 2) * 2 + core, z % 2)

    def member(self, turn, flip):
        z = (self.z + turn) % 4
        core = (self.core + flip) % 2
        return z, core

    def along(self, axis, steps):
        y = (self.y + steps * self.sign + 4) % 4 if axis == "y" else self.y
        x = (self.x + steps * self.sign + 4) % 4 if axis == "x" else self.x
        return self.at(y, x, self.z, self.core)

    def row(self, dy, dx):
        return ((self.y + dy * self.sign + 4) % 4) * 4 + (self.x + dx * self.sign + 4) % 4


def greet(spot):
    barrier = pltpu.get_barrier_semaphore()
    others = [spot.member(t, f) for t in range(4) for f in range(2) if t or f]
    ids = [spot.at(spot.y, spot.x, z, c) for z, c in others]
    ids += [spot.along(a, s) for a in ("y", "x") for s in (1, -1)]
    for d in ids:
        pl.semaphore_signal(barrier, inc=1, device_id=d, device_id_type=MESH)
    pl.semaphore_wait(barrier, len(ids))


class Sender:
    def __init__(self, send, recv):
        self.send, self.recv, self.made = send, recv, []

    def go(self, src, dst, device):
        n = len(self.made)
        copy = pltpu.make_async_remote_copy(
            src_ref=src, dst_ref=dst, send_sem=self.send.at[n], recv_sem=self.recv.at[n],
            device_id=device, device_id_type=MESH,
        )
        copy.start()
        self.made.append(copy)
        return copy


def spread_kernel(qn, qc, dn, dc, kn, vn, kc, vc, q, nkv, kv, send, recv, own):
    spot = Spot()
    greet(spot)
    out = Sender(send, recv)
    mine = spot.z * 2 + spot.core
    here = spot.row(0, 0)

    def pieces(z, core):
        head = pl.ds(pl.multiple_of((z % 2) * 128, 128), 128)
        cols = pl.ds(pl.multiple_of(((z % 2) * 4 + (z // 2) * 2 + core) * 256, 256), 256)
        found = [(a.at[:, cols], q.at[mine, i]) for i, a in enumerate((qn, qc, dn, dc))]
        found += [(kn.at[:, head], nkv.at[mine, :, :128]), (vn.at[:, head], nkv.at[mine, :, 128:])]
        return found

    def clean(z):
        head = pl.ds(pl.multiple_of((z % 2) * 128, 128), 128)
        slot = kv.at[here, spot.core, spot.z]
        return [(kc.at[:, head], slot.at[:, :128]), (vc.at[:, head], slot.at[:, 128:])]

    local = [pltpu.make_async_copy(s, d, own.at[i]) for i, (s, d) in enumerate(clean(spot.z) + pieces(spot.z, spot.core))]
    for c in local:
        c.start()
    first = []
    for turn in (1, 3, 2):
        z, _ = spot.member(turn, 0)
        for s, d in clean(z):
            first.append(out.go(s, d, spot.at(spot.y, spot.x, z, spot.core)))

    def send_group(turn, flip):
        z, core = spot.member(turn, flip)
        for s, d in pieces(z, core):
            out.go(s, d, spot.at(spot.y, spot.x, z, core))

    for turn, flip in ((2, 0), (2, 1), (1, 0), (3, 0), (1, 1), (3, 1), (0, 1)):
        send_group(turn, flip)
    local[0].wait()
    local[1].wait()
    for c in first:
        c.wait_recv()

    sibling = spot.at(spot.y, spot.x, spot.z, 1 - spot.core)
    last = []
    done = list(first)

    def block(dy, dx, half):
        return kv.at[spot.row(dy, dx), spot.core, pl.ds(half * 2, 2)]

    def offer(dy, dx, half, axis, steps):
        b = block(dy, dx, half)
        c = out.go(b, b, spot.along(axis, steps))
        return c

    def twin(dy, dx, half):
        b = block(dy, dx, half)
        last.append(out.go(b, b, sibling))

    def got(c):
        c.wait_recv()
        done.append(c)

    pair = {}
    for half, axis in ((0, "x"), (1, "y")):
        pair[half] = (offer(0, 0, half, axis, 1), offer(0, 0, half, axis, -1))
    late = {}
    for half, axis in ((0, "y"), (1, "x")):
        late[half, 0] = (offer(0, 0, half, axis, 1), offer(0, 0, half, axis, -1))
    for half in (0, 1):
        twin(0, 0, half)

    def spot_of(half, first_step, second_step):
        return (second_step, first_step) if half == 0 else (first_step, second_step)

    hop = {}
    for half, axis in ((0, "x"), (1, "y")):
        got(pair[half][0])
        dy, dx = spot_of(half, -1, 0)
        hop[half] = offer(dy, dx, half, axis, 1)
        other = "y" if half == 0 else "x"
        late[half, -1] = (offer(dy, dx, half, other, 1), offer(dy, dx, half, other, -1))
        twin(dy, dx, half)
    for half in (0, 1):
        got(pair[half][1])
        dy, dx = spot_of(half, 1, 0)
        other = "y" if half == 0 else "x"
        late[half, 1] = (offer(dy, dx, half, other, 1), offer(dy, dx, half, other, -1))
        twin(dy, dx, half)
    far = {}

    def second(step):
        for half in (0, 1):
            other = "y" if half == 0 else "x"
            got(late[half, step][0])
            dy, dx = spot_of(half, step, -1)
            far[half, step] = offer(dy, dx, half, other, 1)
            twin(dy, dx, half)

    second(0)
    for half in (0, 1):
        got(hop[half])
        dy, dx = spot_of(half, 2, 0)
        other = "y" if half == 0 else "x"
        late[half, 2] = (offer(dy, dx, half, other, 1), offer(dy, dx, half, other, -1))
        twin(dy, dx, half)
    for step in (-1, 1, 2):
        second(step)
    for step in (0, -1, 1, 2):
        for half in (0, 1):
            got(late[half, step][1])
            dy, dx = spot_of(half, step, 1)
            twin(dy, dx, half)
    for step in (0, -1, 1, 2):
        for half in (0, 1):
            got(far[half, step])
            dy, dx = spot_of(half, step, 2)
            twin(dy, dx, half)
    for c in local[2:]:
        c.wait()
    for c in out.made:
        if not any(c is d for d in done):
            c.wait_recv()
    for c in out.made:
        c.wait_send()


SPREAD_COPIES = 6 + 42 + 2 * (3 + 12 + 16)


def spread(qn, qc, dn, dc, kn, vn, kc, vc):
    half = jnp.bfloat16
    hbm = pl.BlockSpec(memory_space=pl.ANY)
    return pl.pallas_call(
        spread_kernel,
        out_shape=(
            jax.ShapeDtypeStruct((8, 4, 64, 256), half),
            jax.ShapeDtypeStruct((8, 64, 256), half),
            jax.ShapeDtypeStruct((16, 2, 4, 64, 256), half),
        ),
        in_specs=[hbm] * 8,
        out_specs=(hbm,) * 3,
        scratch_shapes=[
            pltpu.SemaphoreType.DMA((SPREAD_COPIES,)),
            pltpu.SemaphoreType.DMA((SPREAD_COPIES,)),
            pltpu.SemaphoreType.DMA((8,)),
        ],
        compiler_params=pltpu.CompilerParams(collective_id=0, has_side_effects=True),
        name="spread",
    )(qn, qc, dn, dc, kn, vn, kc, vc)


def gather_kernel(dq, dnkv, dkv, dqn, dqc, dkn, dvn, dkc, dvc, twins, parts, slots, stage, zout, zin, nin, send, recv, own):
    spot = Spot()
    greet(spot)
    out = Sender(send, recv)
    mine = spot.z * 2 + spot.core
    sibling = spot.at(spot.y, spot.x, spot.z, 1 - spot.core)
    cols = pl.ds(pl.multiple_of(((spot.z % 2) * 4 + (spot.z // 2) * 2 + spot.core) * 256, 256), 256)
    wide = jnp.float32

    twin = {}
    lanes = (2, -1, 1, 0)
    order = []
    for steps in ((2,), (-1, 1), (0,)):
        for lane in lanes:
            for pair in [(s, lane) for s in steps] + [(lane, s) for s in steps]:
                if pair not in order:
                    order.append(pair)

    for dy, dx in order:
        r = spot.row(-dy, -dx)
        twin[dy, dx] = out.go(dkv.at[r, 1 - spot.core], twins.at[r], sibling)

    def send_group(turn, flip):
        z, core = spot.member(turn, flip)
        to = z * 2 + core
        device = spot.at(spot.y, spot.x, z, core)
        return [
            out.go(dq.at[to, 0], dqn.at[:, cols], device),
            out.go(dq.at[to, 1], dqc.at[:, cols], device),
            out.go(dnkv.at[to], nin.at[mine], device),
        ]

    group = []
    for turn, flip in ((2, 0), (2, 1), (1, 0), (3, 0), (1, 1), (3, 1), (0, 1)):
        group += send_group(turn, flip)
    local = [
        pltpu.make_async_copy(dq.at[mine, 0], dqn.at[:, cols], own.at[0]),
        pltpu.make_async_copy(dq.at[mine, 1], dqc.at[:, cols], own.at[1]),
        pltpu.make_async_copy(dnkv.at[mine], nin.at[mine], own.at[2]),
    ]
    for c in local:
        c.start()

    ready = set()

    def part(dy, dx):
        r = spot.row(dy, dx)
        if (dy, dx) not in ready:
            ready.add((dy, dx))
            twin[dy, dx].wait_recv()
            parts[r] = (dkv[r, spot.core].astype(wide) + twins[r].astype(wide)).astype(jnp.bfloat16)
        return r

    def owner(half, lane, step):
        return (step, lane) if half == 0 else (lane, step)

    first_axis = ("y", "x")
    sent = {}
    for lane in lanes:
        for half in (0, 1):
            r = part(*owner(half, lane, 2))
            n = lanes.index(lane)
            sent[half, lane, 0] = out.go(parts.at[r, pl.ds(half * 2, 2)], slots.at[half, n, 0], spot.along(first_axis[half], -1))
    for lane in lanes:
        for half in (0, 1):
            n = lanes.index(lane)
            r = part(*owner(half, lane, -1))
            part(*owner(half, lane, 1))
            sent[half, lane, 0].wait_recv()
            stage[half, n] = (parts[r, half * 2:half * 2 + 2].astype(wide) + slots[half, n, 0].astype(wide)).astype(jnp.bfloat16)
            sent[half, lane, 1] = out.go(stage.at[half, n], slots.at[half, n, 1], spot.along(first_axis[half], -1))
            r = part(*owner(half, lane, 1))
            sent[half, lane, 2] = out.go(parts.at[r, pl.ds(half * 2, 2)], slots.at[half, n, 2], spot.along(first_axis[half], 1))

    def total(half, lane):
        n = lanes.index(lane)
        r = part(*owner(half, lane, 0))
        sent[half, lane, 1].wait_recv()
        sent[half, lane, 2].wait_recv()
        return parts[r, half * 2:half * 2 + 2].astype(wide) + slots[half, n, 1].astype(wide) + slots[half, n, 2].astype(wide)

    second_axis = ("x", "y")
    deep = {}
    for half in (0, 1):
        stage[half, 4] = total(half, 2).astype(jnp.bfloat16)
        deep[half, 0] = out.go(stage.at[half, 4], slots.at[half, 4, 0], spot.along(second_axis[half], -1))
    passed = {}
    for half in (0, 1):
        passed[half] = total(half, -1)
        deep[half, 0].wait_recv()
        stage[half, 5] = (passed[half] + slots[half, 4, 0].astype(wide)).astype(jnp.bfloat16)
        deep[half, 1] = out.go(stage.at[half, 5], slots.at[half, 4, 1], spot.along(second_axis[half], -1))
    for half in (0, 1):
        stage[half, 6] = total(half, 1).astype(jnp.bfloat16)
        deep[half, 2] = out.go(stage.at[half, 6], slots.at[half, 4, 2], spot.along(second_axis[half], 1))
    for half in (0, 1):
        mid = total(half, 0)
        deep[half, 1].wait_recv()
        deep[half, 2].wait_recv()
        zout[half * 2:half * 2 + 2] = (mid + slots[half, 4, 1].astype(wide) + slots[half, 4, 2].astype(wide)).astype(jnp.bfloat16)
    deep_z = []
    for turn in (2, 1, 3):
        z, _ = spot.member(turn, 0)
        deep_z.append(out.go(zout.at[z], zin.at[spot.z], spot.at(spot.y, spot.x, z, spot.core)))
    zin[spot.z] = zout[spot.z]

    for c in group:
        c.wait_recv()
    for c in local:
        c.wait()
    for head in (0, 1):
        at = slice(head * 128, head * 128 + 128)
        noisy = sum(nin[z * 2 + core].astype(wide) for z in (head, head + 2) for core in (0, 1))
        dkn[:, at] = noisy[:, :128].astype(jnp.bfloat16)
        dvn[:, at] = noisy[:, 128:].astype(jnp.bfloat16)
    for c in deep_z:
        c.wait_recv()
    for head in (0, 1):
        at = slice(head * 128, head * 128 + 128)
        clean = zin[head].astype(wide) + zin[head + 2].astype(wide)
        dkc[:, at] = clean[:, :128].astype(jnp.bfloat16)
        dvc[:, at] = clean[:, 128:].astype(jnp.bfloat16)
    for c in out.made:
        c.wait_send()


GATHER_COPIES = 16 + 21 + 24 + 6 + 3


def gather(dq, dnkv, dkv):
    half = jnp.bfloat16
    vmem = pl.BlockSpec(memory_space=pltpu.VMEM)
    hbm = pl.BlockSpec(memory_space=pl.ANY)
    return pl.pallas_call(
        gather_kernel,
        out_shape=(jax.ShapeDtypeStruct((64, 2048), half),) * 2 + (jax.ShapeDtypeStruct((64, 256), half),) * 4,
        in_specs=[hbm, hbm, vmem],
        out_specs=(hbm, hbm, vmem, vmem, vmem, vmem),
        scratch_shapes=[
            pltpu.VMEM((16, 4, 64, 256), half),
            pltpu.VMEM((16, 4, 64, 256), half),
            pltpu.VMEM((2, 5, 3, 2, 64, 256), half),
            pltpu.VMEM((2, 7, 2, 64, 256), half),
            pltpu.VMEM((4, 64, 256), half),
            pltpu.VMEM((4, 64, 256), half),
            pltpu.VMEM((8, 64, 256), half),
            pltpu.SemaphoreType.DMA((GATHER_COPIES,)),
            pltpu.SemaphoreType.DMA((GATHER_COPIES,)),
            pltpu.SemaphoreType.DMA((3,)),
        ],
        compiler_params=pltpu.CompilerParams(collective_id=1, has_side_effects=True, vmem_limit_bytes=40 * MIB),
        name="gather",
    )(dq, dnkv, dkv)


def local(qn, qc, kn, vn, kc, vc, dn, dc, block_ids, stretch_order):
    q, nkv, kv = spread(qn, qc, dn, dc, kn, vn, kc, vc)
    dq, dnkv, dkv = attention(stretch_order, block_ids, q, nkv, kv.reshape(128, 64, 256), tile=1024)
    return gather(dq, dnkv, dkv.reshape(16, 2, 4, 64, 256))


def solution(mesh):
    both = P(("seq", "head"), None)
    return jax.shard_map(
        local, mesh=mesh, in_specs=(both,) * 8 + (P(), P()), out_specs=(both,) * 6, check_vma=False
    )
```

```python
import functools, math
import jax
import jax.numpy as jnp
from jax import lax
from jax.experimental import pallas as pl
from jax.experimental.pallas import tpu as pltpu
from jax.sharding import PartitionSpec as P

NEG = -1e30
MIB = 1 << 20


def attention_kernel(sizes, order, ids, q, nkv, kv, dq, dnkv, dkv, rows_kv, cols_k, acc, sbuf, pbuf, qtot):
    yx = lax.axis_index("seq") // 4
    stretches, chunk, _ = kv.shape
    tokens = stretches * chunk
    scale = 1.0 / math.sqrt(128)
    to_exp2 = scale * math.log2(math.e)
    wide = jnp.float32
    half = jnp.bfloat16
    unit = sizes[-1]

    def each_chunk(body):
        def some(row, _):
            for j in range(8):
                at = (j // 2 % 2) * 4 + (j // 4) * 2 + j % 2
                body(row * 8 + at, order[row * 8 + j])
            return 0

        lax.fori_loop(0, stretches // 8, some, 0)

    def chunk_rows(p):
        return pl.ds(pl.multiple_of(p * chunk, chunk), chunk)

    def bring(at, p):
        rows_kv[chunk_rows(p), :] = kv[at]

    each_chunk(bring)

    def clear(t, _):
        acc[pl.ds(pl.multiple_of(t * 1024, 1024), 1024), :] = jnp.zeros((1024, 256), wide)
        return 0

    lax.fori_loop(0, tokens // 1024, clear, 0)

    def turn(t, _):
        for i in range(1024 // unit):
            rows = pl.ds(pl.multiple_of(t * 1024 + i * unit, unit), unit)
            cols_k[t * (1024 // unit) + i] = rows_kv[rows, :128].T
        return 0

    lax.fori_loop(0, tokens // 1024, turn, 0)

    def fold(values, op):
        return op(values.reshape(values.shape[0] // 8, 8, values.shape[1]), axis=0)

    def dot(a, b):
        return jnp.dot(a, b, preferred_element_type=wide)

    def one(g, _):
        c = yx * 8 + (g // 4) * 4 + (g % 2) * 2 + (g // 2) % 2
        p = order[c]
        limit = p * chunk
        first = ids[limit]
        split = jnp.int32(0)
        for bit in (64, 32, 16, 8, 4, 2, 1):
            near = jnp.minimum(split + bit, chunk)
            hit = jnp.logical_and(split + bit <= chunk, ids[limit + near - 1] == first)
            split = jnp.where(hit, split + bit, split)
        units = (limit + unit - 1) // unit

        def walk(body, state):
            start = jnp.int32(0)
            left = units
            for size in sizes:
                many = size // unit
                count = left // many
                state = lax.fori_loop(0, count, lambda t, s: body(pl.multiple_of(start + t * size, unit), size, s), state)
                start = start + count * size
                left = left - count * many
            return state

        stack = lambda a, b: jnp.concatenate([q[g, a, :, :128], q[g, a, :, 128:], q[g, b, :, :128], q[g, b, :, 128:]], axis=0)
        q_t = stack(0, 1).T
        d_t = stack(2, 3).T
        diag_kv = jnp.concatenate([rows_kv[chunk_rows(p), :], nkv[g]], axis=0)
        diag_k, diag_v = diag_kv[:, :128], diag_kv[:, 128:]
        key_at = lax.broadcasted_iota(jnp.int32, (128, 256), 0)
        row_at = lax.broadcasted_iota(jnp.int32, (128, 256), 1)
        key_run = jnp.where(key_at % chunk >= split, 1, 0)
        row_run = jnp.where(row_at % chunk >= split, 1, 0)
        clean_row = jnp.where(row_at >= 128, 1, 0)
        gap = jnp.where(key_at < chunk, row_run + clean_row - key_run, jnp.where(key_run == row_run, 1, 0) - clean_row)
        diag_s = jnp.where(gap > 0, dot(diag_k, q_t), NEG)

        def scores(at, size, top):
            rows = pl.ds(at, size)
            s = dot(rows_kv[rows, :128], q_t)
            s = jnp.where(lax.broadcasted_iota(jnp.int32, (size, 256), 0) < limit - at, s, NEG)
            sbuf[rows, :] = s
            return jnp.maximum(top, fold(s, jnp.max))

        top = walk(scores, fold(diag_s, jnp.max))
        top = jnp.max(top, axis=0, keepdims=True)
        diag_p = jnp.exp2((diag_s - top) * to_exp2)
        diag_dp = dot(diag_v, d_t)

        def sums(at, size, state):
            total, dots = state
            rows = pl.ds(at, size)
            dp = dot(rows_kv[rows, 128:], d_t)
            e = jnp.exp2((sbuf[rows, :] - top) * to_exp2)
            sbuf[rows, :] = e
            pbuf[rows, :] = dp
            return (total + fold(e, jnp.sum), dots + fold(e * dp, jnp.sum))

        total, dots = walk(sums, (fold(diag_p, jnp.sum), fold(diag_p * diag_dp, jnp.sum)))
        total = jnp.sum(total, axis=0, keepdims=True)
        over = 1.0 / total
        mean = jnp.sum(dots, axis=0, keepdims=True) * over
        q_s = (q_t.astype(wide) * over).T.astype(half)
        d_s = (d_t.astype(wide) * over).T.astype(half)

        def grads(e, dp, keys_t):
            ds = (e * (dp - mean)).astype(half)
            return dot(keys_t, ds), dot(ds, q_s), dot(e.astype(half), d_s)

        gq, gk, gv = grads(diag_p, diag_dp, diag_k.T)
        qtot[...] = gq
        acc[chunk_rows(p), :128] += gk[:chunk]
        acc[chunk_rows(p), 128:] += gv[:chunk]
        dnkv[g, :, :128] = (gk[chunk:] * scale).astype(half)
        dnkv[g, :, 128:] = gv[chunk:].astype(half)

        def back(at, size, _):
            rows = pl.ds(at, size)
            keys_t = jnp.concatenate([cols_k[at // unit + i] for i in range(size // unit)], axis=1)
            gq, gk, gv = grads(sbuf[rows, :], pbuf[rows, :], keys_t)
            qtot[...] += gq
            acc[rows, :128] += gk
            acc[rows, 128:] += gv
            return 0

        walk(back, 0)
        out = (qtot[...] * (over * scale)).T.astype(half)
        for i in range(4):
            dq[g, i // 2, :, (i % 2) * 128:(i % 2) * 128 + 128] = out[i * 64:i * 64 + 64]
        return 0

    lax.fori_loop(0, q.shape[0], one, 0)

    def give(at, p):
        dkv[at, :, :128] = (acc[chunk_rows(p), :128] * scale).astype(half)
        dkv[at, :, 128:] = acc[chunk_rows(p), 128:].astype(half)

    each_chunk(give)


def attention(order, ids, q, nkv, kv, tile=(2048, 1024)):
    tokens = kv.shape[0] * kv.shape[1]
    vmem = pl.BlockSpec(memory_space=pltpu.VMEM)
    smem = pl.BlockSpec(memory_space=pltpu.SMEM)
    half = jnp.bfloat16
    wide = jnp.float32
    return pl.pallas_call(
        functools.partial(attention_kernel, tile),
        out_shape=(
            jax.ShapeDtypeStruct((8, 2, 64, 256), half),
            jax.ShapeDtypeStruct((8, 64, 256), half),
            jax.ShapeDtypeStruct(kv.shape, half),
        ),
        in_specs=[smem, smem, vmem, vmem, vmem],
        out_specs=(vmem, vmem, vmem),
        scratch_shapes=[
            pltpu.VMEM((tokens, 256), half),
            pltpu.VMEM((tokens // tile[-1], 128, tile[-1]), half),
            pltpu.VMEM((tokens, 256), wide),
            pltpu.VMEM((tokens, 256), wide),
            pltpu.VMEM((tokens, 256), wide),
            pltpu.VMEM((128, 256), wide),
        ],
        compiler_params=pltpu.CompilerParams(vmem_limit_bytes=42 * MIB),
        name="attention",
    )(order, ids, q, nkv, kv)
MESH = pl.DeviceIdType.MESH


class Spot:
    def __init__(self):
        seq, head = lax.axis_index("seq"), lax.axis_index("head")
        self.y, self.x, self.core = seq // 16, (seq // 4) % 4, seq % 2
        self.z = ((seq // 2) % 2) * 2 + head
        self.sign = 1 - 2 * self.core

    def at(self, y, x, z, core):
        return (((y * 4 + x) * 2 + z // 2) * 2 + core, z % 2)

    def member(self, turn, flip):
        z = (self.z + turn) % 4
        core = (self.core + flip) % 2
        return z, core

    def along(self, axis, steps):
        y = (self.y + steps * self.sign + 4) % 4 if axis == "y" else self.y
        x = (self.x + steps * self.sign + 4) % 4 if axis == "x" else self.x
        return self.at(y, x, self.z, self.core)

    def row(self, dy, dx):
        return ((self.y + dy * self.sign + 4) % 4) * 4 + (self.x + dx * self.sign + 4) % 4


def greet(spot):
    barrier = pltpu.get_barrier_semaphore()
    others = [spot.member(t, f) for t in range(4) for f in range(2) if t or f]
    ids = [spot.at(spot.y, spot.x, z, c) for z, c in others]
    ids += [spot.along(a, s) for a in ("y", "x") for s in (1, -1)]
    for d in ids:
        pl.semaphore_signal(barrier, inc=1, device_id=d, device_id_type=MESH)
    pl.semaphore_wait(barrier, len(ids))


class Sender:
    def __init__(self, send, recv):
        self.send, self.recv, self.made = send, recv, []

    def go(self, src, dst, device):
        n = len(self.made)
        copy = pltpu.make_async_remote_copy(
            src_ref=src, dst_ref=dst, send_sem=self.send.at[n], recv_sem=self.recv.at[n],
            device_id=device, device_id_type=MESH,
        )
        copy.start()
        self.made.append(copy)
        return copy


def spread_kernel(qn, qc, dn, dc, kn, vn, kc, vc, q, nkv, kv, send, recv, own):
    spot = Spot()
    greet(spot)
    out = Sender(send, recv)
    mine = spot.z * 2 + spot.core
    here = spot.row(0, 0)

    def pieces(z, core):
        head = pl.ds(pl.multiple_of((z % 2) * 128, 128), 128)
        cols = pl.ds(pl.multiple_of(((z % 2) * 4 + (z // 2) * 2 + core) * 256, 256), 256)
        found = [(a.at[:, cols], q.at[mine, i]) for i, a in enumerate((qn, qc, dn, dc))]
        found += [(kn.at[:, head], nkv.at[mine, :, :128]), (vn.at[:, head], nkv.at[mine, :, 128:])]
        return found

    def clean(z):
        head = pl.ds(pl.multiple_of((z % 2) * 128, 128), 128)
        slot = kv.at[here, spot.core, spot.z]
        return [(kc.at[:, head], slot.at[:, :128]), (vc.at[:, head], slot.at[:, 128:])]

    local = [pltpu.make_async_copy(s, d, own.at[i]) for i, (s, d) in enumerate(clean(spot.z) + pieces(spot.z, spot.core))]
    for c in local:
        c.start()
    first = []
    for turn in (1, 3, 2):
        z, _ = spot.member(turn, 0)
        for s, d in clean(z):
            first.append(out.go(s, d, spot.at(spot.y, spot.x, z, spot.core)))

    def send_group(turn, flip):
        z, core = spot.member(turn, flip)
        for s, d in pieces(z, core):
            out.go(s, d, spot.at(spot.y, spot.x, z, core))

    for turn, flip in ((2, 0), (2, 1), (1, 0), (3, 0), (1, 1), (3, 1), (0, 1)):
        send_group(turn, flip)
    local[0].wait()
    local[1].wait()
    for c in first:
        c.wait_recv()

    sibling = spot.at(spot.y, spot.x, spot.z, 1 - spot.core)
    last = []
    done = list(first)

    def block(dy, dx, half):
        return kv.at[spot.row(dy, dx), spot.core, pl.ds(half * 2, 2)]

    def offer(dy, dx, half, axis, steps):
        b = block(dy, dx, half)
        c = out.go(b, b, spot.along(axis, steps))
        return c

    def twin(dy, dx, half):
        b = block(dy, dx, half)
        last.append(out.go(b, b, sibling))

    def got(c):
        c.wait_recv()
        done.append(c)

    pair = {}
    for half, axis in ((0, "x"), (1, "y")):
        pair[half] = (offer(0, 0, half, axis, 1), offer(0, 0, half, axis, -1))
    late = {}
    for half, axis in ((0, "y"), (1, "x")):
        late[half, 0] = (offer(0, 0, half, axis, 1), offer(0, 0, half, axis, -1))
    for half in (0, 1):
        twin(0, 0, half)

    def spot_of(half, first_step, second_step):
        return (second_step, first_step) if half == 0 else (first_step, second_step)

    hop = {}
    for half, axis in ((0, "x"), (1, "y")):
        got(pair[half][0])
        dy, dx = spot_of(half, -1, 0)
        hop[half] = offer(dy, dx, half, axis, 1)
        other = "y" if half == 0 else "x"
        late[half, -1] = (offer(dy, dx, half, other, 1), offer(dy, dx, half, other, -1))
        twin(dy, dx, half)
    for half in (0, 1):
        got(pair[half][1])
        dy, dx = spot_of(half, 1, 0)
        other = "y" if half == 0 else "x"
        late[half, 1] = (offer(dy, dx, half, other, 1), offer(dy, dx, half, other, -1))
        twin(dy, dx, half)
    far = {}

    def second(step):
        for half in (0, 1):
            other = "y" if half == 0 else "x"
            got(late[half, step][0])
            dy, dx = spot_of(half, step, -1)
            far[half, step] = offer(dy, dx, half, other, 1)
            twin(dy, dx, half)

    second(0)
    for half in (0, 1):
        got(hop[half])
        dy, dx = spot_of(half, 2, 0)
        other = "y" if half == 0 else "x"
        late[half, 2] = (offer(dy, dx, half, other, 1), offer(dy, dx, half, other, -1))
        twin(dy, dx, half)
    for step in (-1, 1, 2):
        second(step)
    for step in (0, -1, 1, 2):
        for half in (0, 1):
            got(late[half, step][1])
            dy, dx = spot_of(half, step, 1)
            twin(dy, dx, half)
    for step in (0, -1, 1, 2):
        for half in (0, 1):
            got(far[half, step])
            dy, dx = spot_of(half, step, 2)
            twin(dy, dx, half)
    for c in local[2:]:
        c.wait()
    for c in out.made:
        if not any(c is d for d in done):
            c.wait_recv()
    for c in out.made:
        c.wait_send()


SPREAD_COPIES = 6 + 42 + 2 * (3 + 12 + 16)


def spread(qn, qc, dn, dc, kn, vn, kc, vc):
    half = jnp.bfloat16
    hbm = pl.BlockSpec(memory_space=pl.ANY)
    return pl.pallas_call(
        spread_kernel,
        out_shape=(
            jax.ShapeDtypeStruct((8, 4, 64, 256), half),
            jax.ShapeDtypeStruct((8, 64, 256), half),
            jax.ShapeDtypeStruct((16, 2, 4, 64, 256), half),
        ),
        in_specs=[hbm] * 8,
        out_specs=(hbm,) * 3,
        scratch_shapes=[
            pltpu.SemaphoreType.DMA((SPREAD_COPIES,)),
            pltpu.SemaphoreType.DMA((SPREAD_COPIES,)),
            pltpu.SemaphoreType.DMA((8,)),
        ],
        compiler_params=pltpu.CompilerParams(collective_id=0, has_side_effects=True, vmem_limit_bytes=4 * MIB),
        name="spread",
    )(qn, qc, dn, dc, kn, vn, kc, vc)


def gather_kernel(dq, dnkv, dkv, dqn, dqc, dkn, dvn, dkc, dvc, twins, parts, slots, stage, zout, zin, nin, send, recv, own):
    spot = Spot()
    greet(spot)
    out = Sender(send, recv)
    mine = spot.z * 2 + spot.core
    sibling = spot.at(spot.y, spot.x, spot.z, 1 - spot.core)
    cols = pl.ds(pl.multiple_of(((spot.z % 2) * 4 + (spot.z // 2) * 2 + spot.core) * 256, 256), 256)
    wide = jnp.float32

    twin = {}
    lanes = (2, -1, 1, 0)
    order = []
    for steps in ((2,), (-1, 1), (0,)):
        for lane in lanes:
            for pair in [(s, lane) for s in steps] + [(lane, s) for s in steps]:
                if pair not in order:
                    order.append(pair)

    for dy, dx in order:
        r = spot.row(-dy, -dx)
        twin[dy, dx] = out.go(dkv.at[r, 1 - spot.core], twins.at[r], sibling)

    def send_group(turn, flip):
        z, core = spot.member(turn, flip)
        to = z * 2 + core
        device = spot.at(spot.y, spot.x, z, core)
        return [
            out.go(dq.at[to, 0], dqn.at[:, cols], device),
            out.go(dq.at[to, 1], dqc.at[:, cols], device),
            out.go(dnkv.at[to], nin.at[mine], device),
        ]

    group = []
    for turn, flip in ((2, 0), (2, 1), (1, 0), (3, 0), (1, 1), (3, 1), (0, 1)):
        group += send_group(turn, flip)
    local = [
        pltpu.make_async_copy(dq.at[mine, 0], dqn.at[:, cols], own.at[0]),
        pltpu.make_async_copy(dq.at[mine, 1], dqc.at[:, cols], own.at[1]),
        pltpu.make_async_copy(dnkv.at[mine], nin.at[mine], own.at[2]),
    ]
    for c in local:
        c.start()

    ready = set()

    def part(dy, dx):
        r = spot.row(dy, dx)
        if (dy, dx) not in ready:
            ready.add((dy, dx))
            twin[dy, dx].wait_recv()
            parts[r] = (dkv[r, spot.core].astype(wide) + twins[r].astype(wide)).astype(jnp.bfloat16)
        return r

    def owner(half, lane, step):
        return (step, lane) if half == 0 else (lane, step)

    first_axis = ("y", "x")
    sent = {}
    for lane in lanes:
        for half in (0, 1):
            r = part(*owner(half, lane, 2))
            n = lanes.index(lane)
            sent[half, lane, 0] = out.go(parts.at[r, pl.ds(half * 2, 2)], slots.at[half, n, 0], spot.along(first_axis[half], -1))
    for lane in lanes:
        for half in (0, 1):
            n = lanes.index(lane)
            r = part(*owner(half, lane, -1))
            part(*owner(half, lane, 1))
            sent[half, lane, 0].wait_recv()
            stage[half, n] = (parts[r, half * 2:half * 2 + 2].astype(wide) + slots[half, n, 0].astype(wide)).astype(jnp.bfloat16)
            sent[half, lane, 1] = out.go(stage.at[half, n], slots.at[half, n, 1], spot.along(first_axis[half], -1))
            r = part(*owner(half, lane, 1))
            sent[half, lane, 2] = out.go(parts.at[r, pl.ds(half * 2, 2)], slots.at[half, n, 2], spot.along(first_axis[half], 1))

    def total(half, lane):
        n = lanes.index(lane)
        r = part(*owner(half, lane, 0))
        sent[half, lane, 1].wait_recv()
        sent[half, lane, 2].wait_recv()
        return parts[r, half * 2:half * 2 + 2].astype(wide) + slots[half, n, 1].astype(wide) + slots[half, n, 2].astype(wide)

    second_axis = ("x", "y")
    deep = {}
    for half in (0, 1):
        stage[half, 4] = total(half, 2).astype(jnp.bfloat16)
        deep[half, 0] = out.go(stage.at[half, 4], slots.at[half, 4, 0], spot.along(second_axis[half], -1))
    passed = {}
    for half in (0, 1):
        passed[half] = total(half, -1)
        deep[half, 0].wait_recv()
        stage[half, 5] = (passed[half] + slots[half, 4, 0].astype(wide)).astype(jnp.bfloat16)
        deep[half, 1] = out.go(stage.at[half, 5], slots.at[half, 4, 1], spot.along(second_axis[half], -1))
    for half in (0, 1):
        stage[half, 6] = total(half, 1).astype(jnp.bfloat16)
        deep[half, 2] = out.go(stage.at[half, 6], slots.at[half, 4, 2], spot.along(second_axis[half], 1))
    for half in (0, 1):
        mid = total(half, 0)
        deep[half, 1].wait_recv()
        deep[half, 2].wait_recv()
        zout[half * 2:half * 2 + 2] = (mid + slots[half, 4, 1].astype(wide) + slots[half, 4, 2].astype(wide)).astype(jnp.bfloat16)
    deep_z = []
    for turn in (2, 1, 3):
        z, _ = spot.member(turn, 0)
        deep_z.append(out.go(zout.at[z], zin.at[spot.z], spot.at(spot.y, spot.x, z, spot.core)))
    zin[spot.z] = zout[spot.z]

    for c in group:
        c.wait_recv()
    for c in local:
        c.wait()
    for head in (0, 1):
        at = slice(head * 128, head * 128 + 128)
        noisy = sum(nin[z * 2 + core].astype(wide) for z in (head, head + 2) for core in (0, 1))
        dkn[:, at] = noisy[:, :128].astype(jnp.bfloat16)
        dvn[:, at] = noisy[:, 128:].astype(jnp.bfloat16)
    for c in deep_z:
        c.wait_recv()
    for head in (0, 1):
        at = slice(head * 128, head * 128 + 128)
        clean = zin[head].astype(wide) + zin[head + 2].astype(wide)
        dkc[:, at] = clean[:, :128].astype(jnp.bfloat16)
        dvc[:, at] = clean[:, 128:].astype(jnp.bfloat16)
    for c in out.made:
        c.wait_send()


GATHER_COPIES = 16 + 21 + 24 + 6 + 3


def gather(dq, dnkv, dkv):
    half = jnp.bfloat16
    vmem = pl.BlockSpec(memory_space=pltpu.VMEM)
    hbm = pl.BlockSpec(memory_space=pl.ANY)
    return pl.pallas_call(
        gather_kernel,
        out_shape=(jax.ShapeDtypeStruct((64, 2048), half),) * 2 + (jax.ShapeDtypeStruct((64, 256), half),) * 4,
        in_specs=[hbm, hbm, vmem],
        out_specs=(hbm, hbm, vmem, vmem, vmem, vmem),
        scratch_shapes=[
            pltpu.VMEM((16, 4, 64, 256), half),
            pltpu.VMEM((16, 4, 64, 256), half),
            pltpu.VMEM((2, 5, 3, 2, 64, 256), half),
            pltpu.VMEM((2, 7, 2, 64, 256), half),
            pltpu.VMEM((4, 64, 256), half),
            pltpu.VMEM((4, 64, 256), half),
            pltpu.VMEM((8, 64, 256), half),
            pltpu.SemaphoreType.DMA((GATHER_COPIES,)),
            pltpu.SemaphoreType.DMA((GATHER_COPIES,)),
            pltpu.SemaphoreType.DMA((3,)),
        ],
        compiler_params=pltpu.CompilerParams(collective_id=1, has_side_effects=True, vmem_limit_bytes=14 * MIB),
        name="gather",
    )(dq, dnkv, dkv)


def local(qn, qc, kn, vn, kc, vc, dn, dc, block_ids, stretch_order):
    q, nkv, kv = spread(qn, qc, dn, dc, kn, vn, kc, vc)
    dq, dnkv, dkv = attention(stretch_order, block_ids, q, nkv, kv.reshape(128, 64, 256), tile=(2048, 1024, 512))
    return gather(dq, dnkv, dkv.reshape(16, 2, 4, 64, 256))


def solution(mesh):
    both = P(("seq", "head"), None)
    return jax.shard_map(
        local, mesh=mesh, in_specs=(both,) * 8 + (P(), P()), out_specs=(both,) * 6, check_vma=False
    )
```

```python
import functools, math
import jax
import jax.numpy as jnp
from jax import lax
from jax.experimental import pallas as pl
from jax.experimental.pallas import tpu as pltpu
from jax.sharding import PartitionSpec as P

NEG = -1e30
MIB = 1 << 20


def attention_kernel(sizes, order_hbm, ids_hbm, q, nkv, kv, dq, dnkv, dkv, rows_kv, cols_k, acc, sbuf, pbuf, qtot, order, ids, sem):
    facts = [pltpu.make_async_copy(order_hbm, order, sem.at[0]), pltpu.make_async_copy(ids_hbm, ids, sem.at[1])]
    for c in facts:
        c.start()
    yx = lax.axis_index("seq") // 4
    stretches, chunk, _ = kv.shape
    tokens = stretches * chunk
    scale = 1.0 / math.sqrt(128)
    to_exp2 = scale * math.log2(math.e)
    wide = jnp.float32
    half = jnp.bfloat16
    unit = sizes[-1]

    def each_chunk(body):
        def some(row, _):
            for j in range(8):
                at = (j // 2 % 2) * 4 + (j // 4) * 2 + j % 2
                body(row * 8 + at, order[row * 8 + j])
            return 0

        lax.fori_loop(0, stretches // 8, some, 0)

    def chunk_rows(p):
        return pl.ds(pl.multiple_of(p * chunk, chunk), chunk)

    def clear(t, _):
        acc[pl.ds(pl.multiple_of(t * 1024, 1024), 1024), :] = jnp.zeros((1024, 256), wide)
        return 0

    lax.fori_loop(0, tokens // 1024, clear, 0)

    for c in facts:
        c.wait()

    def bring(at, p):
        rows_kv[chunk_rows(p), :] = kv[at]

    each_chunk(bring)

    def turn(t, _):
        for i in range(1024 // unit):
            rows = pl.ds(pl.multiple_of(t * 1024 + i * unit, unit), unit)
            cols_k[t * (1024 // unit) + i] = rows_kv[rows, :128].T
        return 0

    lax.fori_loop(0, tokens // 1024, turn, 0)

    def fold(values, op):
        return op(values.reshape(values.shape[0] // 8, 8, values.shape[1]), axis=0)

    def dot(a, b):
        return jnp.dot(a, b, preferred_element_type=wide)

    def one(g, _):
        c = yx * 8 + (g // 4) * 4 + (g % 2) * 2 + (g // 2) % 2
        p = order[c]
        limit = p * chunk
        first = ids[limit]
        split = jnp.int32(0)
        for bit in (64, 32, 16, 8, 4, 2, 1):
            near = jnp.minimum(split + bit, chunk)
            hit = jnp.logical_and(split + bit <= chunk, ids[limit + near - 1] == first)
            split = jnp.where(hit, split + bit, split)
        units = (limit + unit - 1) // unit

        def walk(body, state):
            start = jnp.int32(0)
            left = units
            for size in sizes:
                many = size // unit
                count = left // many
                state = lax.fori_loop(0, count, lambda t, s: body(pl.multiple_of(start + t * size, unit), size, s), state)
                start = start + count * size
                left = left - count * many
            return state

        stack = lambda a, b: jnp.concatenate([q[g, a, :, :128], q[g, a, :, 128:], q[g, b, :, :128], q[g, b, :, 128:]], axis=0)
        q_t = stack(0, 1).T
        d_t = stack(2, 3).T
        diag_kv = jnp.concatenate([rows_kv[chunk_rows(p), :], nkv[g]], axis=0)
        diag_k, diag_v = diag_kv[:, :128], diag_kv[:, 128:]
        key_at = lax.broadcasted_iota(jnp.int32, (128, 256), 0)
        row_at = lax.broadcasted_iota(jnp.int32, (128, 256), 1)
        key_run = jnp.where(key_at % chunk >= split, 1, 0)
        row_run = jnp.where(row_at % chunk >= split, 1, 0)
        clean_row = jnp.where(row_at >= 128, 1, 0)
        gap = jnp.where(key_at < chunk, row_run + clean_row - key_run, jnp.where(key_run == row_run, 1, 0) - clean_row)
        diag_s = jnp.where(gap > 0, dot(diag_k, q_t), NEG)

        def scores(at, size, top):
            rows = pl.ds(at, size)
            s = dot(rows_kv[rows, :128], q_t)
            s = jnp.where(lax.broadcasted_iota(jnp.int32, (size, 256), 0) < limit - at, s, NEG)
            sbuf[rows, :] = s
            return jnp.maximum(top, fold(s, jnp.max))

        top = walk(scores, fold(diag_s, jnp.max))
        top = jnp.max(top, axis=0, keepdims=True)
        diag_p = jnp.exp2((diag_s - top) * to_exp2)
        diag_dp = dot(diag_v, d_t)

        def sums(at, size, state):
            total, dots = state
            rows = pl.ds(at, size)
            dp = dot(rows_kv[rows, 128:], d_t)
            e = jnp.exp2((sbuf[rows, :] - top) * to_exp2)
            sbuf[rows, :] = e
            pbuf[rows, :] = dp
            return (total + fold(e, jnp.sum), dots + fold(e * dp, jnp.sum))

        total, dots = walk(sums, (fold(diag_p, jnp.sum), fold(diag_p * diag_dp, jnp.sum)))
        total = jnp.sum(total, axis=0, keepdims=True)
        over = 1.0 / total
        mean = jnp.sum(dots, axis=0, keepdims=True) * over
        q_s = (q_t.astype(wide) * over).T.astype(half)
        d_s = (d_t.astype(wide) * over).T.astype(half)

        def grads(e, dp, keys_t):
            ds = (e * (dp - mean)).astype(half)
            return dot(keys_t, ds), dot(ds, q_s), dot(e.astype(half), d_s)

        gq, gk, gv = grads(diag_p, diag_dp, diag_k.T)
        qtot[...] = gq
        acc[chunk_rows(p), :128] += gk[:chunk]
        acc[chunk_rows(p), 128:] += gv[:chunk]
        dnkv[g, :, :128] = (gk[chunk:] * scale).astype(half)
        dnkv[g, :, 128:] = gv[chunk:].astype(half)

        def back(at, size, _):
            rows = pl.ds(at, size)
            keys_t = jnp.concatenate([cols_k[at // unit + i] for i in range(size // unit)], axis=1)
            gq, gk, gv = grads(sbuf[rows, :], pbuf[rows, :], keys_t)
            qtot[...] += gq
            acc[rows, :128] += gk
            acc[rows, 128:] += gv
            return 0

        walk(back, 0)
        out = (qtot[...] * (over * scale)).T.astype(half)
        for i in range(4):
            dq[g, i // 2, :, (i % 2) * 128:(i % 2) * 128 + 128] = out[i * 64:i * 64 + 64]
        return 0

    lax.fori_loop(0, q.shape[0], one, 0)

    def give(at, p):
        dkv[at, :, :128] = (acc[chunk_rows(p), :128] * scale).astype(half)
        dkv[at, :, 128:] = acc[chunk_rows(p), 128:].astype(half)

    each_chunk(give)


def attention(order, ids, q, nkv, kv, tile=(2048, 1024)):
    tokens = kv.shape[0] * kv.shape[1]
    vmem = pl.BlockSpec(memory_space=pltpu.VMEM)
    hbm = pl.BlockSpec(memory_space=pltpu.HBM)
    half = jnp.bfloat16
    wide = jnp.float32
    return pl.pallas_call(
        functools.partial(attention_kernel, tile),
        out_shape=(
            jax.ShapeDtypeStruct((8, 2, 64, 256), half),
            jax.ShapeDtypeStruct((8, 64, 256), half),
            jax.ShapeDtypeStruct(kv.shape, half),
        ),
        in_specs=[hbm, hbm, vmem, vmem, vmem],
        out_specs=(vmem, vmem, vmem),
        scratch_shapes=[
            pltpu.VMEM((tokens, 256), half),
            pltpu.VMEM((tokens // tile[-1], 128, tile[-1]), half),
            pltpu.VMEM((tokens, 256), wide),
            pltpu.VMEM((tokens, 256), wide),
            pltpu.VMEM((tokens, 256), wide),
            pltpu.VMEM((128, 256), wide),
            pltpu.SMEM(order.shape, jnp.int32),
            pltpu.SMEM(ids.shape, jnp.int32),
            pltpu.SemaphoreType.DMA((2,)),
        ],
        compiler_params=pltpu.CompilerParams(vmem_limit_bytes=42 * MIB),
        name="attention",
    )(order, ids, q, nkv, kv)
MESH = pl.DeviceIdType.MESH


class Spot:
    def __init__(self):
        seq, head = lax.axis_index("seq"), lax.axis_index("head")
        self.y, self.x, self.core = seq // 16, (seq // 4) % 4, seq % 2
        self.z = ((seq // 2) % 2) * 2 + head
        self.sign = 1 - 2 * self.core

    def at(self, y, x, z, core):
        return (((y * 4 + x) * 2 + z // 2) * 2 + core, z % 2)

    def member(self, turn, flip):
        z = (self.z + turn) % 4
        core = (self.core + flip) % 2
        return z, core

    def along(self, axis, steps):
        y = (self.y + steps * self.sign + 4) % 4 if axis == "y" else self.y
        x = (self.x + steps * self.sign + 4) % 4 if axis == "x" else self.x
        return self.at(y, x, self.z, self.core)

    def row(self, dy, dx):
        return ((self.y + dy * self.sign + 4) % 4) * 4 + (self.x + dx * self.sign + 4) % 4


def greet(spot):
    barrier = pltpu.get_barrier_semaphore()
    others = [spot.member(t, f) for t in range(4) for f in range(2) if t or f]
    ids = [spot.at(spot.y, spot.x, z, c) for z, c in others]
    ids += [spot.along(a, s) for a in ("y", "x") for s in (1, -1)]
    for d in ids:
        pl.semaphore_signal(barrier, inc=1, device_id=d, device_id_type=MESH)
    pl.semaphore_wait(barrier, len(ids))


class Sender:
    def __init__(self, send, recv):
        self.send, self.recv, self.made = send, recv, []

    def go(self, src, dst, device):
        n = len(self.made)
        copy = pltpu.make_async_remote_copy(
            src_ref=src, dst_ref=dst, send_sem=self.send.at[n], recv_sem=self.recv.at[n],
            device_id=device, device_id_type=MESH,
        )
        copy.start()
        self.made.append(copy)
        return copy


def spread_kernel(qn, qc, dn, dc, kn, vn, kc, vc, q, nkv, kv, send, recv, own):
    spot = Spot()
    greet(spot)
    out = Sender(send, recv)
    mine = spot.z * 2 + spot.core
    here = spot.row(0, 0)

    def pieces(z, core):
        head = pl.ds(pl.multiple_of((z % 2) * 128, 128), 128)
        cols = pl.ds(pl.multiple_of(((z % 2) * 4 + (z // 2) * 2 + core) * 256, 256), 256)
        found = [(a.at[:, cols], q.at[mine, i]) for i, a in enumerate((qn, qc, dn, dc))]
        found += [(kn.at[:, head], nkv.at[mine, :, :128]), (vn.at[:, head], nkv.at[mine, :, 128:])]
        return found

    def clean(z):
        head = pl.ds(pl.multiple_of((z % 2) * 128, 128), 128)
        slot = kv.at[here, spot.core, spot.z]
        return [(kc.at[:, head], slot.at[:, :128]), (vc.at[:, head], slot.at[:, 128:])]

    local = [pltpu.make_async_copy(s, d, own.at[i]) for i, (s, d) in enumerate(clean(spot.z) + pieces(spot.z, spot.core))]
    for c in local:
        c.start()
    first = []
    for turn in (1, 3, 2):
        z, _ = spot.member(turn, 0)
        for s, d in clean(z):
            first.append(out.go(s, d, spot.at(spot.y, spot.x, z, spot.core)))

    def send_group(turn, flip):
        z, core = spot.member(turn, flip)
        for s, d in pieces(z, core):
            out.go(s, d, spot.at(spot.y, spot.x, z, core))

    for turn, flip in ((2, 0), (2, 1), (1, 0), (3, 0), (1, 1), (3, 1), (0, 1)):
        send_group(turn, flip)
    local[0].wait()
    local[1].wait()
    for c in first:
        c.wait_recv()

    sibling = spot.at(spot.y, spot.x, spot.z, 1 - spot.core)
    last = []
    done = list(first)

    def block(dy, dx, half):
        return kv.at[spot.row(dy, dx), spot.core, pl.ds(half * 2, 2)]

    def offer(dy, dx, half, axis, steps):
        b = block(dy, dx, half)
        c = out.go(b, b, spot.along(axis, steps))
        return c

    def twin(dy, dx, half):
        b = block(dy, dx, half)
        last.append(out.go(b, b, sibling))

    def got(c):
        c.wait_recv()
        done.append(c)

    pair = {}
    for half, axis in ((0, "x"), (1, "y")):
        pair[half] = (offer(0, 0, half, axis, 1), offer(0, 0, half, axis, -1))
    late = {}
    for half, axis in ((0, "y"), (1, "x")):
        late[half, 0] = (offer(0, 0, half, axis, 1), offer(0, 0, half, axis, -1))
    for half in (0, 1):
        twin(0, 0, half)

    def spot_of(half, first_step, second_step):
        return (second_step, first_step) if half == 0 else (first_step, second_step)

    hop = {}
    for half, axis in ((0, "x"), (1, "y")):
        got(pair[half][0])
        dy, dx = spot_of(half, -1, 0)
        hop[half] = offer(dy, dx, half, axis, 1)
        other = "y" if half == 0 else "x"
        late[half, -1] = (offer(dy, dx, half, other, 1), offer(dy, dx, half, other, -1))
        twin(dy, dx, half)
    for half in (0, 1):
        got(pair[half][1])
        dy, dx = spot_of(half, 1, 0)
        other = "y" if half == 0 else "x"
        late[half, 1] = (offer(dy, dx, half, other, 1), offer(dy, dx, half, other, -1))
        twin(dy, dx, half)
    far = {}

    def second(step):
        for half in (0, 1):
            other = "y" if half == 0 else "x"
            got(late[half, step][0])
            dy, dx = spot_of(half, step, -1)
            far[half, step] = offer(dy, dx, half, other, 1)
            twin(dy, dx, half)

    second(0)
    for half in (0, 1):
        got(hop[half])
        dy, dx = spot_of(half, 2, 0)
        other = "y" if half == 0 else "x"
        late[half, 2] = (offer(dy, dx, half, other, 1), offer(dy, dx, half, other, -1))
        twin(dy, dx, half)
    for step in (-1, 1, 2):
        second(step)
    for step in (0, -1, 1, 2):
        for half in (0, 1):
            got(late[half, step][1])
            dy, dx = spot_of(half, step, 1)
            twin(dy, dx, half)
    for step in (0, -1, 1, 2):
        for half in (0, 1):
            got(far[half, step])
            dy, dx = spot_of(half, step, 2)
            twin(dy, dx, half)
    for c in local[2:]:
        c.wait()
    for c in out.made:
        if not any(c is d for d in done):
            c.wait_recv()
    for c in out.made:
        c.wait_send()


SPREAD_COPIES = 6 + 42 + 2 * (3 + 12 + 16)


def spread(qn, qc, dn, dc, kn, vn, kc, vc):
    half = jnp.bfloat16
    hbm = pl.BlockSpec(memory_space=pl.ANY)
    return pl.pallas_call(
        spread_kernel,
        out_shape=(
            jax.ShapeDtypeStruct((8, 4, 64, 256), half),
            jax.ShapeDtypeStruct((8, 64, 256), half),
            jax.ShapeDtypeStruct((16, 2, 4, 64, 256), half),
        ),
        in_specs=[pl.BlockSpec(memory_space=pltpu.HBM)] * 8,
        out_specs=(hbm,) * 3,
        scratch_shapes=[
            pltpu.SemaphoreType.DMA((SPREAD_COPIES,)),
            pltpu.SemaphoreType.DMA((SPREAD_COPIES,)),
            pltpu.SemaphoreType.DMA((8,)),
        ],
        compiler_params=pltpu.CompilerParams(collective_id=0, has_side_effects=True, vmem_limit_bytes=4 * MIB),
        name="spread",
    )(qn, qc, dn, dc, kn, vn, kc, vc)


def gather_kernel(dq, dnkv, dkv, dqn, dqc, nin, zin, twins, parts, slots, stage, zout, send, recv, own):
    spot = Spot()
    greet(spot)
    out = Sender(send, recv)
    mine = spot.z * 2 + spot.core
    sibling = spot.at(spot.y, spot.x, spot.z, 1 - spot.core)
    cols = pl.ds(pl.multiple_of(((spot.z % 2) * 4 + (spot.z // 2) * 2 + spot.core) * 256, 256), 256)
    wide = jnp.float32

    twin = {}
    lanes = (2, -1, 1, 0)
    order = []
    for steps in ((2,), (-1, 1), (0,)):
        for lane in lanes:
            for pair in [(s, lane) for s in steps] + [(lane, s) for s in steps]:
                if pair not in order:
                    order.append(pair)

    for dy, dx in order:
        r = spot.row(-dy, -dx)
        twin[dy, dx] = out.go(dkv.at[r, 1 - spot.core], twins.at[r], sibling)

    def send_group(turn, flip):
        z, core = spot.member(turn, flip)
        to = z * 2 + core
        device = spot.at(spot.y, spot.x, z, core)
        return [
            out.go(dq.at[to, 0], dqn.at[:, cols], device),
            out.go(dq.at[to, 1], dqc.at[:, cols], device),
            out.go(dnkv.at[to], nin.at[mine], device),
        ]

    group = []
    for turn, flip in ((2, 0), (2, 1), (1, 0), (3, 0), (1, 1), (3, 1), (0, 1)):
        group += send_group(turn, flip)
    local = [
        pltpu.make_async_copy(dq.at[mine, 0], dqn.at[:, cols], own.at[0]),
        pltpu.make_async_copy(dq.at[mine, 1], dqc.at[:, cols], own.at[1]),
        pltpu.make_async_copy(dnkv.at[mine], nin.at[mine], own.at[2]),
    ]
    for c in local:
        c.start()

    ready = set()

    def part(dy, dx):
        r = spot.row(dy, dx)
        if (dy, dx) not in ready:
            ready.add((dy, dx))
            twin[dy, dx].wait_recv()
            parts[r] = (dkv[r, spot.core].astype(wide) + twins[r].astype(wide)).astype(jnp.bfloat16)
        return r

    def owner(half, lane, step):
        return (step, lane) if half == 0 else (lane, step)

    first_axis = ("y", "x")
    sent = {}
    for lane in lanes:
        for half in (0, 1):
            r = part(*owner(half, lane, 2))
            n = lanes.index(lane)
            sent[half, lane, 0] = out.go(parts.at[r, pl.ds(half * 2, 2)], slots.at[half, n, 0], spot.along(first_axis[half], -1))
    for lane in lanes:
        for half in (0, 1):
            n = lanes.index(lane)
            r = part(*owner(half, lane, -1))
            part(*owner(half, lane, 1))
            sent[half, lane, 0].wait_recv()
            stage[half, n] = (parts[r, half * 2:half * 2 + 2].astype(wide) + slots[half, n, 0].astype(wide)).astype(jnp.bfloat16)
            sent[half, lane, 1] = out.go(stage.at[half, n], slots.at[half, n, 1], spot.along(first_axis[half], -1))
            r = part(*owner(half, lane, 1))
            sent[half, lane, 2] = out.go(parts.at[r, pl.ds(half * 2, 2)], slots.at[half, n, 2], spot.along(first_axis[half], 1))

    def total(half, lane):
        n = lanes.index(lane)
        r = part(*owner(half, lane, 0))
        sent[half, lane, 1].wait_recv()
        sent[half, lane, 2].wait_recv()
        return parts[r, half * 2:half * 2 + 2].astype(wide) + slots[half, n, 1].astype(wide) + slots[half, n, 2].astype(wide)

    second_axis = ("x", "y")
    deep = {}
    for half in (0, 1):
        stage[half, 4] = total(half, 2).astype(jnp.bfloat16)
        deep[half, 0] = out.go(stage.at[half, 4], slots.at[half, 4, 0], spot.along(second_axis[half], -1))
    passed = {}
    for half in (0, 1):
        passed[half] = total(half, -1)
        deep[half, 0].wait_recv()
        stage[half, 5] = (passed[half] + slots[half, 4, 0].astype(wide)).astype(jnp.bfloat16)
        deep[half, 1] = out.go(stage.at[half, 5], slots.at[half, 4, 1], spot.along(second_axis[half], -1))
    for half in (0, 1):
        stage[half, 6] = total(half, 1).astype(jnp.bfloat16)
        deep[half, 2] = out.go(stage.at[half, 6], slots.at[half, 4, 2], spot.along(second_axis[half], 1))
    for half in (0, 1):
        mid = total(half, 0)
        deep[half, 1].wait_recv()
        deep[half, 2].wait_recv()
        zout[half * 2:half * 2 + 2] = (mid + slots[half, 4, 1].astype(wide) + slots[half, 4, 2].astype(wide)).astype(jnp.bfloat16)
    deep_z = []
    for turn in (2, 1, 3):
        z, _ = spot.member(turn, 0)
        deep_z.append(out.go(zout.at[z], zin.at[spot.z], spot.at(spot.y, spot.x, z, spot.core)))
    zin[spot.z] = zout[spot.z]

    for c in group + deep_z:
        c.wait_recv()
    for c in local:
        c.wait()
    for c in out.made:
        c.wait_send()


GATHER_COPIES = 16 + 21 + 24 + 6 + 3


def gather(dq, dnkv, dkv):
    half = jnp.bfloat16
    vmem = pl.BlockSpec(memory_space=pltpu.VMEM)
    hbm = pl.BlockSpec(memory_space=pl.ANY)
    return pl.pallas_call(
        gather_kernel,
        out_shape=(
            jax.ShapeDtypeStruct((64, 2048), half),
            jax.ShapeDtypeStruct((64, 2048), half),
            jax.ShapeDtypeStruct((8, 64, 256), half),
            jax.ShapeDtypeStruct((4, 64, 256), half),
        ),
        in_specs=[hbm, hbm, vmem],
        out_specs=(hbm, hbm, vmem, vmem),
        scratch_shapes=[
            pltpu.VMEM((16, 4, 64, 256), half),
            pltpu.VMEM((16, 4, 64, 256), half),
            pltpu.VMEM((2, 5, 3, 2, 64, 256), half),
            pltpu.VMEM((2, 7, 2, 64, 256), half),
            pltpu.VMEM((4, 64, 256), half),
            pltpu.SemaphoreType.DMA((GATHER_COPIES,)),
            pltpu.SemaphoreType.DMA((GATHER_COPIES,)),
            pltpu.SemaphoreType.DMA((3,)),
        ],
        compiler_params=pltpu.CompilerParams(collective_id=1, has_side_effects=True, vmem_limit_bytes=14 * MIB),
        name="gather",
    )(dq, dnkv, dkv)


def finish_kernel(dqn, dqc, nin, zin, dqn_out, dqc_out, dkn, dvn, dkc, dvc, sem):
    copies = [pltpu.make_async_copy(dqn, dqn_out, sem.at[0]), pltpu.make_async_copy(dqc, dqc_out, sem.at[1])]
    for c in copies:
        c.start()
    wide = jnp.float32
    for head in (0, 1):
        at = slice(head * 128, head * 128 + 128)
        noisy = sum(nin[z * 2 + core].astype(wide) for z in (head, head + 2) for core in (0, 1))
        dkn[:, at] = noisy[:, :128].astype(jnp.bfloat16)
        dvn[:, at] = noisy[:, 128:].astype(jnp.bfloat16)
        clean = zin[head].astype(wide) + zin[head + 2].astype(wide)
        dkc[:, at] = clean[:, :128].astype(jnp.bfloat16)
        dvc[:, at] = clean[:, 128:].astype(jnp.bfloat16)
    for c in copies:
        c.wait()


def finish(dqn, dqc, nin, zin):
    half = jnp.bfloat16
    vmem = pl.BlockSpec(memory_space=pltpu.VMEM)
    hbm = pl.BlockSpec(memory_space=pl.ANY)
    return pl.pallas_call(
        finish_kernel,
        out_shape=(jax.ShapeDtypeStruct((64, 2048), half),) * 2 + (jax.ShapeDtypeStruct((64, 256), half),) * 4,
        in_specs=[hbm, hbm, vmem, vmem],
        out_specs=(hbm, hbm, vmem, vmem, vmem, vmem),
        scratch_shapes=[pltpu.SemaphoreType.DMA((2,))],
        compiler_params=pltpu.CompilerParams(vmem_limit_bytes=4 * MIB),
        name="finish",
    )(dqn, dqc, nin, zin)


def local(qn, qc, kn, vn, kc, vc, dn, dc, block_ids, stretch_order):
    far = lambda *arrays: [pltpu.with_memory_space_constraint(a, pltpu.HBM) for a in arrays]
    q, nkv, kv = spread(*far(qn, qc, dn, dc, kn, vn, kc, vc))
    dq, dnkv, dkv = attention(*far(stretch_order, block_ids), q, nkv, kv.reshape(128, 64, 256), tile=(2048, 1024, 512))
    return finish(*gather(dq, dnkv, dkv.reshape(16, 2, 4, 64, 256)))


def solution(mesh):
    both = P(("seq", "head"), None)
    return jax.shard_map(
        local, mesh=mesh, in_specs=(both,) * 8 + (P(), P()), out_specs=(both,) * 6, check_vma=False
    )
```

```python
import functools, math
import jax
import jax.numpy as jnp
from jax import lax
from jax.experimental import pallas as pl
from jax.experimental.pallas import tpu as pltpu
from jax.sharding import PartitionSpec as P

NEG = -1e30
MIB = 1 << 20


def attention_kernel(sizes, order_hbm, ids_hbm, q, nkv, kv, dq, dnkv, dkv, rows_kv, cols_k, acc, sbuf, pbuf, qtot, turned, diag, order, ids, sem):
    facts = [pltpu.make_async_copy(order_hbm, order, sem.at[0]), pltpu.make_async_copy(ids_hbm, ids, sem.at[1])]
    for c in facts:
        c.start()
    yx = lax.axis_index("seq") // 4
    stretches, chunk, _ = kv.shape
    tokens = stretches * chunk
    scale = 1.0 / math.sqrt(128)
    to_exp2 = scale * math.log2(math.e)
    wide = jnp.float32
    half = jnp.bfloat16
    unit = sizes[-1]

    def each_chunk(body):
        def some(row, _):
            for j in range(8):
                at = (j // 2 % 2) * 4 + (j // 4) * 2 + j % 2
                body(row * 8 + at, order[row * 8 + j])
            return 0

        lax.fori_loop(0, stretches // 8, some, 0)

    def chunk_rows(p):
        return pl.ds(pl.multiple_of(p * chunk, chunk), chunk)

    def clear(t, _):
        acc[pl.ds(pl.multiple_of(t * 1024, 1024), 1024), :] = jnp.zeros((1024, 256), wide)
        return 0

    lax.fori_loop(0, tokens // 1024, clear, 0)

    for c in facts:
        c.wait()

    def bring(at, p):
        rows_kv[chunk_rows(p), :] = kv[at]

    each_chunk(bring)

    def turn(t, _):
        for i in range(1024 // unit):
            rows = pl.ds(pl.multiple_of(t * 1024 + i * unit, unit), unit)
            cols_k[t * (1024 // unit) + i] = rows_kv[rows, :128].T
        return 0

    lax.fori_loop(0, tokens // 1024, turn, 0)

    def fold(values, op):
        pieces = values.reshape(values.shape[0] // 16, 2, 8, values.shape[1])
        return op(op(pieces, axis=0), axis=0)

    def dot(a, b):
        return jnp.dot(a, b, preferred_element_type=wide)

    def stack(g, a, b):
        return jnp.concatenate([q[g, a, :, :128], q[g, a, :, 128:], q[g, b, :, :128], q[g, b, :, 128:]], axis=0)

    def position(g):
        return order[yx * 8 + (g // 4) * 4 + (g % 2) * 2 + (g // 2) % 2]

    key_at = lax.broadcasted_iota(jnp.int32, (128, 256), 0)
    row_at = lax.broadcasted_iota(jnp.int32, (128, 256), 1)
    clean_row = jnp.where(row_at >= 128, 1, 0)

    def prepare(g, _):
        p = position(g)
        limit = p * chunk
        first = ids[limit]
        split = jnp.int32(0)
        for bit in (64, 32, 16, 8, 4, 2, 1):
            near = jnp.minimum(split + bit, chunk)
            hit = jnp.logical_and(split + bit <= chunk, ids[limit + near - 1] == first)
            split = jnp.where(hit, split + bit, split)
        q_t = stack(g, 0, 1).T
        d_t = stack(g, 2, 3).T
        turned[g, 0] = q_t
        turned[g, 1] = d_t
        diag_kv = jnp.concatenate([rows_kv[chunk_rows(p), :], nkv[g]], axis=0)
        key_run = jnp.where(key_at % chunk >= split, 1, 0)
        row_run = jnp.where(row_at % chunk >= split, 1, 0)
        gap = jnp.where(key_at < chunk, row_run + clean_row - key_run, jnp.where(key_run == row_run, 1, 0) - clean_row)
        diag[g, 0] = jnp.where(gap > 0, dot(diag_kv[:, :128], q_t) * to_exp2, NEG)
        diag[g, 1] = dot(diag_kv[:, 128:], d_t)
        return 0

    lax.fori_loop(0, q.shape[0], prepare, 0, unroll=4)

    def one(g, _):
        p = position(g)
        limit = p * chunk
        units = (limit + unit - 1) // unit

        def walk(body, state):
            start = jnp.int32(0)
            left = units
            for size in sizes:
                many = size // unit
                count = left // many
                state = lax.fori_loop(0, count, lambda t, s: body(pl.multiple_of(start + t * size, unit), size, s), state)
                start = start + count * size
                left = left - count * many
            return state

        def scores(at, size, top):
            rows = pl.ds(at, size)
            s = dot(rows_kv[rows, :128], turned[g, 0])
            s = jnp.where(lax.broadcasted_iota(jnp.int32, (size, 256), 0) < limit - at, s, NEG) * to_exp2
            sbuf[rows, :] = s
            return jnp.maximum(top, fold(s, jnp.max))

        diag_s = diag[g, 0]
        top = walk(scores, fold(diag_s, jnp.max))
        top = jnp.max(top, axis=0, keepdims=True)
        diag_p = jnp.exp2(diag_s - top)
        diag_dp = diag[g, 1]

        def sums(at, size, state):
            total, dots = state
            rows = pl.ds(at, size)
            dp = dot(rows_kv[rows, 128:], turned[g, 1])
            e = jnp.exp2(sbuf[rows, :] - top)
            sbuf[rows, :] = e
            pbuf[rows, :] = dp
            return (total + fold(e, jnp.sum), dots + fold(e * dp, jnp.sum))

        total, dots = walk(sums, (fold(diag_p, jnp.sum), fold(diag_p * diag_dp, jnp.sum)))
        over = 1.0 / jnp.sum(total, axis=0, keepdims=True)
        mean = jnp.sum(dots, axis=0, keepdims=True) * over
        q_rows = stack(g, 0, 1)
        d_rows = stack(g, 2, 3)

        def grads(e, dp, keys_t):
            p = e * over
            ds = (p * (dp - mean)).astype(half)
            return dot(keys_t, ds), dot(ds, q_rows), dot(p.astype(half), d_rows)

        diag_k = jnp.concatenate([rows_kv[chunk_rows(p), :128], nkv[g, :, :128]], axis=0)
        gq, gk, gv = grads(diag_p, diag_dp, diag_k.T)
        qtot[g] = gq
        acc[chunk_rows(p), :128] += gk[:chunk]
        acc[chunk_rows(p), 128:] += gv[:chunk]
        dnkv[g, :, :128] = (gk[chunk:] * scale).astype(half)
        dnkv[g, :, 128:] = gv[chunk:].astype(half)

        def back(at, size, _):
            gqs = 0.0
            for part in range(size // 256):
                rows = pl.ds(at + part * 256, 256)
                keys_t = cols_k[at // unit + part * 256 // unit][:, part * 256 % unit:part * 256 % unit + 256]
                gq, gk, gv = grads(sbuf[rows, :], pbuf[rows, :], keys_t)
                gqs = gqs + gq
                acc[rows, :128] += gk
                acc[rows, 128:] += gv
            qtot[g] += gqs
            return 0

        walk(back, 0)
        return 0

    lax.fori_loop(0, q.shape[0], one, 0)

    def finish_q(g, _):
        out = (qtot[g] * scale).T.astype(half)
        for i in range(4):
            dq[g, i // 2, :, (i % 2) * 128:(i % 2) * 128 + 128] = out[i * 64:i * 64 + 64]
        return 0

    lax.fori_loop(0, q.shape[0], finish_q, 0, unroll=4)

    def give(at, p):
        dkv[at, :, :128] = (acc[chunk_rows(p), :128] * scale).astype(half)
        dkv[at, :, 128:] = acc[chunk_rows(p), 128:].astype(half)

    each_chunk(give)


def attention(order, ids, q, nkv, kv, tile=(2048, 1024)):
    tokens = kv.shape[0] * kv.shape[1]
    vmem = pl.BlockSpec(memory_space=pltpu.VMEM)
    hbm = pl.BlockSpec(memory_space=pltpu.HBM)
    half = jnp.bfloat16
    wide = jnp.float32
    return pl.pallas_call(
        functools.partial(attention_kernel, tile),
        out_shape=(
            jax.ShapeDtypeStruct((8, 2, 64, 256), half),
            jax.ShapeDtypeStruct((8, 64, 256), half),
            jax.ShapeDtypeStruct(kv.shape, half),
        ),
        in_specs=[hbm, hbm, vmem, vmem, vmem],
        out_specs=(vmem, vmem, vmem),
        scratch_shapes=[
            pltpu.VMEM((tokens, 256), half),
            pltpu.VMEM((tokens // tile[-1], 128, tile[-1]), half),
            pltpu.VMEM((tokens, 256), wide),
            pltpu.VMEM((tokens, 256), wide),
            pltpu.VMEM((tokens, 256), wide),
            pltpu.VMEM((8, 128, 256), wide),
            pltpu.VMEM((8, 2, 128, 256), half),
            pltpu.VMEM((8, 2, 128, 256), wide),
            pltpu.SMEM(order.shape, jnp.int32),
            pltpu.SMEM(ids.shape, jnp.int32),
            pltpu.SemaphoreType.DMA((2,)),
        ],
        compiler_params=pltpu.CompilerParams(vmem_limit_bytes=44 * MIB),
        name="attention",
    )(order, ids, q, nkv, kv)
MESH = pl.DeviceIdType.MESH


class Spot:
    def __init__(self):
        seq, head = lax.axis_index("seq"), lax.axis_index("head")
        self.y, self.x, self.core = seq // 16, (seq // 4) % 4, seq % 2
        self.z = ((seq // 2) % 2) * 2 + head
        self.sign = 1 - 2 * self.core

    def at(self, y, x, z, core):
        return (((y * 4 + x) * 2 + z // 2) * 2 + core, z % 2)

    def member(self, turn, flip):
        z = (self.z + turn) % 4
        core = (self.core + flip) % 2
        return z, core

    def along(self, axis, steps):
        y = (self.y + steps * self.sign + 4) % 4 if axis == "y" else self.y
        x = (self.x + steps * self.sign + 4) % 4 if axis == "x" else self.x
        return self.at(y, x, self.z, self.core)

    def row(self, dy, dx):
        return ((self.y + dy * self.sign + 4) % 4) * 4 + (self.x + dx * self.sign + 4) % 4


def greet(spot):
    barrier = pltpu.get_barrier_semaphore()
    others = [spot.member(t, f) for t in range(4) for f in range(2) if t or f]
    ids = [spot.at(spot.y, spot.x, z, c) for z, c in others]
    ids += [spot.along(a, s) for a in ("y", "x") for s in (1, -1)]
    for d in ids:
        pl.semaphore_signal(barrier, inc=1, device_id=d, device_id_type=MESH)
    pl.semaphore_wait(barrier, len(ids))


class Sender:
    def __init__(self, send, recv):
        self.send, self.recv, self.made = send, recv, []

    def go(self, src, dst, device):
        n = len(self.made)
        copy = pltpu.make_async_remote_copy(
            src_ref=src, dst_ref=dst, send_sem=self.send.at[n], recv_sem=self.recv.at[n],
            device_id=device, device_id_type=MESH,
        )
        copy.start()
        self.made.append(copy)
        return copy


def spread_kernel(qn, qc, dn, dc, kn, vn, kc, vc, q, nkv, kv, send, recv, own):
    spot = Spot()
    greet(spot)
    out = Sender(send, recv)
    mine = spot.z * 2 + spot.core
    here = spot.row(0, 0)

    def pieces(z, core):
        head = pl.ds(pl.multiple_of((z % 2) * 128, 128), 128)
        cols = pl.ds(pl.multiple_of(((z % 2) * 4 + (z // 2) * 2 + core) * 256, 256), 256)
        found = [(a.at[:, cols], q.at[mine, i]) for i, a in enumerate((qn, qc, dn, dc))]
        found += [(kn.at[:, head], nkv.at[mine, :, :128]), (vn.at[:, head], nkv.at[mine, :, 128:])]
        return found

    def clean(z):
        head = pl.ds(pl.multiple_of((z % 2) * 128, 128), 128)
        slot = kv.at[here, spot.core, spot.z]
        return [(kc.at[:, head], slot.at[:, :128]), (vc.at[:, head], slot.at[:, 128:])]

    local = [pltpu.make_async_copy(s, d, own.at[i]) for i, (s, d) in enumerate(clean(spot.z) + pieces(spot.z, spot.core))]
    for c in local:
        c.start()
    first = []
    for turn in (1, 3, 2):
        z, _ = spot.member(turn, 0)
        for s, d in clean(z):
            first.append(out.go(s, d, spot.at(spot.y, spot.x, z, spot.core)))

    def send_group(turn, flip):
        z, core = spot.member(turn, flip)
        for s, d in pieces(z, core):
            out.go(s, d, spot.at(spot.y, spot.x, z, core))

    local[0].wait()
    local[1].wait()
    for c in first:
        c.wait_recv()

    sibling = spot.at(spot.y, spot.x, spot.z, 1 - spot.core)
    last = []
    done = list(first)

    def block(dy, dx, half):
        return kv.at[spot.row(dy, dx), spot.core, pl.ds(half * 2, 2)]

    def offer(dy, dx, half, axis, steps):
        b = block(dy, dx, half)
        c = out.go(b, b, spot.along(axis, steps))
        return c

    def twin(dy, dx, half):
        b = block(dy, dx, half)
        last.append(out.go(b, b, sibling))

    def got(c):
        c.wait_recv()
        done.append(c)

    pair = {}
    for half, axis in ((0, "x"), (1, "y")):
        pair[half] = (offer(0, 0, half, axis, 1), offer(0, 0, half, axis, -1))
    late = {}
    for half, axis in ((0, "y"), (1, "x")):
        late[half, 0] = (offer(0, 0, half, axis, 1), offer(0, 0, half, axis, -1))
    for half in (0, 1):
        twin(0, 0, half)

    def spot_of(half, first_step, second_step):
        return (second_step, first_step) if half == 0 else (first_step, second_step)

    for turn, flip in ((1, 0), (3, 1), (2, 0), (3, 0), (1, 1), (2, 1), (0, 1)):
        send_group(turn, flip)
    hop = {}
    for half, axis in ((0, "x"), (1, "y")):
        got(pair[half][0])
        dy, dx = spot_of(half, -1, 0)
        hop[half] = offer(dy, dx, half, axis, 1)
        other = "y" if half == 0 else "x"
        late[half, -1] = (offer(dy, dx, half, other, 1), offer(dy, dx, half, other, -1))
        twin(dy, dx, half)
    for half in (0, 1):
        got(pair[half][1])
        dy, dx = spot_of(half, 1, 0)
        other = "y" if half == 0 else "x"
        late[half, 1] = (offer(dy, dx, half, other, 1), offer(dy, dx, half, other, -1))
        twin(dy, dx, half)
    far = {}

    def second(step):
        for half in (0, 1):
            other = "y" if half == 0 else "x"
            got(late[half, step][0])
            dy, dx = spot_of(half, step, -1)
            far[half, step] = offer(dy, dx, half, other, 1)
            twin(dy, dx, half)

    second(0)
    for half in (0, 1):
        got(hop[half])
        dy, dx = spot_of(half, 2, 0)
        other = "y" if half == 0 else "x"
        late[half, 2] = (offer(dy, dx, half, other, 1), offer(dy, dx, half, other, -1))
        twin(dy, dx, half)
    for step in (-1, 1, 2):
        second(step)
    for step in (0, -1, 1, 2):
        for half in (0, 1):
            got(late[half, step][1])
            dy, dx = spot_of(half, step, 1)
            twin(dy, dx, half)
    for step in (0, -1, 1, 2):
        for half in (0, 1):
            got(far[half, step])
            dy, dx = spot_of(half, step, 2)
            twin(dy, dx, half)
    for c in local[2:]:
        c.wait()
    for c in out.made:
        if not any(c is d for d in done):
            c.wait_recv()
    for c in out.made:
        c.wait_send()


SPREAD_COPIES = 6 + 42 + 2 * (3 + 12 + 16)


def spread(qn, qc, dn, dc, kn, vn, kc, vc):
    half = jnp.bfloat16
    hbm = pl.BlockSpec(memory_space=pl.ANY)
    return pl.pallas_call(
        spread_kernel,
        out_shape=(
            jax.ShapeDtypeStruct((8, 4, 64, 256), half),
            jax.ShapeDtypeStruct((8, 64, 256), half),
            jax.ShapeDtypeStruct((16, 2, 4, 64, 256), half),
        ),
        in_specs=[pl.BlockSpec(memory_space=pltpu.HBM)] * 8,
        out_specs=(hbm,) * 3,
        scratch_shapes=[
            pltpu.SemaphoreType.DMA((SPREAD_COPIES,)),
            pltpu.SemaphoreType.DMA((SPREAD_COPIES,)),
            pltpu.SemaphoreType.DMA((8,)),
        ],
        compiler_params=pltpu.CompilerParams(collective_id=0, has_side_effects=True, vmem_limit_bytes=4 * MIB),
        name="spread",
    )(qn, qc, dn, dc, kn, vn, kc, vc)


def gather_kernel(dq, dnkv, dkv, dqn, dqc, nin, zin, twins, parts, slots, stage, zout, send, recv, own):
    spot = Spot()
    greet(spot)
    out = Sender(send, recv)
    mine = spot.z * 2 + spot.core
    sibling = spot.at(spot.y, spot.x, spot.z, 1 - spot.core)
    cols = pl.ds(pl.multiple_of(((spot.z % 2) * 4 + (spot.z // 2) * 2 + spot.core) * 256, 256), 256)
    wide = jnp.float32

    twin = {}
    lanes = (2, -1, 1, 0)
    order = []
    for steps in ((2,), (-1, 1), (0,)):
        for lane in lanes:
            for pair in [(s, lane) for s in steps] + [(lane, s) for s in steps]:
                if pair not in order:
                    order.append(pair)

    for dy, dx in order:
        r = spot.row(-dy, -dx)
        twin[dy, dx] = out.go(dkv.at[r, 1 - spot.core], twins.at[r], sibling)

    def send_group(turn, flip):
        z, core = spot.member(turn, flip)
        to = z * 2 + core
        device = spot.at(spot.y, spot.x, z, core)
        return [
            out.go(dq.at[to, 0], dqn.at[:, cols], device),
            out.go(dq.at[to, 1], dqc.at[:, cols], device),
            out.go(dnkv.at[to], nin.at[mine], device),
        ]

    group = []
    for turn, flip in ((2, 0), (2, 1), (1, 0), (3, 0), (1, 1), (3, 1), (0, 1)):
        group += send_group(turn, flip)
    local = [
        pltpu.make_async_copy(dq.at[mine, 0], dqn.at[:, cols], own.at[0]),
        pltpu.make_async_copy(dq.at[mine, 1], dqc.at[:, cols], own.at[1]),
        pltpu.make_async_copy(dnkv.at[mine], nin.at[mine], own.at[2]),
    ]
    for c in local:
        c.start()

    ready = set()

    def part(dy, dx):
        r = spot.row(dy, dx)
        if (dy, dx) not in ready:
            ready.add((dy, dx))
            twin[dy, dx].wait_recv()
            parts[r] = (dkv[r, spot.core].astype(wide) + twins[r].astype(wide)).astype(jnp.bfloat16)
        return r

    def owner(half, lane, step):
        return (step, lane) if half == 0 else (lane, step)

    first_axis = ("y", "x")
    sent = {}
    for lane in lanes:
        for half in (0, 1):
            r = part(*owner(half, lane, 2))
            n = lanes.index(lane)
            sent[half, lane, 0] = out.go(parts.at[r, pl.ds(half * 2, 2)], slots.at[half, n, 0], spot.along(first_axis[half], -1))
    for lane in lanes:
        for half in (0, 1):
            n = lanes.index(lane)
            r = part(*owner(half, lane, -1))
            part(*owner(half, lane, 1))
            sent[half, lane, 0].wait_recv()
            stage[half, n] = (parts[r, half * 2:half * 2 + 2].astype(wide) + slots[half, n, 0].astype(wide)).astype(jnp.bfloat16)
            sent[half, lane, 1] = out.go(stage.at[half, n], slots.at[half, n, 1], spot.along(first_axis[half], -1))
            r = part(*owner(half, lane, 1))
            sent[half, lane, 2] = out.go(parts.at[r, pl.ds(half * 2, 2)], slots.at[half, n, 2], spot.along(first_axis[half], 1))

    def total(half, lane):
        n = lanes.index(lane)
        r = part(*owner(half, lane, 0))
        sent[half, lane, 1].wait_recv()
        sent[half, lane, 2].wait_recv()
        return parts[r, half * 2:half * 2 + 2].astype(wide) + slots[half, n, 1].astype(wide) + slots[half, n, 2].astype(wide)

    second_axis = ("x", "y")
    deep = {}
    for half in (0, 1):
        stage[half, 4] = total(half, 2).astype(jnp.bfloat16)
        deep[half, 0] = out.go(stage.at[half, 4], slots.at[half, 4, 0], spot.along(second_axis[half], -1))
    passed = {}
    for half in (0, 1):
        passed[half] = total(half, -1)
        deep[half, 0].wait_recv()
        stage[half, 5] = (passed[half] + slots[half, 4, 0].astype(wide)).astype(jnp.bfloat16)
        deep[half, 1] = out.go(stage.at[half, 5], slots.at[half, 4, 1], spot.along(second_axis[half], -1))
    for half in (0, 1):
        stage[half, 6] = total(half, 1).astype(jnp.bfloat16)
        deep[half, 2] = out.go(stage.at[half, 6], slots.at[half, 4, 2], spot.along(second_axis[half], 1))
    for half in (0, 1):
        mid = total(half, 0)
        deep[half, 1].wait_recv()
        deep[half, 2].wait_recv()
        zout[half * 2:half * 2 + 2] = (mid + slots[half, 4, 1].astype(wide) + slots[half, 4, 2].astype(wide)).astype(jnp.bfloat16)
    deep_z = []
    for turn in (2, 1, 3):
        z, _ = spot.member(turn, 0)
        deep_z.append(out.go(zout.at[z], zin.at[spot.z], spot.at(spot.y, spot.x, z, spot.core)))
    zin[spot.z] = zout[spot.z]

    for c in group + deep_z:
        c.wait_recv()
    for c in local:
        c.wait()
    for c in out.made:
        c.wait_send()


GATHER_COPIES = 16 + 21 + 24 + 6 + 3


def gather(dq, dnkv, dkv):
    half = jnp.bfloat16
    vmem = pl.BlockSpec(memory_space=pltpu.VMEM)
    hbm = pl.BlockSpec(memory_space=pl.ANY)
    return pl.pallas_call(
        gather_kernel,
        out_shape=(
            jax.ShapeDtypeStruct((64, 2048), half),
            jax.ShapeDtypeStruct((64, 2048), half),
            jax.ShapeDtypeStruct((8, 64, 256), half),
            jax.ShapeDtypeStruct((4, 64, 256), half),
        ),
        in_specs=[hbm, hbm, vmem],
        out_specs=(hbm, hbm, vmem, vmem),
        scratch_shapes=[
            pltpu.VMEM((16, 4, 64, 256), half),
            pltpu.VMEM((16, 4, 64, 256), half),
            pltpu.VMEM((2, 5, 3, 2, 64, 256), half),
            pltpu.VMEM((2, 7, 2, 64, 256), half),
            pltpu.VMEM((4, 64, 256), half),
            pltpu.SemaphoreType.DMA((GATHER_COPIES,)),
            pltpu.SemaphoreType.DMA((GATHER_COPIES,)),
            pltpu.SemaphoreType.DMA((3,)),
        ],
        compiler_params=pltpu.CompilerParams(collective_id=1, has_side_effects=True, vmem_limit_bytes=14 * MIB),
        name="gather",
    )(dq, dnkv, dkv)


def finish_kernel(dqn, dqc, nin, zin, dqn_out, dqc_out, dkn, dvn, dkc, dvc, sem):
    copies = [pltpu.make_async_copy(dqn, dqn_out, sem.at[0]), pltpu.make_async_copy(dqc, dqc_out, sem.at[1])]
    for c in copies:
        c.start()
    wide = jnp.float32
    for head in (0, 1):
        at = slice(head * 128, head * 128 + 128)
        noisy = sum(nin[z * 2 + core].astype(wide) for z in (head, head + 2) for core in (0, 1))
        dkn[:, at] = noisy[:, :128].astype(jnp.bfloat16)
        dvn[:, at] = noisy[:, 128:].astype(jnp.bfloat16)
        clean = zin[head].astype(wide) + zin[head + 2].astype(wide)
        dkc[:, at] = clean[:, :128].astype(jnp.bfloat16)
        dvc[:, at] = clean[:, 128:].astype(jnp.bfloat16)
    for c in copies:
        c.wait()


def finish(dqn, dqc, nin, zin):
    half = jnp.bfloat16
    vmem = pl.BlockSpec(memory_space=pltpu.VMEM)
    hbm = pl.BlockSpec(memory_space=pl.ANY)
    return pl.pallas_call(
        finish_kernel,
        out_shape=(jax.ShapeDtypeStruct((64, 2048), half),) * 2 + (jax.ShapeDtypeStruct((64, 256), half),) * 4,
        in_specs=[hbm, hbm, vmem, vmem],
        out_specs=(hbm, hbm, vmem, vmem, vmem, vmem),
        scratch_shapes=[pltpu.SemaphoreType.DMA((2,))],
        compiler_params=pltpu.CompilerParams(vmem_limit_bytes=4 * MIB),
        name="finish",
    )(dqn, dqc, nin, zin)


def local(qn, qc, kn, vn, kc, vc, dn, dc, block_ids, stretch_order):
    far = lambda *arrays: [pltpu.with_memory_space_constraint(a, pltpu.HBM) for a in arrays]
    q, nkv, kv = spread(*far(qn, qc, dn, dc, kn, vn, kc, vc))
    dq, dnkv, dkv = attention(*far(stretch_order, block_ids), q, nkv, kv.reshape(128, 64, 256), tile=(2048, 1024, 512))
    return finish(*gather(dq, dnkv, dkv.reshape(16, 2, 4, 64, 256)))


def solution(mesh):
    both = P(("seq", "head"), None)
    return jax.shard_map(
        local, mesh=mesh, in_specs=(both,) * 8 + (P(), P()), out_specs=(both,) * 6, check_vma=False
    )
```

```python
import functools, math
import jax
import jax.numpy as jnp
from jax import lax
from jax.experimental import pallas as pl
from jax.experimental.pallas import tpu as pltpu
from jax.sharding import PartitionSpec as P

NEG = -1e30
MIB = 1 << 20


def attention_kernel(sizes, order_hbm, ids_hbm, q, nkv, kv, dq, dnkv, dkv, rows_kv, cols_k, acc, ebuf, pbuf, tops, qtot, turned, diag, order, ids, sem):
    facts = [pltpu.make_async_copy(order_hbm, order, sem.at[0]), pltpu.make_async_copy(ids_hbm, ids, sem.at[1])]
    for c in facts:
        c.start()
    yx = lax.axis_index("seq") // 4
    stretches, chunk, _ = kv.shape
    tokens = stretches * chunk
    scale = 1.0 / math.sqrt(128)
    to_exp2 = scale * math.log2(math.e)
    wide = jnp.float32
    half = jnp.bfloat16
    unit = sizes[-1]

    def each_chunk(body):
        def some(row, _):
            for j in range(8):
                at = (j // 2 % 2) * 4 + (j // 4) * 2 + j % 2
                body(row * 8 + at, order[row * 8 + j])
            return 0

        lax.fori_loop(0, stretches // 8, some, 0)

    def chunk_rows(p):
        return pl.ds(pl.multiple_of(p * chunk, chunk), chunk)

    for c in facts:
        c.wait()

    def bring(at, p):
        rows_kv[chunk_rows(p), :] = kv[at]

    each_chunk(bring)

    def turn(t, _):
        acc[pl.ds(pl.multiple_of(t * 1024, 1024), 1024), :] = jnp.zeros((1024, 256), wide)
        for i in range(1024 // unit):
            rows = pl.ds(pl.multiple_of(t * 1024 + i * unit, unit), unit)
            cols_k[t * (1024 // unit) + i] = rows_kv[rows, :128].T
        return 0

    lax.fori_loop(0, tokens // 1024, turn, 0)

    def fold(values, op):
        pieces = values.reshape(values.shape[0] // 16, 2, 8, values.shape[1])
        return op(op(pieces, axis=0), axis=0)

    def dot(a, b):
        return jnp.dot(a, b, preferred_element_type=wide)

    def stack(g, a, b):
        return jnp.concatenate([q[g, a, :, :128], q[g, a, :, 128:], q[g, b, :, :128], q[g, b, :, 128:]], axis=0)

    def position(g):
        return order[yx * 8 + (g // 4) * 4 + (g % 2) * 2 + (g // 2) % 2]

    key_at = lax.broadcasted_iota(jnp.int32, (128, 256), 0)
    row_at = lax.broadcasted_iota(jnp.int32, (128, 256), 1)
    clean_row = jnp.where(row_at >= 128, 1, 0)

    def prepare(g, _):
        p = position(g)
        limit = p * chunk
        first = ids[limit]
        split = jnp.int32(0)
        for bit in (64, 32, 16, 8, 4, 2, 1):
            near = jnp.minimum(split + bit, chunk)
            hit = jnp.logical_and(split + bit <= chunk, ids[limit + near - 1] == first)
            split = jnp.where(hit, split + bit, split)
        q_t = stack(g, 0, 1).T
        d_t = stack(g, 2, 3).T
        turned[g, 0] = q_t
        turned[g, 1] = d_t
        diag_kv = jnp.concatenate([rows_kv[chunk_rows(p), :], nkv[g]], axis=0)
        key_run = jnp.where(key_at % chunk >= split, 1, 0)
        row_run = jnp.where(row_at % chunk >= split, 1, 0)
        gap = jnp.where(key_at < chunk, row_run + clean_row - key_run, jnp.where(key_run == row_run, 1, 0) - clean_row)
        diag[g, 0] = jnp.where(gap > 0, dot(diag_kv[:, :128], q_t) * to_exp2, NEG)
        diag[g, 1] = dot(diag_kv[:, 128:], d_t)
        return 0

    lax.fori_loop(0, q.shape[0], prepare, 0, unroll=4)

    def one(g, _):
        p = position(g)
        limit = p * chunk
        units = (limit + unit - 1) // unit

        def walk(body, state):
            start = jnp.int32(0)
            left = units
            for size in sizes:
                many = size // unit
                count = left // many
                state = lax.fori_loop(0, count, lambda t, s: body(pl.multiple_of(start + t * size, unit), size, s), state)
                start = start + count * size
                left = left - count * many
            return state

        def ahead(s, dp, state, keep):
            top, total, dots = state
            new = jnp.maximum(top, fold(s, jnp.max))
            fade = jnp.exp2(top - new)
            e = jnp.exp2(s.reshape(s.shape[0] // 8, 8, 256) - new[None]).reshape(s.shape)
            keep(e, dp, new)
            return new, total * fade + fold(e, jnp.sum), dots * fade + fold(e * dp, jnp.sum)

        def keep_diag(e, dp, top):
            diag[g, 0] = e
            tops[tokens // 256] = top

        def walk_ahead(at, size, state):
            for part in range(size // 256):
                rows = pl.ds(at + part * 256, 256)
                s = dot(rows_kv[rows, :128], turned[g, 0])
                dp = dot(rows_kv[rows, 128:], turned[g, 1])
                s = jnp.where(lax.broadcasted_iota(jnp.int32, (256, 256), 0) < limit - at - part * 256, s, NEG) * to_exp2

                def keep(e, dp, top):
                    ebuf[rows, :] = e
                    pbuf[rows, :] = dp
                    for i in range(256 // 256):
                        tops[at // 256 + part * (256 // 256) + i] = top

                state = ahead(s, dp, state, keep)
            return state

        none = jnp.zeros((8, 256), wide)
        state = ahead(diag[g, 0], diag[g, 1], (none + NEG, none, none), keep_diag)
        last, total, dots = walk(walk_ahead, state)
        top = jnp.max(last, axis=0, keepdims=True)
        fade = jnp.exp2(last - top)
        total, dots = total * fade, dots * fade
        over = 1.0 / jnp.sum(total, axis=0, keepdims=True)
        mean = jnp.sum(dots, axis=0, keepdims=True) * over
        q_rows = stack(g, 0, 1)
        d_rows = stack(g, 2, 3)

        def grads(e, dp, keys_t, piece_top):
            factor = jnp.exp2(piece_top - top) * over
            p = (e.reshape(e.shape[0] // 8, 8, 256) * factor[None]).reshape(e.shape)
            ds = (p * (dp - mean)).astype(half)
            return dot(keys_t, ds), dot(ds, q_rows), dot(p.astype(half), d_rows)

        diag_k = jnp.concatenate([rows_kv[chunk_rows(p), :128], nkv[g, :, :128]], axis=0)
        gq, gk, gv = grads(diag[g, 0], diag[g, 1], diag_k.T, tops[tokens // 256])
        qtot[g] = gq
        acc[chunk_rows(p), :128] += gk[:chunk]
        acc[chunk_rows(p), 128:] += gv[:chunk]
        dnkv[g, :, :128] = (gk[chunk:] * scale).astype(half)
        dnkv[g, :, 128:] = gv[chunk:].astype(half)

        def back(at, size, _):
            gqs = 0.0
            for part in range(size // 256):
                rows = pl.ds(at + part * 256, 256)
                keys_t = cols_k[at // unit + part * 256 // unit][:, part * 256 % unit:part * 256 % unit + 256]
                gq, gk, gv = grads(ebuf[rows, :], pbuf[rows, :], keys_t, tops[at // 256 + part])
                gqs = gqs + gq
                acc[rows, :128] += gk
                acc[rows, 128:] += gv
            qtot[g] += gqs
            return 0

        walk(back, 0)
        return 0

    lax.fori_loop(0, q.shape[0], one, 0)

    def finish_q(g, _):
        out = (qtot[g] * scale).T.astype(half)
        for i in range(4):
            dq[g, i // 2, :, (i % 2) * 128:(i % 2) * 128 + 128] = out[i * 64:i * 64 + 64]
        return 0

    lax.fori_loop(0, q.shape[0], finish_q, 0, unroll=4)

    def give(at, p):
        dkv[at, :, :128] = (acc[chunk_rows(p), :128] * scale).astype(half)
        dkv[at, :, 128:] = acc[chunk_rows(p), 128:].astype(half)

    each_chunk(give)


def attention(order, ids, q, nkv, kv, tile=(2048, 1024)):
    tokens = kv.shape[0] * kv.shape[1]
    vmem = pl.BlockSpec(memory_space=pltpu.VMEM)
    hbm = pl.BlockSpec(memory_space=pltpu.HBM)
    half = jnp.bfloat16
    wide = jnp.float32
    return pl.pallas_call(
        functools.partial(attention_kernel, tile),
        out_shape=(
            jax.ShapeDtypeStruct((8, 2, 64, 256), half),
            jax.ShapeDtypeStruct((8, 64, 256), half),
            jax.ShapeDtypeStruct(kv.shape, half),
        ),
        in_specs=[hbm, hbm, vmem, vmem, vmem],
        out_specs=(vmem, vmem, vmem),
        scratch_shapes=[
            pltpu.VMEM((tokens, 256), half),
            pltpu.VMEM((tokens // tile[-1], 128, tile[-1]), half),
            pltpu.VMEM((tokens, 256), wide),
            pltpu.VMEM((tokens, 256), wide),
            pltpu.VMEM((tokens, 256), wide),
            pltpu.VMEM((tokens // 256 + 1, 8, 256), wide),
            pltpu.VMEM((8, 128, 256), wide),
            pltpu.VMEM((8, 2, 128, 256), half),
            pltpu.VMEM((8, 2, 128, 256), wide),
            pltpu.SMEM(order.shape, jnp.int32),
            pltpu.SMEM(ids.shape, jnp.int32),
            pltpu.SemaphoreType.DMA((2,)),
        ],
        compiler_params=pltpu.CompilerParams(vmem_limit_bytes=42 * MIB),
        name="attention",
    )(order, ids, q, nkv, kv)
MESH = pl.DeviceIdType.MESH


class Spot:
    def __init__(self):
        seq, head = lax.axis_index("seq"), lax.axis_index("head")
        self.y, self.x, self.core = seq // 16, (seq // 4) % 4, seq % 2
        self.z = ((seq // 2) % 2) * 2 + head
        self.sign = 1 - 2 * self.core

    def at(self, y, x, z, core):
        return (((y * 4 + x) * 2 + z // 2) * 2 + core, z % 2)

    def member(self, turn, flip):
        z = (self.z + turn) % 4
        core = (self.core + flip) % 2
        return z, core

    def along(self, axis, steps):
        y = (self.y + steps * self.sign + 4) % 4 if axis == "y" else self.y
        x = (self.x + steps * self.sign + 4) % 4 if axis == "x" else self.x
        return self.at(y, x, self.z, self.core)

    def row(self, dy, dx):
        return ((self.y + dy * self.sign + 4) % 4) * 4 + (self.x + dx * self.sign + 4) % 4


def greet(spot):
    barrier = pltpu.get_barrier_semaphore()
    others = [spot.member(t, f) for t in range(4) for f in range(2) if t or f]
    ids = [spot.at(spot.y, spot.x, z, c) for z, c in others]
    ids += [spot.along(a, s) for a in ("y", "x") for s in (1, -1)]
    for d in ids:
        pl.semaphore_signal(barrier, inc=1, device_id=d, device_id_type=MESH)
    pl.semaphore_wait(barrier, len(ids))


class Sender:
    def __init__(self, send, recv):
        self.send, self.recv, self.made = send, recv, []

    def go(self, src, dst, device):
        n = len(self.made)
        copy = pltpu.make_async_remote_copy(
            src_ref=src, dst_ref=dst, send_sem=self.send.at[n], recv_sem=self.recv.at[n],
            device_id=device, device_id_type=MESH,
        )
        copy.start()
        self.made.append(copy)
        return copy


def spread_kernel(qn, qc, dn, dc, kn, vn, kc, vc, q, nkv, kv, send, recv, own):
    spot = Spot()
    greet(spot)
    out = Sender(send, recv)
    mine = spot.z * 2 + spot.core
    here = spot.row(0, 0)

    def pieces(z, core):
        head = pl.ds(pl.multiple_of((z % 2) * 128, 128), 128)
        cols = pl.ds(pl.multiple_of(((z % 2) * 4 + (z // 2) * 2 + core) * 256, 256), 256)
        found = [(a.at[:, cols], q.at[mine, i]) for i, a in enumerate((qn, qc, dn, dc))]
        found += [(kn.at[:, head], nkv.at[mine, :, :128]), (vn.at[:, head], nkv.at[mine, :, 128:])]
        return found

    def clean(z):
        head = pl.ds(pl.multiple_of((z % 2) * 128, 128), 128)
        slot = kv.at[here, spot.core, spot.z]
        return [(kc.at[:, head], slot.at[:, :128]), (vc.at[:, head], slot.at[:, 128:])]

    local = [pltpu.make_async_copy(s, d, own.at[i]) for i, (s, d) in enumerate(clean(spot.z) + pieces(spot.z, spot.core))]
    for c in local:
        c.start()
    first = []
    for turn in (1, 3, 2):
        z, _ = spot.member(turn, 0)
        for s, d in clean(z):
            first.append(out.go(s, d, spot.at(spot.y, spot.x, z, spot.core)))

    def send_group(turn, flip):
        z, core = spot.member(turn, flip)
        for s, d in pieces(z, core):
            out.go(s, d, spot.at(spot.y, spot.x, z, core))

    local[0].wait()
    local[1].wait()
    for c in first:
        c.wait_recv()

    sibling = spot.at(spot.y, spot.x, spot.z, 1 - spot.core)
    last = []
    done = list(first)

    def block(dy, dx, half):
        return kv.at[spot.row(dy, dx), spot.core, pl.ds(half * 2, 2)]

    def offer(dy, dx, half, axis, steps):
        b = block(dy, dx, half)
        c = out.go(b, b, spot.along(axis, steps))
        return c

    def twin(dy, dx, half):
        b = block(dy, dx, half)
        last.append(out.go(b, b, sibling))

    def got(c):
        c.wait_recv()
        done.append(c)

    pair = {}
    for half, axis in ((0, "x"), (1, "y")):
        pair[half] = (offer(0, 0, half, axis, 1), offer(0, 0, half, axis, -1))
    late = {}
    for half, axis in ((0, "y"), (1, "x")):
        late[half, 0] = (offer(0, 0, half, axis, 1), offer(0, 0, half, axis, -1))
    for half in (0, 1):
        twin(0, 0, half)

    def spot_of(half, first_step, second_step):
        return (second_step, first_step) if half == 0 else (first_step, second_step)

    for turn, flip in ((1, 0), (3, 1), (2, 0), (3, 0), (1, 1), (2, 1), (0, 1)):
        send_group(turn, flip)
    hop = {}
    for half, axis in ((0, "x"), (1, "y")):
        got(pair[half][0])
        dy, dx = spot_of(half, -1, 0)
        hop[half] = offer(dy, dx, half, axis, 1)
        other = "y" if half == 0 else "x"
        late[half, -1] = (offer(dy, dx, half, other, 1), offer(dy, dx, half, other, -1))
        twin(dy, dx, half)
    for half in (0, 1):
        got(pair[half][1])
        dy, dx = spot_of(half, 1, 0)
        other = "y" if half == 0 else "x"
        late[half, 1] = (offer(dy, dx, half, other, 1), offer(dy, dx, half, other, -1))
        twin(dy, dx, half)
    far = {}

    def second(step):
        for half in (0, 1):
            other = "y" if half == 0 else "x"
            got(late[half, step][0])
            dy, dx = spot_of(half, step, -1)
            far[half, step] = offer(dy, dx, half, other, 1)
            twin(dy, dx, half)

    second(0)
    for half in (0, 1):
        got(hop[half])
        dy, dx = spot_of(half, 2, 0)
        other = "y" if half == 0 else "x"
        late[half, 2] = (offer(dy, dx, half, other, 1), offer(dy, dx, half, other, -1))
        twin(dy, dx, half)
    for step in (-1, 1, 2):
        second(step)
    for step in (0, -1, 1, 2):
        for half in (0, 1):
            got(late[half, step][1])
            dy, dx = spot_of(half, step, 1)
            twin(dy, dx, half)
    for step in (0, -1, 1, 2):
        for half in (0, 1):
            got(far[half, step])
            dy, dx = spot_of(half, step, 2)
            twin(dy, dx, half)
    for c in local[2:]:
        c.wait()
    for c in out.made:
        if not any(c is d for d in done):
            c.wait_recv()
    for c in out.made:
        c.wait_send()


SPREAD_COPIES = 6 + 42 + 2 * (3 + 12 + 16)


def spread(qn, qc, dn, dc, kn, vn, kc, vc):
    half = jnp.bfloat16
    hbm = pl.BlockSpec(memory_space=pl.ANY)
    return pl.pallas_call(
        spread_kernel,
        out_shape=(
            jax.ShapeDtypeStruct((8, 4, 64, 256), half),
            jax.ShapeDtypeStruct((8, 64, 256), half),
            jax.ShapeDtypeStruct((16, 2, 4, 64, 256), half),
        ),
        in_specs=[pl.BlockSpec(memory_space=pltpu.HBM)] * 8,
        out_specs=(hbm,) * 3,
        scratch_shapes=[
            pltpu.SemaphoreType.DMA((SPREAD_COPIES,)),
            pltpu.SemaphoreType.DMA((SPREAD_COPIES,)),
            pltpu.SemaphoreType.DMA((8,)),
        ],
        compiler_params=pltpu.CompilerParams(collective_id=0, has_side_effects=True, vmem_limit_bytes=4 * MIB),
        name="spread",
    )(qn, qc, dn, dc, kn, vn, kc, vc)


def gather_kernel(dq, dnkv, dkv, dqn, dqc, nin, zin, twins, parts, slots, stage, zout, send, recv, own):
    spot = Spot()
    greet(spot)
    out = Sender(send, recv)
    mine = spot.z * 2 + spot.core
    sibling = spot.at(spot.y, spot.x, spot.z, 1 - spot.core)
    cols = pl.ds(pl.multiple_of(((spot.z % 2) * 4 + (spot.z // 2) * 2 + spot.core) * 256, 256), 256)
    wide = jnp.float32

    twin = {}
    lanes = (2, -1, 1, 0)
    order = []
    for steps in ((2,), (-1, 1), (0,)):
        for lane in lanes:
            for pair in [(s, lane) for s in steps] + [(lane, s) for s in steps]:
                if pair not in order:
                    order.append(pair)

    for dy, dx in order:
        r = spot.row(-dy, -dx)
        twin[dy, dx] = out.go(dkv.at[r, 1 - spot.core], twins.at[r], sibling)

    def send_group(turn, flip):
        z, core = spot.member(turn, flip)
        to = z * 2 + core
        device = spot.at(spot.y, spot.x, z, core)
        return [
            out.go(dq.at[to, 0], dqn.at[:, cols], device),
            out.go(dq.at[to, 1], dqc.at[:, cols], device),
            out.go(dnkv.at[to], nin.at[mine], device),
        ]

    group = []
    for turn, flip in ((2, 0), (2, 1), (1, 0), (3, 0), (1, 1), (3, 1), (0, 1)):
        group += send_group(turn, flip)
    local = [
        pltpu.make_async_copy(dq.at[mine, 0], dqn.at[:, cols], own.at[0]),
        pltpu.make_async_copy(dq.at[mine, 1], dqc.at[:, cols], own.at[1]),
        pltpu.make_async_copy(dnkv.at[mine], nin.at[mine], own.at[2]),
    ]
    for c in local:
        c.start()

    ready = set()

    def part(dy, dx):
        r = spot.row(dy, dx)
        if (dy, dx) not in ready:
            ready.add((dy, dx))
            twin[dy, dx].wait_recv()
            parts[r] = (dkv[r, spot.core].astype(wide) + twins[r].astype(wide)).astype(jnp.bfloat16)
        return r

    def owner(half, lane, step):
        return (step, lane) if half == 0 else (lane, step)

    first_axis = ("y", "x")
    sent = {}
    for lane in lanes:
        for half in (0, 1):
            r = part(*owner(half, lane, 2))
            n = lanes.index(lane)
            sent[half, lane, 0] = out.go(parts.at[r, pl.ds(half * 2, 2)], slots.at[half, n, 0], spot.along(first_axis[half], -1))
    for lane in lanes:
        for half in (0, 1):
            n = lanes.index(lane)
            r = part(*owner(half, lane, -1))
            part(*owner(half, lane, 1))
            sent[half, lane, 0].wait_recv()
            stage[half, n] = (parts[r, half * 2:half * 2 + 2].astype(wide) + slots[half, n, 0].astype(wide)).astype(jnp.bfloat16)
            sent[half, lane, 1] = out.go(stage.at[half, n], slots.at[half, n, 1], spot.along(first_axis[half], -1))
            r = part(*owner(half, lane, 1))
            sent[half, lane, 2] = out.go(parts.at[r, pl.ds(half * 2, 2)], slots.at[half, n, 2], spot.along(first_axis[half], 1))

    def total(half, lane):
        n = lanes.index(lane)
        r = part(*owner(half, lane, 0))
        sent[half, lane, 1].wait_recv()
        sent[half, lane, 2].wait_recv()
        return parts[r, half * 2:half * 2 + 2].astype(wide) + slots[half, n, 1].astype(wide) + slots[half, n, 2].astype(wide)

    second_axis = ("x", "y")
    deep = {}
    for half in (0, 1):
        stage[half, 4] = total(half, 2).astype(jnp.bfloat16)
        deep[half, 0] = out.go(stage.at[half, 4], slots.at[half, 4, 0], spot.along(second_axis[half], -1))
    passed = {}
    for half in (0, 1):
        passed[half] = total(half, -1)
        deep[half, 0].wait_recv()
        stage[half, 5] = (passed[half] + slots[half, 4, 0].astype(wide)).astype(jnp.bfloat16)
        deep[half, 1] = out.go(stage.at[half, 5], slots.at[half, 4, 1], spot.along(second_axis[half], -1))
    for half in (0, 1):
        stage[half, 6] = total(half, 1).astype(jnp.bfloat16)
        deep[half, 2] = out.go(stage.at[half, 6], slots.at[half, 4, 2], spot.along(second_axis[half], 1))
    for half in (0, 1):
        mid = total(half, 0)
        deep[half, 1].wait_recv()
        deep[half, 2].wait_recv()
        zout[half * 2:half * 2 + 2] = (mid + slots[half, 4, 1].astype(wide) + slots[half, 4, 2].astype(wide)).astype(jnp.bfloat16)
    deep_z = []
    for turn in (2, 1, 3):
        z, _ = spot.member(turn, 0)
        deep_z.append(out.go(zout.at[z], zin.at[spot.z], spot.at(spot.y, spot.x, z, spot.core)))
    zin[spot.z] = zout[spot.z]

    for c in group + deep_z:
        c.wait_recv()
    for c in local:
        c.wait()
    for c in out.made:
        c.wait_send()


GATHER_COPIES = 16 + 21 + 24 + 6 + 3


def gather(dq, dnkv, dkv):
    half = jnp.bfloat16
    vmem = pl.BlockSpec(memory_space=pltpu.VMEM)
    hbm = pl.BlockSpec(memory_space=pl.ANY)
    return pl.pallas_call(
        gather_kernel,
        out_shape=(
            jax.ShapeDtypeStruct((64, 2048), half),
            jax.ShapeDtypeStruct((64, 2048), half),
            jax.ShapeDtypeStruct((8, 64, 256), half),
            jax.ShapeDtypeStruct((4, 64, 256), half),
        ),
        in_specs=[hbm, hbm, vmem],
        out_specs=(hbm, hbm, vmem, vmem),
        scratch_shapes=[
            pltpu.VMEM((16, 4, 64, 256), half),
            pltpu.VMEM((16, 4, 64, 256), half),
            pltpu.VMEM((2, 5, 3, 2, 64, 256), half),
            pltpu.VMEM((2, 7, 2, 64, 256), half),
            pltpu.VMEM((4, 64, 256), half),
            pltpu.SemaphoreType.DMA((GATHER_COPIES,)),
            pltpu.SemaphoreType.DMA((GATHER_COPIES,)),
            pltpu.SemaphoreType.DMA((3,)),
        ],
        compiler_params=pltpu.CompilerParams(collective_id=1, has_side_effects=True, vmem_limit_bytes=14 * MIB),
        name="gather",
    )(dq, dnkv, dkv)


def finish_kernel(dqn, dqc, nin, zin, dqn_out, dqc_out, dkn, dvn, dkc, dvc, sem):
    copies = [pltpu.make_async_copy(dqn, dqn_out, sem.at[0]), pltpu.make_async_copy(dqc, dqc_out, sem.at[1])]
    for c in copies:
        c.start()
    wide = jnp.float32
    for head in (0, 1):
        at = slice(head * 128, head * 128 + 128)
        noisy = sum(nin[z * 2 + core].astype(wide) for z in (head, head + 2) for core in (0, 1))
        dkn[:, at] = noisy[:, :128].astype(jnp.bfloat16)
        dvn[:, at] = noisy[:, 128:].astype(jnp.bfloat16)
        clean = zin[head].astype(wide) + zin[head + 2].astype(wide)
        dkc[:, at] = clean[:, :128].astype(jnp.bfloat16)
        dvc[:, at] = clean[:, 128:].astype(jnp.bfloat16)
    for c in copies:
        c.wait()


def finish(dqn, dqc, nin, zin):
    half = jnp.bfloat16
    vmem = pl.BlockSpec(memory_space=pltpu.VMEM)
    hbm = pl.BlockSpec(memory_space=pl.ANY)
    return pl.pallas_call(
        finish_kernel,
        out_shape=(jax.ShapeDtypeStruct((64, 2048), half),) * 2 + (jax.ShapeDtypeStruct((64, 256), half),) * 4,
        in_specs=[hbm, hbm, vmem, vmem],
        out_specs=(hbm, hbm, vmem, vmem, vmem, vmem),
        scratch_shapes=[pltpu.SemaphoreType.DMA((2,))],
        compiler_params=pltpu.CompilerParams(vmem_limit_bytes=4 * MIB),
        name="finish",
    )(dqn, dqc, nin, zin)


def local(qn, qc, kn, vn, kc, vc, dn, dc, block_ids, stretch_order):
    far = lambda *arrays: [pltpu.with_memory_space_constraint(a, pltpu.HBM) for a in arrays]
    q, nkv, kv = spread(*far(qn, qc, dn, dc, kn, vn, kc, vc))
    dq, dnkv, dkv = attention(*far(stretch_order, block_ids), q, nkv, kv.reshape(128, 64, 256), tile=(4096, 2048, 1024, 512))
    return finish(*gather(dq, dnkv, dkv.reshape(16, 2, 4, 64, 256)))


def solution(mesh):
    both = P(("seq", "head"), None)
    return jax.shard_map(
        local, mesh=mesh, in_specs=(both,) * 8 + (P(), P()), out_specs=(both,) * 6, check_vma=False
    )
```

```python
import functools, math
import jax
import jax.numpy as jnp
from jax import lax
from jax.experimental import pallas as pl
from jax.experimental.pallas import tpu as pltpu
from jax.sharding import PartitionSpec as P

NEG = -1e30
MIB = 1 << 20


def attention_kernel(sizes, order_hbm, ids_hbm, q, nkv, kv, dq, dnkv, dkv, rows_kv, cols_k, acc, ebuf, pbuf, tops, qtot, turned, diag, order, ids, sem):
    facts = [pltpu.make_async_copy(order_hbm, order, sem.at[0]), pltpu.make_async_copy(ids_hbm, ids, sem.at[1])]
    for c in facts:
        c.start()
    yx = lax.axis_index("seq") // 4
    stretches, chunk, _ = kv.shape
    tokens = stretches * chunk
    scale = 1.0 / math.sqrt(128)
    to_exp2 = scale * math.log2(math.e)
    wide = jnp.float32
    half = jnp.bfloat16
    unit = sizes[-1]

    def each_chunk(body):
        def some(row, _):
            for j in range(8):
                at = (j // 2 % 2) * 4 + (j // 4) * 2 + j % 2
                body(row * 8 + at, order[row * 8 + j])
            return 0

        lax.fori_loop(0, stretches // 8, some, 0)

    def chunk_rows(p):
        return pl.ds(pl.multiple_of(p * chunk, chunk), chunk)

    for c in facts:
        c.wait()

    def bring(at, p):
        rows_kv[chunk_rows(p), :] = kv[at]

    each_chunk(bring)

    def turn(t, _):
        acc[pl.ds(pl.multiple_of(t * 1024, 1024), 1024), :] = jnp.zeros((1024, 256), wide)
        for i in range(1024 // unit):
            rows = pl.ds(pl.multiple_of(t * 1024 + i * unit, unit), unit)
            cols_k[t * (1024 // unit) + i] = rows_kv[rows, :128].T
        return 0

    lax.fori_loop(0, tokens // 1024, turn, 0)

    def fold(values, op):
        pieces = values.reshape(values.shape[0] // 16, 2, 8, values.shape[1])
        return op(op(pieces, axis=0), axis=0)

    def dot(a, b):
        return jnp.dot(a, b, preferred_element_type=wide)

    def stack(g, a, b):
        return jnp.concatenate([q[g, a, :, :128], q[g, a, :, 128:], q[g, b, :, :128], q[g, b, :, 128:]], axis=0)

    def position(g):
        return order[yx * 8 + (g // 4) * 4 + (g % 2) * 2 + (g // 2) % 2]

    key_at = lax.broadcasted_iota(jnp.int32, (128, 256), 0)
    row_at = lax.broadcasted_iota(jnp.int32, (128, 256), 1)
    clean_row = jnp.where(row_at >= 128, 1, 0)

    def prepare(g, _):
        p = position(g)
        limit = p * chunk
        first = ids[limit]
        split = jnp.int32(0)
        for bit in (64, 32, 16, 8, 4, 2, 1):
            near = jnp.minimum(split + bit, chunk)
            hit = jnp.logical_and(split + bit <= chunk, ids[limit + near - 1] == first)
            split = jnp.where(hit, split + bit, split)
        q_t = stack(g, 0, 1).T
        d_t = stack(g, 2, 3).T
        turned[g, 0] = q_t
        turned[g, 1] = d_t
        diag_kv = jnp.concatenate([rows_kv[chunk_rows(p), :], nkv[g]], axis=0)
        key_run = jnp.where(key_at % chunk >= split, 1, 0)
        row_run = jnp.where(row_at % chunk >= split, 1, 0)
        gap = jnp.where(key_at < chunk, row_run + clean_row - key_run, jnp.where(key_run == row_run, 1, 0) - clean_row)
        diag[g, 0] = jnp.where(gap > 0, dot(diag_kv[:, :128], q_t) * to_exp2, NEG)
        diag[g, 1] = dot(diag_kv[:, 128:], d_t)
        return 0

    lax.fori_loop(0, q.shape[0], prepare, 0, unroll=4)

    def one(g, _):
        p = position(g)
        limit = p * chunk
        units = (limit + unit - 1) // unit

        def walk(body, state):
            start = jnp.int32(0)
            left = units
            for size in sizes:
                many = size // unit
                count = left // many
                state = lax.fori_loop(0, count, lambda t, s: body(pl.multiple_of(start + t * size, unit), size, s), state)
                start = start + count * size
                left = left - count * many
            return state

        def ahead(s, dp, state, keep):
            top, total, dots = state
            new = jnp.maximum(top, fold(s, jnp.max))
            fade = jnp.exp2(top - new)
            e = jnp.exp2(s.reshape(s.shape[0] // 8, 8, 256) - new[None]).reshape(s.shape)
            keep(e, dp, new)
            return new, total * fade + fold(e, jnp.sum), dots * fade + fold(e * dp, jnp.sum)

        def keep_diag(e, dp, top):
            diag[g, 0] = e
            tops[tokens // 256] = top

        def walk_ahead(at, size, state):
            for part in range(size // 256):
                rows = pl.ds(at + part * 256, 256)
                s = dot(rows_kv[rows, :128], turned[g, 0])
                dp = dot(rows_kv[rows, 128:], turned[g, 1])
                s = jnp.where(lax.broadcasted_iota(jnp.int32, (256, 256), 0) < limit - at - part * 256, s, NEG) * to_exp2

                def keep(e, dp, top):
                    ebuf[rows, :] = e
                    pbuf[rows, :] = dp
                    for i in range(256 // 256):
                        tops[at // 256 + part * (256 // 256) + i] = top

                state = ahead(s, dp, state, keep)
            return state

        none = jnp.zeros((8, 256), wide)
        state = ahead(diag[g, 0], diag[g, 1], (none + NEG, none, none), keep_diag)
        last, total, dots = walk(walk_ahead, state)
        top = jnp.max(last, axis=0, keepdims=True)
        fade = jnp.exp2(last - top)
        total, dots = total * fade, dots * fade
        over = 1.0 / jnp.sum(total, axis=0, keepdims=True)
        mean = jnp.sum(dots, axis=0, keepdims=True) * over
        q_rows = stack(g, 0, 1)
        d_rows = stack(g, 2, 3)

        def grads(e, dp, keys_t, piece_top):
            factor = jnp.exp2(piece_top - top) * over
            p = (e.reshape(e.shape[0] // 8, 8, 256) * factor[None]).reshape(e.shape)
            ds = (p * (dp - mean)).astype(half)
            return dot(keys_t, ds), dot(ds, q_rows), dot(p.astype(half), d_rows)

        diag_k = jnp.concatenate([rows_kv[chunk_rows(p), :128], nkv[g, :, :128]], axis=0)
        gq, gk, gv = grads(diag[g, 0], diag[g, 1], diag_k.T, tops[tokens // 256])
        qtot[g] = gq
        acc[chunk_rows(p), :128] += gk[:chunk]
        acc[chunk_rows(p), 128:] += gv[:chunk]
        dnkv[g, :, :128] = (gk[chunk:] * scale).astype(half)
        dnkv[g, :, 128:] = gv[chunk:].astype(half)

        def back(at, size, _):
            gqs = 0.0
            for part in range(size // 256):
                rows = pl.ds(at + part * 256, 256)
                keys_t = cols_k[at // unit + part * 256 // unit][:, part * 256 % unit:part * 256 % unit + 256]
                gq, gk, gv = grads(ebuf[rows, :], pbuf[rows, :], keys_t, tops[at // 256 + part])
                gqs = gqs + gq
                acc[rows, :128] += gk
                acc[rows, 128:] += gv
            qtot[g] += gqs
            return 0

        walk(back, 0)
        return 0

    lax.fori_loop(0, q.shape[0], one, 0)

    def finish_q(g, _):
        out = (qtot[g] * scale).T.astype(half)
        for i in range(4):
            dq[g, i // 2, :, (i % 2) * 128:(i % 2) * 128 + 128] = out[i * 64:i * 64 + 64]
        return 0

    lax.fori_loop(0, q.shape[0], finish_q, 0, unroll=4)

    def give(at, p):
        dkv[at, :, :128] = (acc[chunk_rows(p), :128] * scale).astype(half)
        dkv[at, :, 128:] = acc[chunk_rows(p), 128:].astype(half)

    each_chunk(give)


def attention(order, ids, q, nkv, kv, tile=(2048, 1024)):
    tokens = kv.shape[0] * kv.shape[1]
    vmem = pl.BlockSpec(memory_space=pltpu.VMEM)
    hbm = pl.BlockSpec(memory_space=pltpu.HBM)
    half = jnp.bfloat16
    wide = jnp.float32
    return pl.pallas_call(
        functools.partial(attention_kernel, tile),
        out_shape=(
            jax.ShapeDtypeStruct((8, 2, 64, 256), half),
            jax.ShapeDtypeStruct((8, 64, 256), half),
            jax.ShapeDtypeStruct(kv.shape, half),
        ),
        in_specs=[hbm, hbm, vmem, vmem, vmem],
        out_specs=(vmem, vmem, vmem),
        scratch_shapes=[
            pltpu.VMEM((tokens, 256), half),
            pltpu.VMEM((tokens // tile[-1], 128, tile[-1]), half),
            pltpu.VMEM((tokens, 256), wide),
            pltpu.VMEM((tokens, 256), wide),
            pltpu.VMEM((tokens, 256), wide),
            pltpu.VMEM((tokens // 256 + 1, 8, 256), wide),
            pltpu.VMEM((8, 128, 256), wide),
            pltpu.VMEM((8, 2, 128, 256), half),
            pltpu.VMEM((8, 2, 128, 256), wide),
            pltpu.SMEM(order.shape, jnp.int32),
            pltpu.SMEM(ids.shape, jnp.int32),
            pltpu.SemaphoreType.DMA((2,)),
        ],
        compiler_params=pltpu.CompilerParams(vmem_limit_bytes=42 * MIB),
        name="attention",
    )(order, ids, q, nkv, kv)
MESH = pl.DeviceIdType.MESH


class Spot:
    def __init__(self):
        seq, head = lax.axis_index("seq"), lax.axis_index("head")
        self.y, self.x, self.core = seq // 16, (seq // 4) % 4, seq % 2
        self.z = ((seq // 2) % 2) * 2 + head
        self.sign = 1 - 2 * self.core

    def at(self, y, x, z, core):
        return (((y * 4 + x) * 2 + z // 2) * 2 + core, z % 2)

    def member(self, turn, flip):
        z = (self.z + turn) % 4
        core = (self.core + flip) % 2
        return z, core

    def along(self, axis, steps):
        y = (self.y + steps * self.sign + 4) % 4 if axis == "y" else self.y
        x = (self.x + steps * self.sign + 4) % 4 if axis == "x" else self.x
        return self.at(y, x, self.z, self.core)

    def row(self, dy, dx):
        return ((self.y + dy * self.sign + 4) % 4) * 4 + (self.x + dx * self.sign + 4) % 4


def greet(spot):
    barrier = pltpu.get_barrier_semaphore()
    others = [spot.member(t, f) for t in range(4) for f in range(2) if t or f]
    ids = [spot.at(spot.y, spot.x, z, c) for z, c in others]
    ids += [spot.along(a, s) for a in ("y", "x") for s in (1, -1, 2)]
    for d in ids:
        pl.semaphore_signal(barrier, inc=1, device_id=d, device_id_type=MESH)
    pl.semaphore_wait(barrier, len(ids))


class Sender:
    def __init__(self, send, recv):
        self.send, self.recv, self.made = send, recv, []

    def go(self, src, dst, device):
        n = len(self.made)
        copy = pltpu.make_async_remote_copy(
            src_ref=src, dst_ref=dst, send_sem=self.send.at[n], recv_sem=self.recv.at[n],
            device_id=device, device_id_type=MESH,
        )
        copy.start()
        self.made.append(copy)
        return copy


def spread_kernel(qn, qc, dn, dc, kn, vn, kc, vc, q, nkv, kv, send, recv, own):
    spot = Spot()
    greet(spot)
    out = Sender(send, recv)
    mine = spot.z * 2 + spot.core
    here = spot.row(0, 0)

    def pieces(z, core):
        head = pl.ds(pl.multiple_of((z % 2) * 128, 128), 128)
        cols = pl.ds(pl.multiple_of(((z % 2) * 4 + (z // 2) * 2 + core) * 256, 256), 256)
        found = [(a.at[:, cols], q.at[mine, i]) for i, a in enumerate((qn, qc, dn, dc))]
        found += [(kn.at[:, head], nkv.at[mine, :, :128]), (vn.at[:, head], nkv.at[mine, :, 128:])]
        return found

    def clean(z):
        head = pl.ds(pl.multiple_of((z % 2) * 128, 128), 128)
        slot = kv.at[here, spot.core, spot.z]
        return [(kc.at[:, head], slot.at[:, :128]), (vc.at[:, head], slot.at[:, 128:])]

    local = [pltpu.make_async_copy(s, d, own.at[i]) for i, (s, d) in enumerate(clean(spot.z) + pieces(spot.z, spot.core))]
    for c in local:
        c.start()
    first = []
    for turn in (1, 3, 2):
        z, _ = spot.member(turn, 0)
        for s, d in clean(z):
            first.append(out.go(s, d, spot.at(spot.y, spot.x, z, spot.core)))

    def send_group(turn, flip):
        z, core = spot.member(turn, flip)
        for s, d in pieces(z, core):
            out.go(s, d, spot.at(spot.y, spot.x, z, core))

    local[0].wait()
    local[1].wait()
    for c in first:
        c.wait_recv()

    sibling = spot.at(spot.y, spot.x, spot.z, 1 - spot.core)
    last = []
    done = list(first)

    def block(dy, dx, half):
        return kv.at[spot.row(dy, dx), spot.core, pl.ds(half * 2, 2)]

    def offer(dy, dx, half, axis, steps):
        b = block(dy, dx, half)
        c = out.go(b, b, spot.along(axis, steps))
        return c

    def twin(dy, dx, half):
        b = block(dy, dx, half)
        last.append(out.go(b, b, sibling))

    def got(c):
        c.wait_recv()
        done.append(c)

    pair = {}
    for half, axis in ((0, "x"), (1, "y")):
        pair[half] = (offer(0, 0, half, axis, 1), offer(0, 0, half, axis, -1), offer(0, 0, half, axis, 2))
    late = {}
    for half, axis in ((0, "y"), (1, "x")):
        late[half, 0] = (offer(0, 0, half, axis, 1), offer(0, 0, half, axis, -1))
    for half in (0, 1):
        twin(0, 0, half)

    def spot_of(half, first_step, second_step):
        return (second_step, first_step) if half == 0 else (first_step, second_step)

    for turn, flip in ((1, 0), (3, 1), (2, 0), (3, 0), (1, 1), (2, 1), (0, 1)):
        send_group(turn, flip)
    for half in (0, 1):
        got(pair[half][0])
        dy, dx = spot_of(half, -1, 0)
        other = "y" if half == 0 else "x"
        late[half, -1] = (offer(dy, dx, half, other, 1), offer(dy, dx, half, other, -1))
        twin(dy, dx, half)
    for half in (0, 1):
        got(pair[half][1])
        dy, dx = spot_of(half, 1, 0)
        other = "y" if half == 0 else "x"
        late[half, 1] = (offer(dy, dx, half, other, 1), offer(dy, dx, half, other, -1))
        twin(dy, dx, half)
    far = {}

    def second(step):
        for half in (0, 1):
            other = "y" if half == 0 else "x"
            got(late[half, step][0])
            dy, dx = spot_of(half, step, -1)
            far[half, step] = offer(dy, dx, half, other, 1)
            twin(dy, dx, half)

    for half in (0, 1):
        got(pair[half][2])
        dy, dx = spot_of(half, 2, 0)
        other = "y" if half == 0 else "x"
        late[half, 2] = (offer(dy, dx, half, other, 1), offer(dy, dx, half, other, -1))
        twin(dy, dx, half)
    second(0)
    for step in (-1, 1, 2):
        second(step)
    for step in (0, -1, 1, 2):
        for half in (0, 1):
            got(late[half, step][1])
            dy, dx = spot_of(half, step, 1)
            twin(dy, dx, half)
    for step in (0, -1, 1, 2):
        for half in (0, 1):
            got(far[half, step])
            dy, dx = spot_of(half, step, 2)
            twin(dy, dx, half)
    for c in local[2:]:
        c.wait()
    for c in out.made:
        if not any(c is d for d in done):
            c.wait_recv()
    for c in out.made:
        c.wait_send()


SPREAD_COPIES = 6 + 42 + 2 * (3 + 12 + 16)


def spread(qn, qc, dn, dc, kn, vn, kc, vc):
    half = jnp.bfloat16
    hbm = pl.BlockSpec(memory_space=pl.ANY)
    return pl.pallas_call(
        spread_kernel,
        out_shape=(
            jax.ShapeDtypeStruct((8, 4, 64, 256), half),
            jax.ShapeDtypeStruct((8, 64, 256), half),
            jax.ShapeDtypeStruct((16, 2, 4, 64, 256), half),
        ),
        in_specs=[pl.BlockSpec(memory_space=pltpu.HBM)] * 8,
        out_specs=(hbm,) * 3,
        scratch_shapes=[
            pltpu.SemaphoreType.DMA((SPREAD_COPIES,)),
            pltpu.SemaphoreType.DMA((SPREAD_COPIES,)),
            pltpu.SemaphoreType.DMA((8,)),
        ],
        compiler_params=pltpu.CompilerParams(collective_id=0, has_side_effects=True, vmem_limit_bytes=4 * MIB),
        name="spread",
    )(qn, qc, dn, dc, kn, vn, kc, vc)


def gather_kernel(dq, dnkv, dkv, dqn, dqc, nin, zin, twins, parts, slots, stage, zout, send, recv, own):
    spot = Spot()
    greet(spot)
    out = Sender(send, recv)
    mine = spot.z * 2 + spot.core
    sibling = spot.at(spot.y, spot.x, spot.z, 1 - spot.core)
    cols = pl.ds(pl.multiple_of(((spot.z % 2) * 4 + (spot.z // 2) * 2 + spot.core) * 256, 256), 256)
    wide = jnp.float32

    twin = {}
    lanes = (2, -1, 1, 0)
    order = []
    for steps in ((2,), (-1, 1), (0,)):
        for lane in lanes:
            for pair in [(s, lane) for s in steps] + [(lane, s) for s in steps]:
                if pair not in order:
                    order.append(pair)

    for dy, dx in order:
        r = spot.row(-dy, -dx)
        twin[dy, dx] = out.go(dkv.at[r, 1 - spot.core], twins.at[r], sibling)

    def send_group(turn, flip):
        z, core = spot.member(turn, flip)
        to = z * 2 + core
        device = spot.at(spot.y, spot.x, z, core)
        return [
            out.go(dq.at[to, 0], dqn.at[:, cols], device),
            out.go(dq.at[to, 1], dqc.at[:, cols], device),
            out.go(dnkv.at[to], nin.at[mine], device),
        ]

    group = []
    for turn, flip in ((2, 0), (2, 1), (1, 0), (3, 0), (1, 1), (3, 1), (0, 1)):
        group += send_group(turn, flip)
    local = [
        pltpu.make_async_copy(dq.at[mine, 0], dqn.at[:, cols], own.at[0]),
        pltpu.make_async_copy(dq.at[mine, 1], dqc.at[:, cols], own.at[1]),
        pltpu.make_async_copy(dnkv.at[mine], nin.at[mine], own.at[2]),
    ]
    for c in local:
        c.start()

    ready = set()

    def part(dy, dx):
        r = spot.row(dy, dx)
        if (dy, dx) not in ready:
            ready.add((dy, dx))
            twin[dy, dx].wait_recv()
            parts[r] = (dkv[r, spot.core].astype(wide) + twins[r].astype(wide)).astype(jnp.bfloat16)
        return r

    def owner(half, lane, step):
        return (step, lane) if half == 0 else (lane, step)

    first_axis = ("y", "x")
    sent = {}
    for lane in lanes:
        for half in (0, 1):
            r = part(*owner(half, lane, 2))
            n = lanes.index(lane)
            sent[half, lane, 0] = out.go(parts.at[r, pl.ds(half * 2, 2)], slots.at[half, n, 0], spot.along(first_axis[half], -1))
    for lane in lanes:
        for half in (0, 1):
            n = lanes.index(lane)
            r = part(*owner(half, lane, -1))
            part(*owner(half, lane, 1))
            sent[half, lane, 0].wait_recv()
            stage[half, n] = (parts[r, half * 2:half * 2 + 2].astype(wide) + slots[half, n, 0].astype(wide)).astype(jnp.bfloat16)
            sent[half, lane, 1] = out.go(stage.at[half, n], slots.at[half, n, 1], spot.along(first_axis[half], -1))
            r = part(*owner(half, lane, 1))
            sent[half, lane, 2] = out.go(parts.at[r, pl.ds(half * 2, 2)], slots.at[half, n, 2], spot.along(first_axis[half], 1))

    def total(half, lane):
        n = lanes.index(lane)
        r = part(*owner(half, lane, 0))
        sent[half, lane, 1].wait_recv()
        sent[half, lane, 2].wait_recv()
        return parts[r, half * 2:half * 2 + 2].astype(wide) + slots[half, n, 1].astype(wide) + slots[half, n, 2].astype(wide)

    second_axis = ("x", "y")
    deep = {}
    for kind, lane in enumerate((2, -1, 1)):
        for half in (0, 1):
            stage[half, 4 + kind] = total(half, lane).astype(jnp.bfloat16)
            deep[half, kind] = out.go(stage.at[half, 4 + kind], slots.at[half, 4, kind], spot.along(second_axis[half], lane))
    for half in (0, 1):
        mid = total(half, 0)
        for kind in range(3):
            deep[half, kind].wait_recv()
            mid = mid + slots[half, 4, kind].astype(wide)
        zout[half * 2:half * 2 + 2] = mid.astype(jnp.bfloat16)
    deep_z = []
    for turn in (2, 1, 3):
        z, _ = spot.member(turn, 0)
        deep_z.append(out.go(zout.at[z], zin.at[spot.z], spot.at(spot.y, spot.x, z, spot.core)))
    zin[spot.z] = zout[spot.z]

    for c in group + deep_z:
        c.wait_recv()
    for c in local:
        c.wait()
    for c in out.made:
        c.wait_send()


GATHER_COPIES = 16 + 21 + 24 + 6 + 3


def gather(dq, dnkv, dkv):
    half = jnp.bfloat16
    vmem = pl.BlockSpec(memory_space=pltpu.VMEM)
    hbm = pl.BlockSpec(memory_space=pl.ANY)
    return pl.pallas_call(
        gather_kernel,
        out_shape=(
            jax.ShapeDtypeStruct((64, 2048), half),
            jax.ShapeDtypeStruct((64, 2048), half),
            jax.ShapeDtypeStruct((8, 64, 256), half),
            jax.ShapeDtypeStruct((4, 64, 256), half),
        ),
        in_specs=[hbm, hbm, vmem],
        out_specs=(hbm, hbm, vmem, vmem),
        scratch_shapes=[
            pltpu.VMEM((16, 4, 64, 256), half),
            pltpu.VMEM((16, 4, 64, 256), half),
            pltpu.VMEM((2, 5, 3, 2, 64, 256), half),
            pltpu.VMEM((2, 7, 2, 64, 256), half),
            pltpu.VMEM((4, 64, 256), half),
            pltpu.SemaphoreType.DMA((GATHER_COPIES,)),
            pltpu.SemaphoreType.DMA((GATHER_COPIES,)),
            pltpu.SemaphoreType.DMA((3,)),
        ],
        compiler_params=pltpu.CompilerParams(collective_id=1, has_side_effects=True, vmem_limit_bytes=14 * MIB),
        name="gather",
    )(dq, dnkv, dkv)


def finish_kernel(dqn, dqc, nin, zin, dqn_out, dqc_out, dkn, dvn, dkc, dvc, sem):
    copies = [pltpu.make_async_copy(dqn, dqn_out, sem.at[0]), pltpu.make_async_copy(dqc, dqc_out, sem.at[1])]
    for c in copies:
        c.start()
    wide = jnp.float32
    for head in (0, 1):
        at = slice(head * 128, head * 128 + 128)
        noisy = sum(nin[z * 2 + core].astype(wide) for z in (head, head + 2) for core in (0, 1))
        dkn[:, at] = noisy[:, :128].astype(jnp.bfloat16)
        dvn[:, at] = noisy[:, 128:].astype(jnp.bfloat16)
        clean = zin[head].astype(wide) + zin[head + 2].astype(wide)
        dkc[:, at] = clean[:, :128].astype(jnp.bfloat16)
        dvc[:, at] = clean[:, 128:].astype(jnp.bfloat16)
    for c in copies:
        c.wait()


def finish(dqn, dqc, nin, zin):
    half = jnp.bfloat16
    vmem = pl.BlockSpec(memory_space=pltpu.VMEM)
    hbm = pl.BlockSpec(memory_space=pl.ANY)
    return pl.pallas_call(
        finish_kernel,
        out_shape=(jax.ShapeDtypeStruct((64, 2048), half),) * 2 + (jax.ShapeDtypeStruct((64, 256), half),) * 4,
        in_specs=[hbm, hbm, vmem, vmem],
        out_specs=(hbm, hbm, vmem, vmem, vmem, vmem),
        scratch_shapes=[pltpu.SemaphoreType.DMA((2,))],
        compiler_params=pltpu.CompilerParams(vmem_limit_bytes=4 * MIB),
        name="finish",
    )(dqn, dqc, nin, zin)


def local(qn, qc, kn, vn, kc, vc, dn, dc, block_ids, stretch_order):
    far = lambda *arrays: [pltpu.with_memory_space_constraint(a, pltpu.HBM) for a in arrays]
    q, nkv, kv = spread(*far(qn, qc, dn, dc, kn, vn, kc, vc))
    dq, dnkv, dkv = attention(*far(stretch_order, block_ids), q, nkv, kv.reshape(128, 64, 256), tile=(4096, 2048, 1024, 512))
    return finish(*gather(dq, dnkv, dkv.reshape(16, 2, 4, 64, 256)))


def solution(mesh):
    both = P(("seq", "head"), None)
    return jax.shard_map(
        local, mesh=mesh, in_specs=(both,) * 8 + (P(), P()), out_specs=(both,) * 6, check_vma=False
    )
```

```python
import functools, math
import jax
import jax.numpy as jnp
from jax import lax
from jax.experimental import pallas as pl
from jax.experimental.pallas import tpu as pltpu
from jax.sharding import PartitionSpec as P

NEG = -1e30
MIB = 1 << 20


def attention_kernel(sizes, order_hbm, ids_hbm, q, nkv, kv, dq, dnkv, dkv, rows_kv, cols_k, acc, ebuf, pbuf, tops, diag_tops, facts_of, qtot, turned, diag, order, ids, sem):
    facts = [pltpu.make_async_copy(order_hbm, order, sem.at[0]), pltpu.make_async_copy(ids_hbm, ids, sem.at[1])]
    for c in facts:
        c.start()
    yx = lax.axis_index("seq") // 4
    stretches, chunk, _ = kv.shape
    tokens = stretches * chunk
    scale = 1.0 / math.sqrt(128)
    to_exp2 = scale * math.log2(math.e)
    wide = jnp.float32
    half = jnp.bfloat16
    unit = sizes[-1]

    def each_chunk(body):
        def some(row, _):
            for j in range(8):
                at = (j // 2 % 2) * 4 + (j // 4) * 2 + j % 2
                body(row * 8 + at, order[row * 8 + j])
            return 0

        lax.fori_loop(0, stretches // 8, some, 0)

    def chunk_rows(p):
        return pl.ds(pl.multiple_of(p * chunk, chunk), chunk)

    facts[0].wait()

    def bring(at, p):
        rows_kv[chunk_rows(p), :] = kv[at]

    each_chunk(bring)

    def turn(t, _):
        acc[pl.ds(pl.multiple_of(t * 1024, 1024), 1024), :] = jnp.zeros((1024, 256), wide)
        for i in range(1024 // unit):
            rows = pl.ds(pl.multiple_of(t * 1024 + i * unit, unit), unit)
            cols_k[t * (1024 // unit) + i] = rows_kv[rows, :128].T
        return 0

    lax.fori_loop(0, tokens // 1024, turn, 0)

    def fold(values, op):
        pieces = values.reshape(values.shape[0] // 16, 2, 8, values.shape[1])
        return op(op(pieces, axis=0), axis=0)

    def dot(a, b):
        return jnp.dot(a, b, preferred_element_type=wide)

    def stack(g, a, b):
        return jnp.concatenate([q[g, a, :, :128], q[g, a, :, 128:], q[g, b, :, :128], q[g, b, :, 128:]], axis=0)

    def position(g):
        return order[yx * 8 + (g // 4) * 4 + (g % 2) * 2 + (g // 2) % 2]

    key_at = lax.broadcasted_iota(jnp.int32, (128, 256), 0)
    row_at = lax.broadcasted_iota(jnp.int32, (128, 256), 1)
    clean_row = jnp.where(row_at >= 128, 1, 0)

    def prepare(g, _):
        p = position(g)
        limit = p * chunk
        first = ids[limit]
        split = jnp.int32(0)
        for bit in (64, 32, 16, 8, 4, 2, 1):
            near = jnp.minimum(split + bit, chunk)
            hit = jnp.logical_and(split + bit <= chunk, ids[limit + near - 1] == first)
            split = jnp.where(hit, split + bit, split)
        q_t = stack(g, 0, 1).T
        d_t = stack(g, 2, 3).T
        turned[g, 0] = q_t
        turned[g, 1] = d_t
        diag_kv = jnp.concatenate([rows_kv[chunk_rows(p), :], nkv[g]], axis=0)
        key_run = jnp.where(key_at % chunk >= split, 1, 0)
        row_run = jnp.where(row_at % chunk >= split, 1, 0)
        gap = jnp.where(key_at < chunk, row_run + clean_row - key_run, jnp.where(key_run == row_run, 1, 0) - clean_row)
        diag[g, 0] = jnp.where(gap > 0, dot(diag_kv[:, :128], q_t) * to_exp2, NEG)
        diag[g, 1] = dot(diag_kv[:, 128:], d_t)
        return 0

    facts[1].wait()
    lax.fori_loop(0, q.shape[0], prepare, 0, unroll=4)

    def grads(e, dp, keys_t, piece_top, known):
        top, over, mean, q_rows, d_rows = known
        factor = jnp.exp2(piece_top - top) * over
        p = (e.reshape(e.shape[0] // 8, 8, 256) * factor[None]).reshape(e.shape)
        ds = (p * (dp - mean)).astype(half)
        return dot(keys_t, ds), dot(ds, q_rows), dot(p.astype(half), d_rows)

    def one(g, _):
        p = position(g)
        limit = p * chunk
        units = (limit + unit - 1) // unit

        def walk(body, state):
            start = jnp.int32(0)
            left = units
            for size in sizes:
                many = size // unit
                count = left // many
                state = lax.fori_loop(0, count, lambda t, s: body(pl.multiple_of(start + t * size, unit), size, s), state)
                start = start + count * size
                left = left - count * many
            return state

        def ahead(s, dp, state, keep):
            top, total, dots = state
            new = jnp.maximum(top, fold(s, jnp.max))
            fade = jnp.exp2(top - new)
            e = jnp.exp2(s.reshape(s.shape[0] // 8, 8, 256) - new[None]).reshape(s.shape)
            keep(e, dp, new)
            return new, total * fade + fold(e, jnp.sum), dots * fade + fold(e * dp, jnp.sum)

        def keep_diag(e, dp, top):
            diag[g, 0] = e
            diag_tops[g] = top

        def walk_ahead(at, size, state):
            for part in range(size // 256):
                rows = pl.ds(at + part * 256, 256)
                s = dot(rows_kv[rows, :128], turned[g, 0])
                dp = dot(rows_kv[rows, 128:], turned[g, 1])
                s = jnp.where(lax.broadcasted_iota(jnp.int32, (256, 256), 0) < limit - at - part * 256, s, NEG) * to_exp2

                def keep(e, dp, top):
                    ebuf[rows, :] = e
                    pbuf[rows, :] = dp
                    for i in range(256 // 256):
                        tops[at // 256 + part * (256 // 256) + i] = top

                state = ahead(s, dp, state, keep)
            return state

        none = jnp.zeros((8, 256), wide)
        state = ahead(diag[g, 0], diag[g, 1], (none + NEG, none, none), keep_diag)
        last, total, dots = walk(walk_ahead, state)
        top = jnp.max(last, axis=0, keepdims=True)
        fade = jnp.exp2(last - top)
        total, dots = total * fade, dots * fade
        over = 1.0 / jnp.sum(total, axis=0, keepdims=True)
        mean = jnp.sum(dots, axis=0, keepdims=True) * over
        q_rows, d_rows = stack(g, 0, 1), stack(g, 2, 3)

        qtot[g] = jnp.zeros((128, 256), wide)
        facts_of[g, 0:1], facts_of[g, 1:2], facts_of[g, 2:3] = top, over, mean

        def back(at, size, _):
            gqs = 0.0
            for part in range(size // 256):
                rows = pl.ds(at + part * 256, 256)
                keys_t = cols_k[at // unit + part * 256 // unit][:, part * 256 % unit:part * 256 % unit + 256]
                gq, gk, gv = grads(ebuf[rows, :], pbuf[rows, :], keys_t, tops[at // 256 + part], (top, over, mean, q_rows, d_rows))
                gqs = gqs + gq
                acc[rows, :128] += gk
                acc[rows, 128:] += gv
            qtot[g] += gqs
            return 0

        walk(back, 0)
        return 0

    lax.fori_loop(0, q.shape[0], one, 0)

    def finish_q(g, _):
        p = position(g)
        diag_k = jnp.concatenate([rows_kv[chunk_rows(p), :128], nkv[g, :, :128]], axis=0)
        known = (facts_of[g, 0:1], facts_of[g, 1:2], facts_of[g, 2:3], stack(g, 0, 1), stack(g, 2, 3))
        gq, gk, gv = grads(diag[g, 0], diag[g, 1], diag_k.T, diag_tops[g], known)
        acc[chunk_rows(p), :128] += gk[:chunk]
        acc[chunk_rows(p), 128:] += gv[:chunk]
        dnkv[g, :, :128] = (gk[chunk:] * scale).astype(half)
        dnkv[g, :, 128:] = gv[chunk:].astype(half)
        out = ((qtot[g] + gq) * scale).T.astype(half)
        for i in range(4):
            dq[g, i // 2, :, (i % 2) * 128:(i % 2) * 128 + 128] = out[i * 64:i * 64 + 64]
        return 0

    lax.fori_loop(0, q.shape[0], finish_q, 0, unroll=4)

    def give(at, p):
        dkv[at, :, :128] = (acc[chunk_rows(p), :128] * scale).astype(half)
        dkv[at, :, 128:] = acc[chunk_rows(p), 128:].astype(half)

    each_chunk(give)


def attention(order, ids, q, nkv, kv, tile=(2048, 1024)):
    tokens = kv.shape[0] * kv.shape[1]
    vmem = pl.BlockSpec(memory_space=pltpu.VMEM)
    hbm = pl.BlockSpec(memory_space=pltpu.HBM)
    half = jnp.bfloat16
    wide = jnp.float32
    return pl.pallas_call(
        functools.partial(attention_kernel, tile),
        out_shape=(
            jax.ShapeDtypeStruct((8, 2, 64, 256), half),
            jax.ShapeDtypeStruct((8, 64, 256), half),
            jax.ShapeDtypeStruct(kv.shape, half),
        ),
        in_specs=[hbm, hbm, vmem, vmem, vmem],
        out_specs=(vmem, vmem, vmem),
        scratch_shapes=[
            pltpu.VMEM((tokens, 256), half),
            pltpu.VMEM((tokens // tile[-1], 128, tile[-1]), half),
            pltpu.VMEM((tokens, 256), wide),
            pltpu.VMEM((tokens, 256), wide),
            pltpu.VMEM((tokens, 256), wide),
            pltpu.VMEM((tokens // 256, 8, 256), wide),
            pltpu.VMEM((8, 8, 256), wide),
            pltpu.VMEM((8, 8, 256), wide),
            pltpu.VMEM((8, 128, 256), wide),
            pltpu.VMEM((8, 2, 128, 256), half),
            pltpu.VMEM((8, 2, 128, 256), wide),
            pltpu.SMEM(order.shape, jnp.int32),
            pltpu.SMEM(ids.shape, jnp.int32),
            pltpu.SemaphoreType.DMA((2,)),
        ],
        compiler_params=pltpu.CompilerParams(vmem_limit_bytes=42 * MIB),
        name="attention",
    )(order, ids, q, nkv, kv)
MESH = pl.DeviceIdType.MESH


class Spot:
    def __init__(self):
        seq, head = lax.axis_index("seq"), lax.axis_index("head")
        self.y, self.x, self.core = seq // 16, (seq // 4) % 4, seq % 2
        self.z = ((seq // 2) % 2) * 2 + head
        self.sign = 1 - 2 * self.core

    def at(self, y, x, z, core):
        return (((y * 4 + x) * 2 + z // 2) * 2 + core, z % 2)

    def member(self, turn, flip):
        z = (self.z + turn) % 4
        core = (self.core + flip) % 2
        return z, core

    def along(self, axis, steps):
        y = (self.y + steps * self.sign + 4) % 4 if axis == "y" else self.y
        x = (self.x + steps * self.sign + 4) % 4 if axis == "x" else self.x
        return self.at(y, x, self.z, self.core)

    def row(self, dy, dx):
        return ((self.y + dy * self.sign + 4) % 4) * 4 + (self.x + dx * self.sign + 4) % 4


def greet(spot):
    barrier = pltpu.get_barrier_semaphore()
    others = [spot.member(t, f) for t in range(4) for f in range(2) if t or f]
    ids = [spot.at(spot.y, spot.x, z, c) for z, c in others]
    ids += [spot.along(a, s) for a in ("y", "x") for s in (1, -1, 2)]
    for d in ids:
        pl.semaphore_signal(barrier, inc=1, device_id=d, device_id_type=MESH)
    pl.semaphore_wait(barrier, len(ids))


class Sender:
    def __init__(self, send, recv):
        self.send, self.recv, self.made = send, recv, []

    def go(self, src, dst, device):
        n = len(self.made)
        copy = pltpu.make_async_remote_copy(
            src_ref=src, dst_ref=dst, send_sem=self.send.at[n], recv_sem=self.recv.at[n],
            device_id=device, device_id_type=MESH,
        )
        copy.start()
        self.made.append(copy)
        return copy


def spread_kernel(qn, qc, dn, dc, kn, vn, kc, vc, q, nkv, kv, send, recv, own):
    spot = Spot()
    greet(spot)
    out = Sender(send, recv)
    mine = spot.z * 2 + spot.core
    here = spot.row(0, 0)

    def pieces(z, core):
        head = pl.ds(pl.multiple_of((z % 2) * 128, 128), 128)
        cols = pl.ds(pl.multiple_of(((z % 2) * 4 + (z // 2) * 2 + core) * 256, 256), 256)
        found = [(a.at[:, cols], q.at[mine, i]) for i, a in enumerate((qn, qc, dn, dc))]
        found += [(kn.at[:, head], nkv.at[mine, :, :128]), (vn.at[:, head], nkv.at[mine, :, 128:])]
        return found

    def clean(z):
        head = pl.ds(pl.multiple_of((z % 2) * 128, 128), 128)
        slot = kv.at[here, spot.core, spot.z]
        return [(kc.at[:, head], slot.at[:, :128]), (vc.at[:, head], slot.at[:, 128:])]

    local = [pltpu.make_async_copy(s, d, own.at[i]) for i, (s, d) in enumerate(clean(spot.z) + pieces(spot.z, spot.core))]
    for c in local:
        c.start()
    first = []
    for turn in (1, 3, 2):
        z, _ = spot.member(turn, 0)
        for s, d in clean(z):
            first.append(out.go(s, d, spot.at(spot.y, spot.x, z, spot.core)))

    def send_group(turn, flip):
        z, core = spot.member(turn, flip)
        for s, d in pieces(z, core):
            out.go(s, d, spot.at(spot.y, spot.x, z, core))

    local[0].wait()
    local[1].wait()
    for c in first:
        c.wait_recv()

    sibling = spot.at(spot.y, spot.x, spot.z, 1 - spot.core)
    last = []
    done = list(first)

    def block(dy, dx, half):
        return kv.at[spot.row(dy, dx), spot.core, pl.ds(half * 2, 2)]

    def offer(dy, dx, half, axis, steps):
        b = block(dy, dx, half)
        c = out.go(b, b, spot.along(axis, steps))
        return c

    def twin(dy, dx, half):
        b = block(dy, dx, half)
        last.append(out.go(b, b, sibling))

    def got(c):
        c.wait_recv()
        done.append(c)

    pair = {}
    for half, axis in ((0, "x"), (1, "y")):
        pair[half] = (offer(0, 0, half, axis, 1), offer(0, 0, half, axis, -1), offer(0, 0, half, axis, 2))
    late = {}
    for half, axis in ((0, "y"), (1, "x")):
        late[half, 0] = (offer(0, 0, half, axis, 1), offer(0, 0, half, axis, -1))
    for half in (0, 1):
        twin(0, 0, half)

    def spot_of(half, first_step, second_step):
        return (second_step, first_step) if half == 0 else (first_step, second_step)

    for turn, flip in ((1, 0), (3, 1), (2, 0), (3, 0), (1, 1), (2, 1), (0, 1)):
        send_group(turn, flip)
    for half in (0, 1):
        got(pair[half][0])
        dy, dx = spot_of(half, -1, 0)
        other = "y" if half == 0 else "x"
        late[half, -1] = (offer(dy, dx, half, other, 1), offer(dy, dx, half, other, -1))
        twin(dy, dx, half)
    for half in (0, 1):
        got(pair[half][1])
        dy, dx = spot_of(half, 1, 0)
        other = "y" if half == 0 else "x"
        late[half, 1] = (offer(dy, dx, half, other, 1), offer(dy, dx, half, other, -1))
        twin(dy, dx, half)
    far = {}

    def second(step):
        for half in (0, 1):
            other = "y" if half == 0 else "x"
            got(late[half, step][0])
            dy, dx = spot_of(half, step, -1)
            far[half, step] = offer(dy, dx, half, other, 1)
            twin(dy, dx, half)

    for half in (0, 1):
        got(pair[half][2])
        dy, dx = spot_of(half, 2, 0)
        other = "y" if half == 0 else "x"
        late[half, 2] = (offer(dy, dx, half, other, 1), offer(dy, dx, half, other, -1))
        twin(dy, dx, half)
    second(0)
    for step in (-1, 1, 2):
        second(step)
    for step in (0, -1, 1, 2):
        for half in (0, 1):
            got(late[half, step][1])
            dy, dx = spot_of(half, step, 1)
            twin(dy, dx, half)
    for step in (0, -1, 1, 2):
        for half in (0, 1):
            got(far[half, step])
            dy, dx = spot_of(half, step, 2)
            twin(dy, dx, half)
    for c in local[2:]:
        c.wait()
    for c in out.made:
        if not any(c is d for d in done):
            c.wait_recv()
    for c in out.made:
        c.wait_send()


SPREAD_COPIES = 6 + 42 + 2 * (3 + 12 + 16)


def spread(qn, qc, dn, dc, kn, vn, kc, vc):
    half = jnp.bfloat16
    hbm = pl.BlockSpec(memory_space=pl.ANY)
    return pl.pallas_call(
        spread_kernel,
        out_shape=(
            jax.ShapeDtypeStruct((8, 4, 64, 256), half),
            jax.ShapeDtypeStruct((8, 64, 256), half),
            jax.ShapeDtypeStruct((16, 2, 4, 64, 256), half),
        ),
        in_specs=[pl.BlockSpec(memory_space=pltpu.HBM)] * 8,
        out_specs=(hbm,) * 3,
        scratch_shapes=[
            pltpu.SemaphoreType.DMA((SPREAD_COPIES,)),
            pltpu.SemaphoreType.DMA((SPREAD_COPIES,)),
            pltpu.SemaphoreType.DMA((8,)),
        ],
        compiler_params=pltpu.CompilerParams(collective_id=0, has_side_effects=True, vmem_limit_bytes=4 * MIB),
        name="spread",
    )(qn, qc, dn, dc, kn, vn, kc, vc)


def gather_kernel(dq, dnkv, dkv, dqn, dqc, nin, zin, twins, parts, slots, stage, zout, send, recv, own):
    spot = Spot()
    greet(spot)
    out = Sender(send, recv)
    mine = spot.z * 2 + spot.core
    sibling = spot.at(spot.y, spot.x, spot.z, 1 - spot.core)
    cols = pl.ds(pl.multiple_of(((spot.z % 2) * 4 + (spot.z // 2) * 2 + spot.core) * 256, 256), 256)
    wide = jnp.float32

    twin = {}
    lanes = (2, -1, 1, 0)
    order = []
    for steps in ((2,), (-1, 1), (0,)):
        for lane in lanes:
            for pair in [(s, lane) for s in steps] + [(lane, s) for s in steps]:
                if pair not in order:
                    order.append(pair)

    for dy, dx in order:
        r = spot.row(-dy, -dx)
        twin[dy, dx] = out.go(dkv.at[r, 1 - spot.core], twins.at[r], sibling)

    def send_group(turn, flip):
        z, core = spot.member(turn, flip)
        to = z * 2 + core
        device = spot.at(spot.y, spot.x, z, core)
        return [
            out.go(dq.at[to, 0], dqn.at[:, cols], device),
            out.go(dq.at[to, 1], dqc.at[:, cols], device),
            out.go(dnkv.at[to], nin.at[mine], device),
        ]

    group = []
    for turn, flip in ((2, 0), (2, 1), (1, 0), (3, 0), (1, 1), (3, 1), (0, 1)):
        group += send_group(turn, flip)
    local = [
        pltpu.make_async_copy(dq.at[mine, 0], dqn.at[:, cols], own.at[0]),
        pltpu.make_async_copy(dq.at[mine, 1], dqc.at[:, cols], own.at[1]),
        pltpu.make_async_copy(dnkv.at[mine], nin.at[mine], own.at[2]),
    ]
    for c in local:
        c.start()

    ready = set()

    def part(dy, dx):
        r = spot.row(dy, dx)
        if (dy, dx) not in ready:
            ready.add((dy, dx))
            twin[dy, dx].wait_recv()
            parts[r] = (dkv[r, spot.core].astype(wide) + twins[r].astype(wide)).astype(jnp.bfloat16)
        return r

    def owner(half, lane, step):
        return (step, lane) if half == 0 else (lane, step)

    first_axis = ("y", "x")
    sent = {}
    for lane in lanes:
        for half in (0, 1):
            r = part(*owner(half, lane, 2))
            n = lanes.index(lane)
            sent[half, lane, 0] = out.go(parts.at[r, pl.ds(half * 2, 2)], slots.at[half, n, 0], spot.along(first_axis[half], -1))
    for lane in lanes:
        for half in (0, 1):
            n = lanes.index(lane)
            r = part(*owner(half, lane, -1))
            part(*owner(half, lane, 1))
            sent[half, lane, 0].wait_recv()
            stage[half, n] = (parts[r, half * 2:half * 2 + 2].astype(wide) + slots[half, n, 0].astype(wide)).astype(jnp.bfloat16)
            sent[half, lane, 1] = out.go(stage.at[half, n], slots.at[half, n, 1], spot.along(first_axis[half], -1))
            r = part(*owner(half, lane, 1))
            sent[half, lane, 2] = out.go(parts.at[r, pl.ds(half * 2, 2)], slots.at[half, n, 2], spot.along(first_axis[half], 1))

    def total(half, lane):
        n = lanes.index(lane)
        r = part(*owner(half, lane, 0))
        sent[half, lane, 1].wait_recv()
        sent[half, lane, 2].wait_recv()
        return parts[r, half * 2:half * 2 + 2].astype(wide) + slots[half, n, 1].astype(wide) + slots[half, n, 2].astype(wide)

    second_axis = ("x", "y")
    deep = {}
    for kind, lane in enumerate((2, -1, 1)):
        for half in (0, 1):
            stage[half, 4 + kind] = total(half, lane).astype(jnp.bfloat16)
            deep[half, kind] = out.go(stage.at[half, 4 + kind], slots.at[half, 4, kind], spot.along(second_axis[half], lane))
    for half in (0, 1):
        mid = total(half, 0)
        for kind in range(3):
            deep[half, kind].wait_recv()
            mid = mid + slots[half, 4, kind].astype(wide)
        zout[half * 2:half * 2 + 2] = mid.astype(jnp.bfloat16)
    deep_z = []
    for turn in (2, 1, 3):
        z, _ = spot.member(turn, 0)
        deep_z.append(out.go(zout.at[z], zin.at[spot.z], spot.at(spot.y, spot.x, z, spot.core)))
    zin[spot.z] = zout[spot.z]

    for c in group + deep_z:
        c.wait_recv()
    for c in local:
        c.wait()
    for c in out.made:
        c.wait_send()


GATHER_COPIES = 16 + 21 + 24 + 6 + 3


def gather(dq, dnkv, dkv):
    half = jnp.bfloat16
    vmem = pl.BlockSpec(memory_space=pltpu.VMEM)
    hbm = pl.BlockSpec(memory_space=pl.ANY)
    return pl.pallas_call(
        gather_kernel,
        out_shape=(
            jax.ShapeDtypeStruct((64, 2048), half),
            jax.ShapeDtypeStruct((64, 2048), half),
            jax.ShapeDtypeStruct((8, 64, 256), half),
            jax.ShapeDtypeStruct((4, 64, 256), half),
        ),
        in_specs=[hbm, hbm, vmem],
        out_specs=(hbm, hbm, vmem, vmem),
        scratch_shapes=[
            pltpu.VMEM((16, 4, 64, 256), half),
            pltpu.VMEM((16, 4, 64, 256), half),
            pltpu.VMEM((2, 5, 3, 2, 64, 256), half),
            pltpu.VMEM((2, 7, 2, 64, 256), half),
            pltpu.VMEM((4, 64, 256), half),
            pltpu.SemaphoreType.DMA((GATHER_COPIES,)),
            pltpu.SemaphoreType.DMA((GATHER_COPIES,)),
            pltpu.SemaphoreType.DMA((3,)),
        ],
        compiler_params=pltpu.CompilerParams(collective_id=1, has_side_effects=True, vmem_limit_bytes=14 * MIB),
        name="gather",
    )(dq, dnkv, dkv)


def finish_kernel(dqn, dqc, nin, zin, dqn_out, dqc_out, dkn, dvn, dkc, dvc, sem):
    copies = [pltpu.make_async_copy(dqn, dqn_out, sem.at[0]), pltpu.make_async_copy(dqc, dqc_out, sem.at[1])]
    for c in copies:
        c.start()
    wide = jnp.float32
    for head in (0, 1):
        at = slice(head * 128, head * 128 + 128)
        noisy = sum(nin[z * 2 + core].astype(wide) for z in (head, head + 2) for core in (0, 1))
        dkn[:, at] = noisy[:, :128].astype(jnp.bfloat16)
        dvn[:, at] = noisy[:, 128:].astype(jnp.bfloat16)
        clean = zin[head].astype(wide) + zin[head + 2].astype(wide)
        dkc[:, at] = clean[:, :128].astype(jnp.bfloat16)
        dvc[:, at] = clean[:, 128:].astype(jnp.bfloat16)
    for c in copies:
        c.wait()


def finish(dqn, dqc, nin, zin):
    half = jnp.bfloat16
    vmem = pl.BlockSpec(memory_space=pltpu.VMEM)
    hbm = pl.BlockSpec(memory_space=pl.ANY)
    return pl.pallas_call(
        finish_kernel,
        out_shape=(jax.ShapeDtypeStruct((64, 2048), half),) * 2 + (jax.ShapeDtypeStruct((64, 256), half),) * 4,
        in_specs=[hbm, hbm, vmem, vmem],
        out_specs=(hbm, hbm, vmem, vmem, vmem, vmem),
        scratch_shapes=[pltpu.SemaphoreType.DMA((2,))],
        compiler_params=pltpu.CompilerParams(vmem_limit_bytes=4 * MIB),
        name="finish",
    )(dqn, dqc, nin, zin)


def local(qn, qc, kn, vn, kc, vc, dn, dc, block_ids, stretch_order):
    far = lambda *arrays: [pltpu.with_memory_space_constraint(a, pltpu.HBM) for a in arrays]
    q, nkv, kv = spread(*far(qn, qc, dn, dc, kn, vn, kc, vc))
    dq, dnkv, dkv = attention(*far(stretch_order, block_ids), q, nkv, kv.reshape(128, 64, 256), tile=(4096, 2048, 1024, 512))
    return finish(*gather(dq, dnkv, dkv.reshape(16, 2, 4, 64, 256)))


def solution(mesh):
    both = P(("seq", "head"), None)
    return jax.shard_map(
        local, mesh=mesh, in_specs=(both,) * 8 + (P(), P()), out_specs=(both,) * 6, check_vma=False
    )
```

```python
import functools, math
import jax
import jax.numpy as jnp
from jax import lax
from jax.experimental import pallas as pl
from jax.experimental.pallas import tpu as pltpu
from jax.sharding import PartitionSpec as P

NEG = -1e30
MIB = 1 << 20


def attention_kernel(sizes, order_hbm, ids_hbm, q, nkv, kv, dq, dnkv, dkv, rows_kv, cols_k, acc, ebuf, pbuf, tops, diag_tops, facts_of, qtot, turned, diag, order, ids, sem):
    facts = [pltpu.make_async_copy(order_hbm, order, sem.at[0]), pltpu.make_async_copy(ids_hbm, ids, sem.at[1])]
    for c in facts:
        c.start()
    yx = lax.axis_index("seq") // 4
    stretches, chunk, _ = kv.shape
    tokens = stretches * chunk
    scale = 1.0 / math.sqrt(128)
    to_exp2 = scale * math.log2(math.e)
    wide = jnp.float32
    half = jnp.bfloat16
    unit = sizes[-1]

    def each_chunk(body):
        def some(row, _):
            for j in range(8):
                at = (j // 2 % 2) * 4 + (j // 4) * 2 + j % 2
                body(row * 8 + at, order[row * 8 + j])
            return 0

        lax.fori_loop(0, stretches // 8, some, 0)

    def chunk_rows(p):
        return pl.ds(pl.multiple_of(p * chunk, chunk), chunk)

    facts[0].wait()

    def bring(at, p):
        rows_kv[chunk_rows(p), :] = kv[at]

    each_chunk(bring)

    def turn(t, _):
        acc[pl.ds(pl.multiple_of(t * 1024, 1024), 1024), :] = jnp.zeros((1024, 256), wide)
        for i in range(1024 // unit):
            rows = pl.ds(pl.multiple_of(t * 1024 + i * unit, unit), unit)
            cols_k[t * (1024 // unit) + i] = rows_kv[rows, :128].T
        return 0

    lax.fori_loop(0, tokens // 1024, turn, 0, unroll=2)

    def fold(values, op):
        pieces = values.reshape(values.shape[0] // 16, 2, 8, values.shape[1])
        return op(op(pieces, axis=0), axis=0)

    def dot(a, b):
        return jnp.dot(a, b, preferred_element_type=wide)

    def stack(g, a, b):
        return jnp.concatenate([q[g, a, :, :128], q[g, a, :, 128:], q[g, b, :, :128], q[g, b, :, 128:]], axis=0)

    def position(g):
        return order[yx * 8 + (g // 4) * 4 + (g % 2) * 2 + (g // 2) % 2]

    key_at = lax.broadcasted_iota(jnp.int32, (128, 256), 0)
    row_at = lax.broadcasted_iota(jnp.int32, (128, 256), 1)
    clean_row = jnp.where(row_at >= 128, 1, 0)

    def prepare(g, _):
        p = position(g)
        limit = p * chunk
        first = ids[limit]
        split = jnp.int32(0)
        for bit in (64, 32, 16, 8, 4, 2, 1):
            near = jnp.minimum(split + bit, chunk)
            hit = jnp.logical_and(split + bit <= chunk, ids[limit + near - 1] == first)
            split = jnp.where(hit, split + bit, split)
        q_t = stack(g, 0, 1).T
        d_t = stack(g, 2, 3).T
        turned[g, 0] = q_t
        turned[g, 1] = d_t
        diag_kv = jnp.concatenate([rows_kv[chunk_rows(p), :], nkv[g]], axis=0)
        key_run = jnp.where(key_at % chunk >= split, 1, 0)
        row_run = jnp.where(row_at % chunk >= split, 1, 0)
        gap = jnp.where(key_at < chunk, row_run + clean_row - key_run, jnp.where(key_run == row_run, 1, 0) - clean_row)
        diag[g, 0] = jnp.where(gap > 0, dot(diag_kv[:, :128], q_t) * to_exp2, NEG)
        diag[g, 1] = dot(diag_kv[:, 128:], d_t)
        return 0

    facts[1].wait()
    lax.fori_loop(0, q.shape[0], prepare, 0, unroll=8)

    def grads(e, dp, keys_t, piece_top, known):
        top, over, mean, q_rows, d_rows = known
        factor = jnp.exp2(piece_top - top) * over
        p = (e.reshape(e.shape[0] // 8, 8, 256) * factor[None]).reshape(e.shape)
        ds = (p * (dp - mean)).astype(half)
        return dot(keys_t, ds), dot(ds, q_rows), dot(p.astype(half), d_rows)

    def one(g, _):
        p = position(g)
        limit = p * chunk
        units = (limit + unit - 1) // unit

        def walk(body, state):
            start = jnp.int32(0)
            left = units
            for size in sizes:
                many = size // unit
                count = left // many
                state = lax.fori_loop(0, count, lambda t, s: body(pl.multiple_of(start + t * size, unit), size, s), state)
                start = start + count * size
                left = left - count * many
            return state

        def ahead(s, dp, state, keep):
            top, total, dots = state
            new = jnp.maximum(top, fold(s, jnp.max))
            fade = jnp.exp2(top - new)
            e = jnp.exp2(s.reshape(s.shape[0] // 8, 8, 256) - new[None]).reshape(s.shape)
            keep(e, dp, new)
            return new, total * fade + fold(e, jnp.sum), dots * fade + fold(e * dp, jnp.sum)

        def keep_diag(e, dp, top):
            diag[g, 0] = e
            diag_tops[g] = top

        def walk_ahead(at, size, state):
            for part in range(size // 256):
                rows = pl.ds(at + part * 256, 256)
                s = dot(rows_kv[rows, :128], turned[g, 0])
                dp = dot(rows_kv[rows, 128:], turned[g, 1])
                s = jnp.where(lax.broadcasted_iota(jnp.int32, (256, 256), 0) < limit - at - part * 256, s, NEG) * to_exp2

                def keep(e, dp, top):
                    ebuf[rows, :] = e
                    pbuf[rows, :] = dp
                    for i in range(256 // 256):
                        tops[at // 256 + part * (256 // 256) + i] = top

                state = ahead(s, dp, state, keep)
            return state

        none = jnp.zeros((8, 256), wide)
        state = ahead(diag[g, 0], diag[g, 1], (none + NEG, none, none), keep_diag)
        last, total, dots = walk(walk_ahead, state)
        top = jnp.max(last, axis=0, keepdims=True)
        fade = jnp.exp2(last - top)
        total, dots = total * fade, dots * fade
        over = 1.0 / jnp.sum(total, axis=0, keepdims=True)
        mean = jnp.sum(dots, axis=0, keepdims=True) * over
        q_rows, d_rows = stack(g, 0, 1), stack(g, 2, 3)

        qtot[g] = jnp.zeros((128, 256), wide)
        facts_of[g, 0:1], facts_of[g, 1:2], facts_of[g, 2:3] = top, over, mean

        def back(at, size, _):
            gqs = 0.0
            for part in range(size // 256):
                rows = pl.ds(at + part * 256, 256)
                keys_t = cols_k[at // unit + part * 256 // unit][:, part * 256 % unit:part * 256 % unit + 256]
                gq, gk, gv = grads(ebuf[rows, :], pbuf[rows, :], keys_t, tops[at // 256 + part], (top, over, mean, q_rows, d_rows))
                gqs = gqs + gq
                acc[rows, :128] += gk
                acc[rows, 128:] += gv
            qtot[g] += gqs
            return 0

        walk(back, 0)
        return 0

    lax.fori_loop(0, q.shape[0], one, 0)

    def finish_q(g, _):
        p = position(g)
        diag_k = jnp.concatenate([rows_kv[chunk_rows(p), :128], nkv[g, :, :128]], axis=0)
        known = (facts_of[g, 0:1], facts_of[g, 1:2], facts_of[g, 2:3], stack(g, 0, 1), stack(g, 2, 3))
        gq, gk, gv = grads(diag[g, 0], diag[g, 1], diag_k.T, diag_tops[g], known)
        acc[chunk_rows(p), :128] += gk[:chunk]
        acc[chunk_rows(p), 128:] += gv[:chunk]
        dnkv[g, :, :128] = (gk[chunk:] * scale).astype(half)
        dnkv[g, :, 128:] = gv[chunk:].astype(half)
        out = ((qtot[g] + gq) * scale).T.astype(half)
        for i in range(4):
            dq[g, i // 2, :, (i % 2) * 128:(i % 2) * 128 + 128] = out[i * 64:i * 64 + 64]
        return 0

    lax.fori_loop(0, q.shape[0], finish_q, 0, unroll=8)

    def give(at, p):
        dkv[at, :, :128] = (acc[chunk_rows(p), :128] * scale).astype(half)
        dkv[at, :, 128:] = acc[chunk_rows(p), 128:].astype(half)

    each_chunk(give)


def attention(order, ids, q, nkv, kv, tile=(2048, 1024)):
    tokens = kv.shape[0] * kv.shape[1]
    vmem = pl.BlockSpec(memory_space=pltpu.VMEM)
    hbm = pl.BlockSpec(memory_space=pltpu.HBM)
    half = jnp.bfloat16
    wide = jnp.float32
    return pl.pallas_call(
        functools.partial(attention_kernel, tile),
        out_shape=(
            jax.ShapeDtypeStruct((8, 2, 64, 256), half),
            jax.ShapeDtypeStruct((8, 64, 256), half),
            jax.ShapeDtypeStruct(kv.shape, half),
        ),
        in_specs=[hbm, hbm, vmem, vmem, vmem],
        out_specs=(vmem, vmem, vmem),
        scratch_shapes=[
            pltpu.VMEM((tokens, 256), half),
            pltpu.VMEM((tokens // tile[-1], 128, tile[-1]), half),
            pltpu.VMEM((tokens, 256), wide),
            pltpu.VMEM((tokens, 256), wide),
            pltpu.VMEM((tokens, 256), wide),
            pltpu.VMEM((tokens // 256, 8, 256), wide),
            pltpu.VMEM((8, 8, 256), wide),
            pltpu.VMEM((8, 8, 256), wide),
            pltpu.VMEM((8, 128, 256), wide),
            pltpu.VMEM((8, 2, 128, 256), half),
            pltpu.VMEM((8, 2, 128, 256), wide),
            pltpu.SMEM(order.shape, jnp.int32),
            pltpu.SMEM(ids.shape, jnp.int32),
            pltpu.SemaphoreType.DMA((2,)),
        ],
        compiler_params=pltpu.CompilerParams(vmem_limit_bytes=42 * MIB),
        name="attention",
    )(order, ids, q, nkv, kv)
MESH = pl.DeviceIdType.MESH


class Spot:
    def __init__(self):
        seq, head = lax.axis_index("seq"), lax.axis_index("head")
        self.y, self.x, self.core = seq // 16, (seq // 4) % 4, seq % 2
        self.z = ((seq // 2) % 2) * 2 + head
        self.sign = 1 - 2 * self.core

    def at(self, y, x, z, core):
        return (((y * 4 + x) * 2 + z // 2) * 2 + core, z % 2)

    def member(self, turn, flip):
        z = (self.z + turn) % 4
        core = (self.core + flip) % 2
        return z, core

    def along(self, axis, steps):
        y = (self.y + steps * self.sign + 4) % 4 if axis == "y" else self.y
        x = (self.x + steps * self.sign + 4) % 4 if axis == "x" else self.x
        return self.at(y, x, self.z, self.core)

    def row(self, dy, dx):
        return ((self.y + dy * self.sign + 4) % 4) * 4 + (self.x + dx * self.sign + 4) % 4


def greet(spot):
    barrier = pltpu.get_barrier_semaphore()
    others = [spot.member(t, f) for t in range(4) for f in range(2) if t or f]
    ids = [spot.at(spot.y, spot.x, z, c) for z, c in others]
    ids += [spot.along(a, s) for a in ("y", "x") for s in (1, -1, 2)]
    for d in ids:
        pl.semaphore_signal(barrier, inc=1, device_id=d, device_id_type=MESH)
    pl.semaphore_wait(barrier, len(ids))


class Sender:
    def __init__(self, send, recv):
        self.send, self.recv, self.made = send, recv, []

    def go(self, src, dst, device):
        n = len(self.made)
        copy = pltpu.make_async_remote_copy(
            src_ref=src, dst_ref=dst, send_sem=self.send.at[n], recv_sem=self.recv.at[n],
            device_id=device, device_id_type=MESH,
        )
        copy.start()
        self.made.append(copy)
        return copy


def spread_kernel(qn, qc, dn, dc, kn, vn, kc, vc, q, nkv, kv, send, recv, own):
    spot = Spot()
    greet(spot)
    out = Sender(send, recv)
    mine = spot.z * 2 + spot.core
    here = spot.row(0, 0)

    def pieces(z, core):
        head = pl.ds(pl.multiple_of((z % 2) * 128, 128), 128)
        cols = pl.ds(pl.multiple_of(((z % 2) * 4 + (z // 2) * 2 + core) * 256, 256), 256)
        found = [(a.at[:, cols], q.at[mine, i]) for i, a in enumerate((qn, qc, dn, dc))]
        found += [(kn.at[:, head], nkv.at[mine, :, :128]), (vn.at[:, head], nkv.at[mine, :, 128:])]
        return found

    def clean(z):
        head = pl.ds(pl.multiple_of((z % 2) * 128, 128), 128)
        slot = kv.at[here, spot.core, spot.z]
        return [(kc.at[:, head], slot.at[:, :128]), (vc.at[:, head], slot.at[:, 128:])]

    local = [pltpu.make_async_copy(s, d, own.at[i]) for i, (s, d) in enumerate(clean(spot.z) + pieces(spot.z, spot.core))]
    for c in local:
        c.start()
    first = []
    for turn in (1, 3, 2):
        z, _ = spot.member(turn, 0)
        for s, d in clean(z):
            first.append(out.go(s, d, spot.at(spot.y, spot.x, z, spot.core)))

    def send_group(turn, flip):
        z, core = spot.member(turn, flip)
        for s, d in pieces(z, core):
            out.go(s, d, spot.at(spot.y, spot.x, z, core))

    local[0].wait()
    local[1].wait()
    for c in first:
        c.wait_recv()

    sibling = spot.at(spot.y, spot.x, spot.z, 1 - spot.core)
    last = []
    done = list(first)

    def block(dy, dx, half):
        return kv.at[spot.row(dy, dx), spot.core, pl.ds(half * 2, 2)]

    def offer(dy, dx, half, axis, steps):
        b = block(dy, dx, half)
        c = out.go(b, b, spot.along(axis, steps))
        return c

    def twin(dy, dx, half):
        b = block(dy, dx, half)
        last.append(out.go(b, b, sibling))

    def got(c):
        c.wait_recv()
        done.append(c)

    pair = {}
    for half, axis in ((0, "x"), (1, "y")):
        pair[half] = (offer(0, 0, half, axis, 1), offer(0, 0, half, axis, -1), offer(0, 0, half, axis, 2))
    late = {}
    for half, axis in ((0, "y"), (1, "x")):
        late[half, 0] = (offer(0, 0, half, axis, 1), offer(0, 0, half, axis, -1))
    for half in (0, 1):
        twin(0, 0, half)

    def spot_of(half, first_step, second_step):
        return (second_step, first_step) if half == 0 else (first_step, second_step)

    for turn, flip in ((1, 0), (3, 1), (2, 0), (3, 0), (1, 1), (2, 1), (0, 1)):
        send_group(turn, flip)
    for half in (0, 1):
        got(pair[half][0])
        dy, dx = spot_of(half, -1, 0)
        other = "y" if half == 0 else "x"
        late[half, -1] = (offer(dy, dx, half, other, 1), offer(dy, dx, half, other, -1))
        twin(dy, dx, half)
    for half in (0, 1):
        got(pair[half][1])
        dy, dx = spot_of(half, 1, 0)
        other = "y" if half == 0 else "x"
        late[half, 1] = (offer(dy, dx, half, other, 1), offer(dy, dx, half, other, -1))
        twin(dy, dx, half)
    far = {}

    def second(step):
        for half in (0, 1):
            other = "y" if half == 0 else "x"
            got(late[half, step][0])
            dy, dx = spot_of(half, step, -1)
            far[half, step] = offer(dy, dx, half, other, 1)
            twin(dy, dx, half)

    for half in (0, 1):
        got(pair[half][2])
        dy, dx = spot_of(half, 2, 0)
        other = "y" if half == 0 else "x"
        late[half, 2] = (offer(dy, dx, half, other, 1), offer(dy, dx, half, other, -1))
        twin(dy, dx, half)
    second(0)
    for step in (-1, 1, 2):
        second(step)
    for step in (0, -1, 1, 2):
        for half in (0, 1):
            got(late[half, step][1])
            dy, dx = spot_of(half, step, 1)
            twin(dy, dx, half)
    for step in (0, -1, 1, 2):
        for half in (0, 1):
            got(far[half, step])
            dy, dx = spot_of(half, step, 2)
            twin(dy, dx, half)
    for c in local[2:]:
        c.wait()
    for c in out.made:
        if not any(c is d for d in done):
            c.wait_recv()
    for c in out.made:
        c.wait_send()


SPREAD_COPIES = 6 + 42 + 2 * (3 + 12 + 16)


def spread(qn, qc, dn, dc, kn, vn, kc, vc):
    half = jnp.bfloat16
    hbm = pl.BlockSpec(memory_space=pl.ANY)
    return pl.pallas_call(
        spread_kernel,
        out_shape=(
            jax.ShapeDtypeStruct((8, 4, 64, 256), half),
            jax.ShapeDtypeStruct((8, 64, 256), half),
            jax.ShapeDtypeStruct((16, 2, 4, 64, 256), half),
        ),
        in_specs=[pl.BlockSpec(memory_space=pltpu.HBM)] * 8,
        out_specs=(hbm,) * 3,
        scratch_shapes=[
            pltpu.SemaphoreType.DMA((SPREAD_COPIES,)),
            pltpu.SemaphoreType.DMA((SPREAD_COPIES,)),
            pltpu.SemaphoreType.DMA((8,)),
        ],
        compiler_params=pltpu.CompilerParams(collective_id=0, has_side_effects=True, vmem_limit_bytes=4 * MIB),
        name="spread",
    )(qn, qc, dn, dc, kn, vn, kc, vc)


def gather_kernel(dq, dnkv, dkv, dqn, dqc, nin, zin, twins, parts, slots, stage, zout, send, recv, own):
    spot = Spot()
    greet(spot)
    out = Sender(send, recv)
    mine = spot.z * 2 + spot.core
    sibling = spot.at(spot.y, spot.x, spot.z, 1 - spot.core)
    cols = pl.ds(pl.multiple_of(((spot.z % 2) * 4 + (spot.z // 2) * 2 + spot.core) * 256, 256), 256)
    wide = jnp.float32

    twin = {}
    lanes = (2, -1, 1, 0)
    order = []
    for steps in ((2,), (-1, 1), (0,)):
        for lane in lanes:
            for pair in [(s, lane) for s in steps] + [(lane, s) for s in steps]:
                if pair not in order:
                    order.append(pair)

    for dy, dx in order:
        r = spot.row(-dy, -dx)
        twin[dy, dx] = out.go(dkv.at[r, 1 - spot.core], twins.at[r], sibling)

    def send_group(turn, flip):
        z, core = spot.member(turn, flip)
        to = z * 2 + core
        device = spot.at(spot.y, spot.x, z, core)
        return [
            out.go(dq.at[to, 0], dqn.at[:, cols], device),
            out.go(dq.at[to, 1], dqc.at[:, cols], device),
            out.go(dnkv.at[to], nin.at[mine], device),
        ]

    group = []
    for turn, flip in ((2, 0), (2, 1), (1, 0), (3, 0), (1, 1), (3, 1), (0, 1)):
        group += send_group(turn, flip)
    local = [
        pltpu.make_async_copy(dq.at[mine, 0], dqn.at[:, cols], own.at[0]),
        pltpu.make_async_copy(dq.at[mine, 1], dqc.at[:, cols], own.at[1]),
        pltpu.make_async_copy(dnkv.at[mine], nin.at[mine], own.at[2]),
    ]
    for c in local:
        c.start()

    ready = set()

    def part(dy, dx):
        r = spot.row(dy, dx)
        if (dy, dx) not in ready:
            ready.add((dy, dx))
            twin[dy, dx].wait_recv()
            parts[r] = (dkv[r, spot.core].astype(wide) + twins[r].astype(wide)).astype(jnp.bfloat16)
        return r

    def owner(half, lane, step):
        return (step, lane) if half == 0 else (lane, step)

    first_axis = ("y", "x")
    sent = {}
    for lane in lanes:
        for half in (0, 1):
            r = part(*owner(half, lane, 2))
            n = lanes.index(lane)
            sent[half, lane, 0] = out.go(parts.at[r, pl.ds(half * 2, 2)], slots.at[half, n, 0], spot.along(first_axis[half], -1))
    for lane in lanes:
        for half in (0, 1):
            n = lanes.index(lane)
            r = part(*owner(half, lane, -1))
            part(*owner(half, lane, 1))
            sent[half, lane, 0].wait_recv()
            stage[half, n] = (parts[r, half * 2:half * 2 + 2].astype(wide) + slots[half, n, 0].astype(wide)).astype(jnp.bfloat16)
            sent[half, lane, 1] = out.go(stage.at[half, n], slots.at[half, n, 1], spot.along(first_axis[half], -1))
            r = part(*owner(half, lane, 1))
            sent[half, lane, 2] = out.go(parts.at[r, pl.ds(half * 2, 2)], slots.at[half, n, 2], spot.along(first_axis[half], 1))

    def total(half, lane):
        n = lanes.index(lane)
        r = part(*owner(half, lane, 0))
        sent[half, lane, 1].wait_recv()
        sent[half, lane, 2].wait_recv()
        return parts[r, half * 2:half * 2 + 2].astype(wide) + slots[half, n, 1].astype(wide) + slots[half, n, 2].astype(wide)

    second_axis = ("x", "y")
    deep = {}
    for kind, lane in enumerate((2, -1, 1)):
        for half in (0, 1):
            stage[half, 4 + kind] = total(half, lane).astype(jnp.bfloat16)
            deep[half, kind] = out.go(stage.at[half, 4 + kind], slots.at[half, 4, kind], spot.along(second_axis[half], lane))
    for half in (0, 1):
        mid = total(half, 0)
        for kind in range(3):
            deep[half, kind].wait_recv()
            mid = mid + slots[half, 4, kind].astype(wide)
        zout[half * 2:half * 2 + 2] = mid.astype(jnp.bfloat16)
    deep_z = []
    for turn in (2, 1, 3):
        z, _ = spot.member(turn, 0)
        deep_z.append(out.go(zout.at[z], zin.at[spot.z], spot.at(spot.y, spot.x, z, spot.core)))
    zin[spot.z] = zout[spot.z]

    for c in group + deep_z:
        c.wait_recv()
    for c in local:
        c.wait()
    for c in out.made:
        c.wait_send()


GATHER_COPIES = 16 + 21 + 24 + 6 + 3


def gather(dq, dnkv, dkv):
    half = jnp.bfloat16
    vmem = pl.BlockSpec(memory_space=pltpu.VMEM)
    hbm = pl.BlockSpec(memory_space=pl.ANY)
    return pl.pallas_call(
        gather_kernel,
        out_shape=(
            jax.ShapeDtypeStruct((64, 2048), half),
            jax.ShapeDtypeStruct((64, 2048), half),
            jax.ShapeDtypeStruct((8, 64, 256), half),
            jax.ShapeDtypeStruct((4, 64, 256), half),
        ),
        in_specs=[hbm, hbm, vmem],
        out_specs=(hbm, hbm, vmem, vmem),
        scratch_shapes=[
            pltpu.VMEM((16, 4, 64, 256), half),
            pltpu.VMEM((16, 4, 64, 256), half),
            pltpu.VMEM((2, 5, 3, 2, 64, 256), half),
            pltpu.VMEM((2, 7, 2, 64, 256), half),
            pltpu.VMEM((4, 64, 256), half),
            pltpu.SemaphoreType.DMA((GATHER_COPIES,)),
            pltpu.SemaphoreType.DMA((GATHER_COPIES,)),
            pltpu.SemaphoreType.DMA((3,)),
        ],
        compiler_params=pltpu.CompilerParams(collective_id=1, has_side_effects=True, vmem_limit_bytes=14 * MIB),
        name="gather",
    )(dq, dnkv, dkv)


def finish_kernel(dqn, dqc, nin, zin, dqn_out, dqc_out, dkn, dvn, dkc, dvc, sem):
    copies = [pltpu.make_async_copy(dqn, dqn_out, sem.at[0]), pltpu.make_async_copy(dqc, dqc_out, sem.at[1])]
    for c in copies:
        c.start()
    wide = jnp.float32
    for head in (0, 1):
        at = slice(head * 128, head * 128 + 128)
        noisy = sum(nin[z * 2 + core].astype(wide) for z in (head, head + 2) for core in (0, 1))
        dkn[:, at] = noisy[:, :128].astype(jnp.bfloat16)
        dvn[:, at] = noisy[:, 128:].astype(jnp.bfloat16)
        clean = zin[head].astype(wide) + zin[head + 2].astype(wide)
        dkc[:, at] = clean[:, :128].astype(jnp.bfloat16)
        dvc[:, at] = clean[:, 128:].astype(jnp.bfloat16)
    for c in copies:
        c.wait()


def finish(dqn, dqc, nin, zin):
    half = jnp.bfloat16
    vmem = pl.BlockSpec(memory_space=pltpu.VMEM)
    hbm = pl.BlockSpec(memory_space=pl.ANY)
    return pl.pallas_call(
        finish_kernel,
        out_shape=(jax.ShapeDtypeStruct((64, 2048), half),) * 2 + (jax.ShapeDtypeStruct((64, 256), half),) * 4,
        in_specs=[hbm, hbm, vmem, vmem],
        out_specs=(hbm, hbm, vmem, vmem, vmem, vmem),
        scratch_shapes=[pltpu.SemaphoreType.DMA((2,))],
        compiler_params=pltpu.CompilerParams(vmem_limit_bytes=4 * MIB),
        name="finish",
    )(dqn, dqc, nin, zin)


def local(qn, qc, kn, vn, kc, vc, dn, dc, block_ids, stretch_order):
    far = lambda *arrays: [pltpu.with_memory_space_constraint(a, pltpu.HBM) for a in arrays]
    q, nkv, kv = spread(*far(qn, qc, dn, dc, kn, vn, kc, vc))
    dq, dnkv, dkv = attention(*far(stretch_order, block_ids), q, nkv, kv.reshape(128, 64, 256), tile=(4096, 2048, 1024, 512))
    return finish(*gather(dq, dnkv, dkv.reshape(16, 2, 4, 64, 256)))


def solution(mesh):
    both = P(("seq", "head"), None)
    return jax.shard_map(
        local, mesh=mesh, in_specs=(both,) * 8 + (P(), P()), out_specs=(both,) * 6, check_vma=False
    )
```
